32 devices in a mesh: frame: 8 (over z, x), row: 4 (over y, core).
Axes of the slice: x: 2, y: 2, z: 4, core: 2. Of those that a mesh axis runs over, the one named last changes fastest.
Arguments:
- frames_in: bfloat16 [8, 64, 64, 1152], P('frame', 'row'), may hold values from -6 to 6
- spatial_qkv: bfloat16 [1152, 1728], replicated
- spatial_out: bfloat16 [576, 1152], replicated, may hold values from -0.8984375 to 0.8984375
- temporal_qkv: bfloat16 [1152, 1728], replicated
- temporal_out: bfloat16 [576, 1152], replicated, may hold values from -0.8984375 to 0.8984375
- key_tiles: int32 [8, 64, 9], P('frame', 'row'), may hold values from 0 to 63, as said below
- tile_counts: int32 [8, 64], P('frame', 'row'), may hold values from 1 to 9, as said below
Outputs:
- frames_out: bfloat16 [8, 64, 64, 1152], P('frame', 'row')
The draws below stay inside these ranges and needn't reach their ends.
Inputs may be any that keep to these rules, and one draw needn't show every extreme that they name: `key_tiles`: for query tile t, whose tile row is t // 4 and tile column t % 4, the first tile_counts entries name distinct tiles whose tile row and tile column each differ from t's by at most one; later entries equal t. `tile_counts`: at most the number of tiles within one tile row and one tile column of the query tile.
All inputs are finite; a program needn't handle non-finite values.
Results may differ from the reference program's by a relative error of at most 0.019.
Values may be sent and summed in bfloat16 or wider, within the bound.
No kernel may reach another device: no remote copies, remote signals or barrier semaphores. Data moves between devices by JAX's collectives and lax.ppermute only.
A program may use at most 128 MiB of HBM per device.

```python
import jax
import jax.numpy as jnp
from jax import lax

D = 1152
HEADS = 8
HD = 72
TH = 4
TW = 16
KMAX = 9
W = 64
FRAMES = 8
HEIGHT = 64


def qkv_weight(key):
    inner_dim = HEADS * HD
    key_base = jax.random.fold_in(key, 0)
    base_mat = jax.random.normal(key_base, (D, 3 * inner_dim), jnp.float32) * D ** (-0.5)
    return base_mat


def draw_spatial_qkv(key, part):
    return qkv_weight(jax.random.fold_in(key, 11)).astype(jnp.bfloat16)


def draw_temporal_qkv(key, part):
    return qkv_weight(jax.random.fold_in(key, 23)).astype(jnp.bfloat16)


def tile_lists(key):
    key = jax.random.fold_in(key, 7)
    tile_rows = HEIGHT // TH
    tile_cols = W // TW
    tile_ids = jnp.arange(tile_rows * tile_cols, dtype=jnp.int32)
    tile_row = tile_ids // tile_cols
    tile_col = tile_ids % tile_cols
    offsets = jnp.arange(9, dtype=jnp.int32)
    near_row = tile_row[:, None] + (offsets // 3 - 1)[None, :]
    near_col = tile_col[:, None] + (offsets % 3 - 1)[None, :]
    valid = (near_row >= 0) & (near_row < tile_rows) & (near_col >= 0) & (near_col < tile_cols)
    neighbours = jnp.clip(near_row, 0, tile_rows - 1) * tile_cols + jnp.clip(near_col, 0, tile_cols - 1)
    key_order, key_band, key_light = jax.random.split(key, 3)
    ranks = jax.random.randint(key_order, (FRAMES, tile_rows * tile_cols, 9), 0, 1000) * 9 + offsets
    order_key = jnp.where(valid[None], 0, 100000) + ranks
    order = jnp.argsort(order_key, axis=-1)
    lists = jnp.take_along_axis(jnp.broadcast_to(neighbours[None], order.shape), order, axis=-1)
    valid_num = jnp.sum(valid.astype(jnp.int32), axis=-1)
    busy_row = jax.random.randint(key_band, (FRAMES, 1), 0, tile_rows)
    busy_mask = jnp.abs(tile_row[None, :] - busy_row) <= max(tile_rows // 8, 1)
    light_count = jax.random.randint(key_light, (FRAMES, tile_rows * tile_cols), 1, 4)
    counts = jnp.where(busy_mask, valid_num[None], jnp.minimum(light_count, valid_num[None]))
    counts = counts.at[:, tile_cols + 1].set(9)
    lists = jnp.where(offsets[None, None, :] < counts[:, :, None], lists, tile_ids[None, :, None])
    return (lists.astype(jnp.int32), counts.astype(jnp.int32))


def draw_key_tiles(key, part):
    return tile_lists(key)[0]


def draw_tile_counts(key, part):
    return tile_lists(key)[1]


def block_scale(stream_key, extent, cuts, smallest, high):
    level = 1.0
    for axis_at, blocks in cuts:
        steps = jax.random.uniform(jax.random.fold_in(jax.random.fold_in(stream_key, 6), axis_at), (blocks,), jnp.float32, smallest / len(cuts), high / len(cuts))
        level = level * jnp.repeat(jnp.exp(steps), extent[axis_at] // blocks).reshape((-1,) + (1,) * (len(extent) - 1 - axis_at))
    return level


def noise(rng, dims, scale, bound, cuts=(), kind=jnp.bfloat16):
    gain = block_scale(rng, dims, cuts, -0.22, 0.18) if cuts else 1.0
    values = jax.random.normal(rng, dims, jnp.float32) * scale * gain
    return jnp.minimum(jnp.maximum(values, -bound), bound).astype(kind)


def setup_inputs(seed: int = 0) -> dict:
    key_of = jax.random.split(jax.random.key(seed), 8)
    frames_in = noise(key_of[0], (FRAMES, HEIGHT, W, D), 1.0, 6.0, ((0, 8), (1, 4)))
    spatial_qkv = draw_spatial_qkv(jax.random.fold_in(key_of[7], 71), 0)
    spatial_out = noise(key_of[2], (HEADS * HD, D), 0.15, 0.8984375)
    temporal_qkv = draw_temporal_qkv(jax.random.fold_in(key_of[7], 71), 0)
    temporal_out = noise(key_of[4], (HEADS * HD, D), 0.15, 0.8984375)
    key_tiles = draw_key_tiles(jax.random.fold_in(key_of[7], 71), 0)
    tile_counts = draw_tile_counts(jax.random.fold_in(key_of[7], 71), 0)
    return {"frames_in": frames_in, "spatial_qkv": spatial_qkv, "spatial_out": spatial_out, "temporal_qkv": temporal_qkv, "temporal_out": temporal_out, "key_tiles": key_tiles, "tile_counts": tile_counts}


NORM_EPS = 1e-06

def layer_norm(values):
    values = values.astype(jnp.float32)
    centred = values - lax.optimization_barrier(jnp.mean(values, axis=-1, keepdims=True))
    spread = lax.optimization_barrier(jnp.mean(centred * centred, axis=-1, keepdims=True))
    return (centred * lax.rsqrt(spread + NORM_EPS)).astype(jnp.bfloat16)

def softmax_rows(scores):
    top = lax.optimization_barrier(jnp.max(scores, axis=-1, keepdims=True))
    expo = jnp.exp(scores - top)
    return (expo / lax.optimization_barrier(jnp.sum(expo, axis=-1, keepdims=True))).astype(jnp.bfloat16)

def to_tiles(array):
    row_num, col_num, chan_num = array.shape
    shaped = array.reshape(row_num // TH, TH, col_num // TW, TW, chan_num)
    return shaped.transpose(0, 2, 1, 3, 4).reshape(-1, TH * TW, chan_num)

def from_tiles(array, tile_rows, tile_cols):
    chan_num = array.shape[-1]
    shaped = array.reshape(tile_rows, tile_cols, TH, TW, chan_num)
    return shaped.transpose(0, 2, 1, 3, 4).reshape(tile_rows * TH, tile_cols * TW, chan_num)

def tile_attention(queries, key_vecs, val_vecs, counts):
    scores = jnp.einsum('nqhd,nkhd->nhqk', queries.astype(jnp.float32), key_vecs.astype(jnp.float32)) * HD ** (-0.5)
    slot_ids = jnp.arange(key_vecs.shape[1], dtype=jnp.int32) // queries.shape[1]
    live = slot_ids[None, :] < counts[:, None]
    scores = jnp.where(live[:, None, None, :], scores, -1e+30)
    weights = softmax_rows(scores)
    result = jnp.einsum('nhqk,nkhd->nqhd', weights.astype(jnp.float32), val_vecs.astype(jnp.float32))
    return result.astype(jnp.bfloat16)

def temporal_attention(pieces):
    frame_num, pos_num = (pieces.shape[0], pieces.shape[1])
    queries = pieces[:, :, 0].astype(jnp.float32)
    key_vecs = pieces[:, :, 1].astype(jnp.float32)
    val_vecs = pieces[:, :, 2].astype(jnp.float32)
    scores = jnp.einsum('fphd,gphd->phfg', queries, key_vecs) * HD ** (-0.5)
    weights = softmax_rows(scores)
    result = jnp.einsum('phfg,gphd->fphd', weights.astype(jnp.float32), val_vecs)
    return result.astype(jnp.bfloat16).reshape(frame_num, pos_num, HEADS * HD)

def reference(frames_in, spatial_qkv, spatial_out, temporal_qkv, temporal_out, key_tiles, tile_counts):
    inner_dim = HEADS * HD
    height = frames_in.shape[1]
    columns = frames_in.shape[2]
    tile_len = TH * TW

    def spatial_frame(packed):
        frame_in, targets, counts = packed
        normed = layer_norm(frame_in)
        projected = jnp.dot(normed.reshape(height * columns, -1), spatial_qkv, preferred_element_type=jnp.float32)
        projected = projected.astype(jnp.bfloat16).reshape(height, columns, 3 * inner_dim)
        tile_set = to_tiles(projected)
        tile_num = tile_set.shape[0]
        pieces = tile_set.reshape(tile_num, tile_len, 3, HEADS, HD)
        kv_tiles = pieces[:, :, 1:]
        chosen = kv_tiles[targets].reshape(tile_num, KMAX * tile_len, 2, HEADS, HD)
        attended = tile_attention(pieces[:, :, 0], chosen[:, :, 0], chosen[:, :, 1], counts)
        merged = from_tiles(attended.reshape(tile_num, tile_len, inner_dim), height // TH, columns // TW)
        branch = jnp.dot(merged.reshape(-1, inner_dim), spatial_out, preferred_element_type=jnp.float32)
        return (frame_in.astype(jnp.float32) + branch.reshape(height, columns, -1)).astype(jnp.bfloat16)
    mixed_one = lax.map(spatial_frame, (frames_in, key_tiles, tile_counts))
    frame_num = mixed_one.shape[0]
    normed_two = layer_norm(mixed_one)

    def temporal_row(row_slab):
        projected = jnp.dot(row_slab.reshape(-1, row_slab.shape[-1]), temporal_qkv, preferred_element_type=jnp.float32)
        projected = projected.astype(jnp.bfloat16).reshape(frame_num, columns, 3, HEADS, HD)
        return temporal_attention(projected)
    attended = lax.map(temporal_row, jnp.transpose(normed_two, (1, 0, 2, 3)))
    attended = jnp.transpose(attended, (1, 0, 2, 3))
    branch = jnp.dot(attended.reshape(-1, inner_dim), temporal_out, preferred_element_type=jnp.float32)
    return (mixed_one.astype(jnp.float32) + branch.reshape(mixed_one.shape)).astype(jnp.bfloat16)
```

```python
import functools

import jax
import jax.numpy as jnp
from jax import lax
from jax.experimental import pallas as pl
from jax.experimental.pallas import tpu as pltpu
from jax.sharding import PartitionSpec as P

HEADS = 8
HD = 72
TH = 4
TW = 16
LANES = 128
PACK = 16
NORM_EPS = 1e-06
NEG = -1e30
LOG2E = 1.4426950408889634
F32 = jnp.float32
BF16 = jnp.bfloat16
INNER = HEADS * HD
SHIFT = INNER % LANES
KEY_LO = INNER - SHIFT
EXT = INNER + SHIFT
VMEM_LIMIT = 48 * 1024 * 1024


def layer_norm(values):
    values = values.astype(F32)
    centred = values - jnp.mean(values, axis=-1, keepdims=True)
    spread = jnp.mean(centred * centred, axis=-1, keepdims=True)
    return (centred * lax.rsqrt(spread + NORM_EPS)).astype(BF16)


def window(start):
    return start // LANES * LANES, -(-(start + HD) // LANES) * LANES


def head_lanes(rows, lo, hi, start):
    lane = lax.broadcasted_iota(jnp.int32, (rows, hi - lo), 1) + lo
    return (lane >= start) & (lane < start + HD)


def scaled_queries(prod):
    shifted = pltpu.roll(prod[:, :EXT], SHIFT, 1) if SHIFT else prod[:, :EXT]
    return (shifted * (LOG2E * HD**-0.5)).astype(BF16)


def nt_dot(a, b):
    return lax.dot_general(a, b, (((1,), (1,)), ((), ())), preferred_element_type=F32)


def project_kernel(steps, x_ref, w_ref, q_ref, kv_ref, top_ref, bot_ref):
    step = pl.program_id(0)
    prod = jnp.dot(layer_norm(x_ref[...]), w_ref[...], preferred_element_type=F32)
    q_ref[...] = scaled_queries(prod)
    kv_ref[:, :EXT] = prod[:, KEY_LO : 2 * INNER].astype(BF16)
    kv_ref[:, EXT:] = prod[:, 2 * INNER :].astype(BF16)

    @pl.when(step == 0)
    def _():
        top_ref[...] = kv_ref[...]

    @pl.when(step == steps - 1)
    def _():
        bot_ref[...] = kv_ref[...]


def project(x, w, slab):
    pixels, feat = x.shape
    steps = pixels // slab
    kv_dim = EXT + INNER
    return pl.pallas_call(
        functools.partial(project_kernel, steps),
        grid=(steps,),
        in_specs=[
            pl.BlockSpec((slab, feat), lambda i: (i, 0)),
            pl.BlockSpec(w.shape, lambda i: (0, 0)),
        ],
        out_specs=[
            pl.BlockSpec((slab, EXT), lambda i: (i, 0)),
            pl.BlockSpec((slab, kv_dim), lambda i: (i, 0)),
            pl.BlockSpec((slab, kv_dim), lambda i: (0, 0)),
            pl.BlockSpec((slab, kv_dim), lambda i: (0, 0)),
        ],
        out_shape=[
            jax.ShapeDtypeStruct((pixels, EXT), BF16),
            jax.ShapeDtypeStruct((pixels, kv_dim), BF16),
            jax.ShapeDtypeStruct((slab, kv_dim), BF16),
            jax.ShapeDtypeStruct((slab, kv_dim), BF16),
        ],
        compiler_params=pltpu.CompilerParams(vmem_limit_bytes=VMEM_LIMIT),
        cost_estimate=pl.CostEstimate(
            flops=2 * pixels * feat * 3 * INNER, bytes_accessed=12 * 2**20, transcendentals=0
        ),
        name="project",
    )(x, w)


def fill_bias(bias_ref, tile_row, global_row, tile_cols, slot_num, targets_ref, counts_ref):
    slab, key_num = bias_ref.shape
    columns = tile_cols * TW
    key = lax.broadcasted_iota(jnp.int32, (1, key_num), 1)
    key_tile = key // slab * tile_cols + key % columns // TW
    for col in range(tile_cols):
        tile = tile_row * tile_cols + col
        count = counts_ref[0, tile]
        seen = jnp.zeros((1, key_num), jnp.bool_)
        for slot in range(slot_num):
            target = targets_ref[0, tile, slot]
            cand = lax.div(target, tile_cols) - global_row + 1
            cand = cand * tile_cols + lax.rem(target, tile_cols)
            cand = jnp.where(slot < count, cand, -1)
            seen = seen | (key_tile == cand)
        line = jnp.broadcast_to(jnp.where(seen, 0.0, NEG).astype(F32), (TW, key_num))
        for row in range(slab // columns):
            bias_ref[pl.ds(row * columns + col * TW, TW), :] = line


def spatial_kernel(
    edges, rows_of, group, frame_axis, row_axis, tile_rows, peers, xor,
    targets_ref, counts_ref, x_ref, q_ref, prev_ref, mid_ref, next_ref, *rest,
):
    if edges:
        top_ref, bot_ref, w_ref = rest[:3]
        rest = rest[3:]
    else:
        w_ref = rest[0]
        rest = rest[1:]
    mixed_ref = rest[0]
    send_refs = rest[1 : 1 + peers]
    bias_ref, acc_ref, normed_ref = rest[1 + peers : 4 + peers]
    step = pl.program_id(0)
    steps = len(rows_of)
    slab = x_ref.shape[0]
    if edges:
        prev_s, next_s = rest[4 + peers :]

        @pl.when(step == 0)
        def _():
            prev_s[...] = top_ref[...]
            next_s[...] = next_ref[...]

        @pl.when(step != 0)
        def _():
            prev_s[...] = prev_ref[...]
            next_s[...] = bot_ref[...]

        kv_refs = (prev_s, mid_ref, next_s)
        tile_row = step * (tile_rows - 1)
    else:
        kv_refs = (prev_ref, mid_ref, next_ref)
        tile_row = step + rows_of[0]
    global_row = lax.axis_index(row_axis) * tile_rows + tile_row
    tile_cols = targets_ref.shape[1] // tile_rows
    fill_bias(
        bias_ref, tile_row, global_row, tile_cols, targets_ref.shape[2], targets_ref, counts_ref
    )

    for head in range(HEADS):
        start = SHIFT + head * HD
        lo, hi = window(start)
        queries = jnp.where(head_lanes(slab, lo, hi, start), q_ref[:, lo:hi], 0)
        scores = [
            nt_dot(queries, ref[:, lo:hi]) + bias_ref[:, i * slab : (i + 1) * slab]
            for i, ref in enumerate(kv_refs)
        ]
        top = jnp.max(jnp.maximum(jnp.maximum(scores[0], scores[1]), scores[2]), axis=-1, keepdims=True)
        expo = [jnp.exp2(s - top) for s in scores]
        total = jnp.sum(expo[0] + expo[1] + expo[2], axis=-1, keepdims=True)
        start = head * HD
        lo, hi = window(start)
        hi = min(hi, INNER)
        out = sum(
            jnp.dot(e.astype(BF16), ref[:, EXT + lo : EXT + hi], preferred_element_type=F32)
            for e, ref in zip(expo, kv_refs)
        )
        out = (out / total).astype(BF16)
        if head == 0:
            acc_ref[:, lo:hi] = out
        else:
            mask = head_lanes(slab, lo, hi, start)
            if lo // LANES * LANES < start:
                acc_ref[:, lo:hi] = jnp.where(mask, out, acc_ref[:, lo:hi])
            else:
                acc_ref[:, lo:hi] = out

    branch = jnp.dot(acc_ref[...], w_ref[...], preferred_element_type=F32)
    mixed = (x_ref[...].astype(F32) + branch).astype(BF16)
    mixed_ref[...] = mixed
    normed_ref[pl.ds(pl.multiple_of(step * slab, slab), slab), :] = layer_norm(mixed)

    @pl.when(step == steps - 1)
    def _():
        me = lax.axis_index(frame_axis)
        for j in range(peers):
            peer = me ^ j if xor else lax.rem(me + j, peers)
            begin = pl.multiple_of(peer * group, PACK)
            send_refs[j][...] = normed_ref[pl.ds(begin, group), :]


def spatial(edges, x, q, kv, halos, w, targets, counts, slab, peers, xor):
    pixels, feat = x.shape
    tile_rows = pixels // slab
    rows_of = (0, tile_rows - 1) if edges else tuple(range(1, tile_rows - 1))
    steps = len(rows_of)
    group = steps * slab // peers
    kv_dim = kv.shape[1]
    if edges:
        at = lambda i: i * (tile_rows - 1)
        prev_at = lambda i: tile_rows - 2
        next_at = lambda i: 1
    else:
        at = lambda i: i + 1
        prev_at = lambda i: i
        next_at = lambda i: i + 2
    smem = pl.BlockSpec(memory_space=pltpu.SMEM)
    in_specs = [
        smem,
        smem,
        pl.BlockSpec((slab, feat), lambda i: (at(i), 0)),
        pl.BlockSpec((slab, EXT), lambda i: (at(i), 0)),
        pl.BlockSpec((slab, kv_dim), lambda i: (prev_at(i), 0)),
        pl.BlockSpec((slab, kv_dim), lambda i: (at(i), 0)),
        pl.BlockSpec((slab, kv_dim), lambda i: (next_at(i), 0)),
    ]
    args = [targets, counts, x, q, kv, kv, kv]
    scratch = [
        pltpu.VMEM((slab, 3 * slab), F32),
        pltpu.VMEM((slab, INNER), BF16),
        pltpu.VMEM((steps * slab, feat), BF16),
    ]
    if edges:
        in_specs += [pl.BlockSpec((slab, kv_dim), lambda i: (0, 0))] * 2
        args += list(halos)
        scratch += [pltpu.VMEM((slab, kv_dim), BF16)] * 2
    in_specs.append(pl.BlockSpec(w.shape, lambda i: (0, 0)))
    args.append(w)
    outs = pl.pallas_call(
        functools.partial(
            spatial_kernel, edges, rows_of, group, "frame", "row", tile_rows, peers, xor
        ),
        grid=(steps,),
        in_specs=in_specs,
        out_specs=[pl.BlockSpec((slab, feat), lambda i: (i, 0))]
        + [pl.BlockSpec((group, feat), lambda i: (0, 0))] * peers,
        out_shape=[jax.ShapeDtypeStruct((steps * slab, feat), BF16)]
        + [jax.ShapeDtypeStruct((group, feat), BF16)] * peers,
        scratch_shapes=scratch,
        compiler_params=pltpu.CompilerParams(vmem_limit_bytes=VMEM_LIMIT),
        cost_estimate=pl.CostEstimate(
            flops=8 * 10**9, bytes_accessed=8 * 2**20, transcendentals=0
        ),
        name="spatial_edges" if edges else "spatial_inner",
    )(*args)
    return outs[0], outs[1:]


def temporal_kernel(peers, group, *refs):
    in_refs = refs[:peers]
    w_ref = refs[peers]
    out_refs = refs[peers + 1 : 2 * peers + 1]
    x_ref, q_ref, kv_ref, acc_ref = refs[2 * peers + 1 :]
    block = peers * PACK
    parts = group // PACK
    for part in range(parts):
        for j in range(peers):
            x_ref[pl.ds(part * block + j * PACK, PACK), :] = in_refs[j][pl.ds(part * PACK, PACK), :]
    prod = jnp.dot(x_ref[...], w_ref[...], preferred_element_type=F32)
    q_ref[...] = scaled_queries(prod)
    kv_ref[:, :EXT] = prod[:, KEY_LO : 2 * INNER].astype(BF16)
    kv_ref[:, EXT:] = prod[:, 2 * INNER :].astype(BF16)
    row = lax.broadcasted_iota(jnp.int32, (block, block), 0)
    col = lax.broadcasted_iota(jnp.int32, (block, block), 1)
    bias = jnp.where(row % PACK == col % PACK, 0.0, NEG).astype(F32)
    for part in range(parts):
        rows = pl.ds(part * block, block)
        for head in range(HEADS):
            start = SHIFT + head * HD
            lo, hi = window(start)
            queries = jnp.where(head_lanes(block, lo, hi, start), q_ref[rows, lo:hi], 0)
            scores = nt_dot(queries, kv_ref[rows, lo:hi]) + bias
            expo = jnp.exp2(scores - jnp.max(scores, axis=-1, keepdims=True))
            total = jnp.sum(expo, axis=-1, keepdims=True)
            start = head * HD
            lo, hi = window(start)
            hi = min(hi, INNER)
            out = jnp.dot(expo.astype(BF16), kv_ref[rows, EXT + lo : EXT + hi], preferred_element_type=F32)
            out = (out / total).astype(BF16)
            if lo < start:
                out = jnp.where(head_lanes(block, lo, hi, start), out, acc_ref[rows, lo:hi])
            acc_ref[rows, lo:hi] = out
        for j in range(peers):
            out_refs[j][pl.ds(part * PACK, PACK), :] = acc_ref[pl.ds(part * block + j * PACK, PACK), :]


def temporal(pieces, w):
    peers = len(pieces)
    group, feat = pieces[0].shape
    tokens = peers * group
    return pl.pallas_call(
        functools.partial(temporal_kernel, peers, group),
        out_shape=[jax.ShapeDtypeStruct((group, INNER), BF16)] * peers,
        scratch_shapes=[
            pltpu.VMEM((tokens, feat), BF16),
            pltpu.VMEM((tokens, EXT), BF16),
            pltpu.VMEM((tokens, EXT + INNER), BF16),
            pltpu.VMEM((tokens, INNER), BF16),
        ],
        compiler_params=pltpu.CompilerParams(vmem_limit_bytes=VMEM_LIMIT),
        cost_estimate=pl.CostEstimate(
            flops=4 * 10**9, bytes_accessed=6 * 2**20, transcendentals=0
        ),
        name="temporal",
    )(*pieces, w)


def final_kernel(aliased, peers, group, frame_axis, xor, slab, *refs):
    in_refs = refs[:peers]
    mixed_ref, w_ref = refs[peers : peers + 2]
    out_ref, heads_ref = refs[-2:]
    step = pl.program_id(0)

    @pl.when(step == 0)
    def _():
        me = lax.axis_index(frame_axis)
        for j in range(peers):
            peer = me ^ j if xor else lax.rem(me + j, peers)
            heads_ref[pl.ds(pl.multiple_of(peer * group, PACK), group), :] = in_refs[j][...]

    heads = heads_ref[pl.ds(pl.multiple_of(step * slab, slab), slab), :]
    branch = jnp.dot(heads, w_ref[...], preferred_element_type=F32)
    out_ref[...] = (mixed_ref[...].astype(F32) + branch).astype(BF16)


def final(edges, pieces, mixed, w, slab, pixels, xor, base):
    peers = len(pieces)
    group = pieces[0].shape[0]
    feat = mixed.shape[1]
    steps = mixed.shape[0] // slab
    tile_rows = pixels // slab
    at = (lambda i: i * (tile_rows - 1)) if edges else (lambda i: i + 1)
    in_specs = [pl.BlockSpec((group, INNER), lambda i: (0, 0))] * peers + [
        pl.BlockSpec((slab, feat), lambda i: (i, 0)),
        pl.BlockSpec(w.shape, lambda i: (0, 0)),
    ]
    args = list(pieces) + [mixed, w]
    aliases = {}
    if base is not None:
        in_specs.append(pl.BlockSpec(memory_space=pl.ANY))
        aliases = {len(args): 0}
        args.append(base)
    return pl.pallas_call(
        functools.partial(final_kernel, base is not None, peers, group, "frame", xor, slab),
        grid=(steps,),
        in_specs=in_specs,
        out_specs=pl.BlockSpec((slab, feat), lambda i: (at(i), 0)),
        out_shape=jax.ShapeDtypeStruct((pixels, feat), BF16),
        scratch_shapes=[pltpu.VMEM((peers * group, INNER), BF16)],
        input_output_aliases=aliases,
        compiler_params=pltpu.CompilerParams(vmem_limit_bytes=VMEM_LIMIT),
        cost_estimate=pl.CostEstimate(
            flops=10**9, bytes_accessed=4 * 2**20, transcendentals=0
        ),
        name="final",
    )(*args)


def neighbours(kv_top, kv_bot):
    size = lax.axis_size("row")
    up = [(i, i + 1) for i in range(size - 1)]
    down = [(j, i) for i, j in up]
    return lax.ppermute(kv_bot, "row", up), lax.ppermute(kv_top, "row", down)


def exchange(pieces, xor, back):
    size = lax.axis_size("frame")
    result = [pieces[0]]
    for j in range(1, size):
        if xor:
            pairs = [(i, i ^ j) for i in range(size)]
        else:
            pairs = [(i, (i - j if back else i + j) % size) for i in range(size)]
        result.append(lax.ppermute(pieces[j], "frame", pairs))
    return result


def body(frames_in, spatial_qkv, spatial_out, temporal_qkv, temporal_out, key_tiles, tile_counts):
    _, rows_dev, columns, feat = frames_in.shape
    slab = TH * columns
    pixels = rows_dev * columns
    peers = lax.axis_size("frame")
    xor = peers & (peers - 1) == 0
    x = frames_in.reshape(pixels, feat)
    q, kv, kv_top, kv_bot = project(x, spatial_qkv, slab)
    halos = neighbours(kv_top, kv_bot)
    mixed_a, send_a = spatial(
        False, x, q, kv, None, spatial_out, key_tiles, tile_counts, slab, peers, xor
    )
    got_a = exchange(send_a, xor, False)
    mixed_b, send_b = spatial(
        True, x, q, kv, halos, spatial_out, key_tiles, tile_counts, slab, peers, xor
    )
    got_b = exchange(send_b, xor, False)
    ret_a = exchange(temporal(got_a, temporal_qkv), xor, True)
    ret_b = exchange(temporal(got_b, temporal_qkv), xor, True)
    out = final(False, ret_a, mixed_a, temporal_out, slab, pixels, xor, None)
    out = final(True, ret_b, mixed_b, temporal_out, slab, pixels, xor, out)
    return out.reshape(frames_in.shape)


def solution(mesh):
    in_specs = (
        P("frame", "row", None, None),
        P(),
        P(),
        P(),
        P(),
        P("frame", "row", None),
        P("frame", "row"),
    )
    out_specs = P("frame", "row", None, None)
    return jax.shard_map(body, mesh=mesh, in_specs=in_specs, out_specs=out_specs, check_vma=False)
```

```python
import functools

import jax
import jax.numpy as jnp
from jax import lax
from jax.experimental import pallas as pl
from jax.experimental.pallas import tpu as pltpu
from jax.sharding import PartitionSpec as P

HEADS = 8
HD = 72
TH = 4
TW = 16
LANES = 128
PACK = 16
NORM_EPS = 1e-06
NEG = -1e30
LOG2E = 1.4426950408889634
F32 = jnp.float32
BF16 = jnp.bfloat16
INNER = HEADS * HD
WIDE = -(-INNER // LANES) * LANES
PAIR = 2 * HD
PAIRS = HEADS // 2
PAIR_ROWS = PAIR + PACK
TILE = TH * TW
SPLIT = (True, True, True, True)
VMEM_LIMIT = 48 * 1024 * 1024


def params():
    return pltpu.CompilerParams(vmem_limit_bytes=VMEM_LIMIT)


def cost(flops, bytes_accessed):
    return pl.CostEstimate(flops=flops, bytes_accessed=bytes_accessed, transcendentals=0)


def nt_dot(a, b):
    return lax.dot_general(a, b, (((1,), (1,)), ((), ())), preferred_element_type=F32)


def nn_dot(a, b):
    return jnp.dot(a, b, preferred_element_type=F32)


def moments(x):
    x = x.astype(F32)
    mean = jnp.mean(x, axis=-1, keepdims=True)
    centred = x - mean
    spread = jnp.mean(centred * centred, axis=-1, keepdims=True)
    return mean, lax.rsqrt(spread + NORM_EPS)


def as_rows(column):
    return jnp.broadcast_to(column, (column.shape[0], LANES)).T[:1]


def normed_dot(x, mean, scale, w):
    ones = jnp.ones((PACK, w.shape[1]), BF16)
    return (nt_dot(x, w) - mean * nt_dot(ones, w)[:1]) * scale


def normed_dot_t(x, mean_row, scale_row, w):
    ones = jnp.ones((LANES, w.shape[1]), BF16)
    return (nt_dot(w, x) - nt_dot(w, ones)[:, :1] * mean_row) * scale_row


def tile_order(rows, columns):
    for col in range(columns // TW):
        for row in range(TH):
            yield (col * TH + row) * TW, row * columns + col * TW


def pair_window(pair):
    return pair * PAIR // LANES * LANES, -(-(pair + 1) * PAIR // LANES) * LANES


def two_heads(queries, pair):
    lo, hi = pair_window(pair)
    lane = lax.broadcasted_iota(jnp.int32, queries.shape, 1) + lo
    start = pair * PAIR
    first = jnp.where((lane >= start) & (lane < start + HD), queries, 0)
    second = jnp.where((lane >= start + HD) & (lane < start + PAIR), queries, 0)
    return jnp.concatenate([first, second], axis=0)


def project_kernel(slab, columns, x_ref, w_ref, q_ref, kv_ref, top_ref, bot_ref, xp_ref, mean_ref, rstd_ref):
    step = pl.program_id(0)
    pixels = x_ref.shape[0]

    @pl.when(step == 0)
    def _():
        for base in range(0, pixels, slab):
            for to, at in tile_order(slab, columns):
                xp_ref[pl.ds(base + to, TW), :] = x_ref[pl.ds(base + at, TW), :]
        mean, rstd = moments(xp_ref[...])
        mean_ref[...] = mean
        rstd_ref[...] = rstd
        q = normed_dot(xp_ref[...], mean, rstd * (LOG2E * HD**-0.5), w_ref[...])
        q_ref[:, :INNER] = q.astype(BF16)
        q_ref[:, INNER:] = jnp.zeros((pixels, WIDE - INNER), BF16)

    @pl.when(step == 1)
    def _():
        k = normed_dot(xp_ref[...], mean_ref[...], rstd_ref[...], w_ref[...])
        kv_ref[:, :INNER] = k.astype(BF16)
        kv_ref[:, INNER:WIDE] = jnp.zeros((pixels, WIDE - INNER), BF16)

    @pl.when(step == 2)
    def _():
        mean, rstd = as_rows(mean_ref[...]), as_rows(rstd_ref[...])
        v = normed_dot_t(xp_ref[...], mean, rstd, w_ref[...]).astype(BF16)
        for base in range(0, pixels, slab):
            for part, row in enumerate(range(0, INNER, slab)):
                rows = min(slab, INNER - row)
                at = WIDE + part * slab
                kv_ref[pl.ds(base, rows), at : at + slab] = v[row : row + rows, base : base + slab]
                if rows < slab:
                    kv_ref[pl.ds(base + rows, slab - rows), at : at + slab] = jnp.zeros(
                        (slab - rows, slab), BF16
                    )
        top_ref[...] = kv_ref[:slab, :]
        bot_ref[...] = kv_ref[pixels - slab :, :]


def project(x, w, slab, columns):
    pixels, feat = x.shape
    kv_dim = WIDE + -(-INNER // slab) * slab
    whole = lambda *shape: pl.BlockSpec(shape, lambda i: (0, 0))
    return pl.pallas_call(
        functools.partial(project_kernel, slab, columns),
        grid=(3,),
        in_specs=[whole(pixels, feat), pl.BlockSpec((INNER, feat), lambda i: (i, 0))],
        out_specs=[
            whole(pixels, WIDE),
            whole(pixels, kv_dim),
            whole(slab, kv_dim),
            whole(slab, kv_dim),
        ],
        out_shape=[
            jax.ShapeDtypeStruct((pixels, WIDE), BF16),
            jax.ShapeDtypeStruct((pixels, kv_dim), BF16),
            jax.ShapeDtypeStruct((slab, kv_dim), BF16),
            jax.ShapeDtypeStruct((slab, kv_dim), BF16),
        ],
        scratch_shapes=[
            pltpu.VMEM((pixels, feat), BF16),
            pltpu.VMEM((pixels, 1), F32),
            pltpu.VMEM((pixels, 1), F32),
        ],
        compiler_params=params(),
        cost_estimate=cost(5 * 10**9, 12 * 2**20),
        name="project",
    )(x, w)


def visible_bits(tile, count, global_row, tile_cols, slot_num, targets_ref):
    bits = jnp.int32(0)
    for slot in range(slot_num):
        target = targets_ref[0, tile, slot]
        cand = (lax.div(target, tile_cols) - global_row + 1) * tile_cols + lax.rem(target, tile_cols)
        bits = bits | jnp.where(slot < count, jnp.left_shift(1, cand), 0)
    return bits


def hidden(bits, index):
    return (1 - (jnp.right_shift(bits, index) & 1)).astype(F32) * NEG


def spatial_kernel(
    edges, first_row, group, peers, xor, split, tile_rows, columns,
    targets_ref, counts_ref, x_ref, q_ref, prev_ref, mid_ref, next_ref, *rest,
):
    if edges:
        top_ref, bot_ref = rest[:2]
        rest = rest[2:]
    w_ref, mixed_ref = rest[:2]
    rest = rest[2:]
    if split:
        send_refs, rest = rest[:peers], rest[peers:]
    p_ref, v_ref, acc_ref, out_ref = rest[:4]
    rest = rest[4:]
    step = pl.program_id(0)
    steps = pl.num_programs(0)
    slab, feat = x_ref.shape
    tile_cols = columns // TW
    slot_num = targets_ref.shape[2]

    @pl.when(step == 0)
    def _():
        p_ref[...] = jnp.zeros(p_ref.shape, BF16)
        for pair in range(PAIRS):
            v_ref[:, pair * PAIR_ROWS + PAIR : (pair + 1) * PAIR_ROWS, :] = jnp.ones(
                (3, PACK, slab), BF16
            )

    if edges:
        prev_s, next_s = rest

        @pl.when(step == 0)
        def _():
            prev_s[...] = top_ref[...]
            next_s[...] = next_ref[...]

        @pl.when(step != 0)
        def _():
            prev_s[...] = prev_ref[...]
            next_s[...] = bot_ref[...]

        kv_refs = (prev_s, mid_ref, next_s)
        tile_row = step * (tile_rows - 1)
    else:
        kv_refs = (prev_ref, mid_ref, next_ref)
        tile_row = step + first_row
    global_row = lax.axis_index("row") * tile_rows + tile_row

    for j, ref in enumerate(kv_refs):
        for pair in range(PAIRS):
            done = 0
            while done < PAIR:
                row = pair * PAIR + done
                part, inside = row // slab, row % slab
                rows = min(PAIR - done, slab - inside)
                at = WIDE + part * slab
                v_ref[j, pl.ds(pair * PAIR_ROWS + done, rows), :] = ref[
                    pl.ds(inside, rows), at : at + slab
                ]
                done += rows

    left = lax.broadcasted_iota(jnp.int32, (1, 4 * TILE), 1) % (2 * TILE) < TILE
    for duo in range(tile_cols // 2):
        bits = []
        for tile in (2 * duo, 2 * duo + 1):
            tile = tile_row * tile_cols + tile
            bits.append(
                visible_bits(tile, counts_ref[0, tile], global_row, tile_cols, slot_num, targets_ref)
            )
        lowest, highest = max(2 * duo - 1, 0), min(2 * duo + 2, tile_cols - 1)
        span = range(lowest, highest + 1)
        bias = {}
        for j in range(3):
            for col in span:
                at = j * tile_cols + col
                bias[j, col] = jnp.where(left, hidden(bits[0], at), hidden(bits[1], at))
        for pair in range(PAIRS):
            lo, hi = pair_window(pair)
            queries = two_heads(q_ref[2 * duo * TILE : (2 * duo + 2) * TILE, lo:hi], pair)
            scores = {}
            for j, ref in enumerate(kv_refs):
                part = nt_dot(ref[lowest * TILE : (highest + 1) * TILE, lo:hi], queries)
                for col in span:
                    at = (col - lowest) * TILE
                    scores[j, col] = part[at : at + TILE] + bias[j, col]
            top = functools.reduce(jnp.maximum, scores.values())
            top = jnp.max(top, axis=0, keepdims=True)
            for (j, col), score in scores.items():
                at = j * slab + col * TILE
                p_ref[duo, at : at + TILE, :] = jnp.exp2(score - top).astype(BF16)
            out = sum(
                nn_dot(
                    v_ref[j, pair * PAIR_ROWS : (pair + 1) * PAIR_ROWS, :],
                    p_ref[duo, j * slab : (j + 1) * slab, :],
                )
                for j in range(3)
            )
            out = out[:PAIR] / out[PAIR : PAIR + 1]
            lanes = slice(2 * duo * TILE, (2 * duo + 2) * TILE)
            acc_ref[pair * PAIR : pair * PAIR + HD, lanes] = out[:HD, : 2 * TILE]
            acc_ref[pair * PAIR + HD : (pair + 1) * PAIR, lanes] = out[HD:, 2 * TILE :]

    branch = nn_dot(acc_ref[...].T.astype(BF16), w_ref[...])
    base = step * slab
    for to, at in tile_order(slab, columns):
        mixed = (x_ref[pl.ds(at, TW), :].astype(F32) + branch[to : to + TW]).astype(BF16)
        mixed_ref[pl.ds(to, TW), :] = mixed
        if split:
            out_ref[pl.ds(pl.multiple_of(base + to, TW), TW), :] = mixed

    if split:

        @pl.when(step == steps - 1)
        def _():
            me = lax.axis_index("frame")
            for j in range(peers):
                peer = me ^ j if xor else lax.rem(me + j, peers)
                send_refs[j][...] = out_ref[pl.ds(pl.multiple_of(peer * group, PACK), group), :]


def spatial(edges, split, x, q, kv, halos, w, targets, counts, slab, columns, peers, xor):
    pixels, feat = x.shape
    tile_rows = pixels // slab
    steps = 2 if edges else tile_rows - 2
    group = steps * slab // peers
    kv_dim = kv.shape[1]
    if edges:
        at = lambda i: i * (tile_rows - 1)
        prev_at = lambda i: tile_rows - 2
        next_at = lambda i: 1
    else:
        at = lambda i: i + 1
        prev_at = lambda i: i
        next_at = lambda i: i + 2
    smem = pl.BlockSpec(memory_space=pltpu.SMEM)
    whole = lambda *shape: pl.BlockSpec(shape, lambda i: (0, 0))
    in_specs = [
        smem,
        smem,
        pl.BlockSpec((slab, feat), lambda i: (at(i), 0)),
        pl.BlockSpec((slab, WIDE), lambda i: (at(i), 0)),
        pl.BlockSpec((slab, kv_dim), lambda i: (prev_at(i), 0)),
        pl.BlockSpec((slab, kv_dim), lambda i: (at(i), 0)),
        pl.BlockSpec((slab, kv_dim), lambda i: (next_at(i), 0)),
    ]
    args = [targets, counts, x, q, kv, kv, kv]
    scratch = [
        pltpu.VMEM((columns // TW // 2, 3 * slab, 4 * TILE), BF16),
        pltpu.VMEM((3, PAIRS * PAIR_ROWS, slab), BF16),
        pltpu.VMEM((INNER, slab), F32),
        pltpu.VMEM((steps * slab, feat), BF16),
    ]
    if edges:
        in_specs += [whole(slab, kv_dim)] * 2
        args += list(halos)
        scratch += [pltpu.VMEM((slab, kv_dim), BF16)] * 2
    in_specs.append(whole(*w.shape))
    args.append(w)
    out_specs = [pl.BlockSpec((slab, feat), lambda i: (i, 0))]
    out_shape = [jax.ShapeDtypeStruct((steps * slab, feat), BF16)]
    if split:
        out_specs += [whole(group, feat)] * peers
        out_shape += [jax.ShapeDtypeStruct((group, feat), BF16)] * peers
    outs = pl.pallas_call(
        functools.partial(
            spatial_kernel, edges, 0 if edges else 1, group, peers, xor, split, tile_rows, columns
        ),
        grid=(steps,),
        in_specs=in_specs,
        out_specs=out_specs,
        out_shape=out_shape,
        scratch_shapes=scratch,
        compiler_params=params(),
        cost_estimate=cost(6 * 10**9, 8 * 2**20),
        name="spatial_edges" if edges else "spatial_inner",
    )(*args)
    return outs[0], outs[1:] if split else [outs[0]]


def temporal_kernel(peers, group, split_in, split_out, *refs):
    count = peers if split_in else 1
    in_refs, w_ref, refs = refs[:count], refs[count], refs[count + 1 :]
    count = peers if split_out else 1
    out_refs = refs[:count]
    x_ref, q_ref, k_ref, v_ref, acc_ref = refs[count:]
    block = peers * PACK
    parts = group // PACK
    tokens = peers * group
    for part in range(parts):
        for j in range(peers):
            to = pl.ds(part * block + j * PACK, PACK)
            if split_in:
                x_ref[to, :] = in_refs[j][pl.ds(part * PACK, PACK), :]
            else:
                x_ref[to, :] = in_refs[0][pl.ds(j * group + part * PACK, PACK), :]
    x = x_ref[...]
    mean, rstd = moments(x)
    q = normed_dot(x, mean, rstd * (LOG2E * HD**-0.5), w_ref[:INNER, :])
    q_ref[:, :INNER] = q.astype(BF16)
    q_ref[:, INNER:] = jnp.zeros((tokens, WIDE - INNER), BF16)
    k_ref[:, :INNER] = normed_dot(x, mean, rstd, w_ref[INNER : 2 * INNER, :]).astype(BF16)
    k_ref[:, INNER:] = jnp.zeros((tokens, WIDE - INNER), BF16)
    v = normed_dot_t(x, as_rows(mean), as_rows(rstd), w_ref[2 * INNER :, :]).astype(BF16)
    for pair in range(PAIRS):
        at = pair * PAIR_ROWS
        v_ref[at : at + PAIR, :] = v[pair * PAIR : (pair + 1) * PAIR]
        v_ref[at + PAIR : at + PAIR_ROWS, :] = jnp.ones((PACK, tokens), BF16)
    row = lax.broadcasted_iota(jnp.int32, (block, 2 * block), 0)
    col = lax.broadcasted_iota(jnp.int32, (block, 2 * block), 1)
    bias = jnp.where(row % PACK == col % PACK, 0.0, NEG).astype(F32)
    for part in range(parts):
        at = part * block
        for pair in range(PAIRS):
            lo, hi = pair_window(pair)
            queries = two_heads(q_ref[at : at + block, lo:hi], pair)
            scores = nt_dot(k_ref[at : at + block, lo:hi], queries) + bias
            expo = jnp.exp2(scores - jnp.max(scores, axis=0, keepdims=True)).astype(BF16)
            out = nn_dot(v_ref[pair * PAIR_ROWS : (pair + 1) * PAIR_ROWS, at : at + block], expo)
            out = out[:PAIR] / out[PAIR : PAIR + 1]
            acc_ref[pair * PAIR : pair * PAIR + HD, at : at + block] = out[:HD, :block]
            acc_ref[pair * PAIR + HD : (pair + 1) * PAIR, at : at + block] = out[HD:, block:]
        heads = acc_ref[:, at : at + block].T.astype(BF16)
        for j in range(peers):
            rows = heads[j * PACK : (j + 1) * PACK]
            if split_out:
                out_refs[j][pl.ds(part * PACK, PACK), :] = rows
            else:
                out_refs[0][pl.ds(j * group + part * PACK, PACK), :] = rows


def temporal(pieces, w, peers, split_out):
    split_in = len(pieces) > 1
    feat = pieces[0].shape[1]
    tokens = sum(piece.shape[0] for piece in pieces)
    group = tokens // peers
    if split_out:
        out_shape = [jax.ShapeDtypeStruct((group, INNER), BF16)] * peers
    else:
        out_shape = [jax.ShapeDtypeStruct((tokens, INNER), BF16)]
    return pl.pallas_call(
        functools.partial(temporal_kernel, peers, group, split_in, split_out),
        out_shape=out_shape,
        scratch_shapes=[
            pltpu.VMEM((tokens, feat), BF16),
            pltpu.VMEM((tokens, WIDE), BF16),
            pltpu.VMEM((tokens, WIDE), BF16),
            pltpu.VMEM((PAIRS * PAIR_ROWS, tokens), BF16),
            pltpu.VMEM((INNER, tokens), F32),
        ],
        compiler_params=params(),
        cost_estimate=cost(4 * 10**9, 6 * 2**20),
        name="temporal",
    )(*pieces, w)


def final_kernel(peers, group, xor, split, columns, *refs):
    count = peers if split else 1
    in_refs = refs[:count]
    mixed_ref, w_ref = refs[count : count + 2]
    out_ref, heads_ref = refs[-2:]
    step = pl.program_id(0)
    slab = mixed_ref.shape[0]

    if split:

        @pl.when(step == 0)
        def _():
            me = lax.axis_index("frame")
            for j in range(peers):
                peer = me ^ j if xor else lax.rem(me + j, peers)
                heads_ref[pl.ds(pl.multiple_of(peer * group, PACK), group), :] = in_refs[j][...]

        heads = heads_ref[pl.ds(pl.multiple_of(step * slab, slab), slab), :]
    else:
        heads = in_refs[0][pl.ds(pl.multiple_of(step * slab, slab), slab), :]
    result = mixed_ref[...].astype(F32) + nn_dot(heads, w_ref[...])
    for to, at in tile_order(slab, columns):
        out_ref[pl.ds(at, TW), :] = result[to : to + TW].astype(BF16)


def final(edges, pieces, mixed, w, slab, columns, pixels, peers, xor, base):
    split = len(pieces) > 1
    group = mixed.shape[0] // peers
    feat = mixed.shape[1]
    steps = mixed.shape[0] // slab
    tile_rows = pixels // slab
    at = (lambda i: i * (tile_rows - 1)) if edges else (lambda i: i + 1)
    whole = lambda *shape: pl.BlockSpec(shape, lambda i: (0, 0))
    in_specs = [whole(*piece.shape) for piece in pieces] + [
        pl.BlockSpec((slab, feat), lambda i: (i, 0)),
        whole(*w.shape),
    ]
    args = list(pieces) + [mixed, w]
    aliases = {}
    if base is not None:
        in_specs.append(pl.BlockSpec(memory_space=pl.ANY))
        aliases = {len(args): 0}
        args.append(base)
    return pl.pallas_call(
        functools.partial(final_kernel, peers, group, xor, split, columns),
        grid=(steps,),
        in_specs=in_specs,
        out_specs=pl.BlockSpec((slab, feat), lambda i: (at(i), 0)),
        out_shape=jax.ShapeDtypeStruct((pixels, feat), BF16),
        scratch_shapes=[pltpu.VMEM((peers * group, INNER), BF16)],
        input_output_aliases=aliases,
        compiler_params=params(),
        cost_estimate=cost(10**9, 4 * 2**20),
        name="final",
    )(*args)


def neighbours(kv_top, kv_bot):
    size = lax.axis_size("row")
    up = [(i, i + 1) for i in range(size - 1)]
    down = [(j, i) for i, j in up]
    return lax.ppermute(kv_bot, "row", up), lax.ppermute(kv_top, "row", down)


def exchange(pieces, xor, back):
    size = lax.axis_size("frame")
    if len(pieces) == 1:
        whole = pieces[0].reshape(size, -1, pieces[0].shape[-1])
        got = lax.all_to_all(whole, "frame", split_axis=0, concat_axis=0)
        return [got.reshape(pieces[0].shape)]
    result = [pieces[0]]
    for j in range(1, size):
        if xor:
            pairs = [(i, i ^ j) for i in range(size)]
        else:
            pairs = [(i, (i - j if back else i + j) % size) for i in range(size)]
        result.append(lax.ppermute(pieces[j], "frame", pairs))
    return result


def body(frames_in, spatial_qkv, spatial_out, temporal_qkv, temporal_out, key_tiles, tile_counts):
    _, rows_dev, columns, feat = frames_in.shape
    slab = TH * columns
    pixels = rows_dev * columns
    peers = lax.axis_size("frame")
    xor = peers & (peers - 1) == 0
    x = frames_in.reshape(pixels, feat)
    q, kv, kv_top, kv_bot = project(x, spatial_qkv.T, slab, columns)
    halos = neighbours(kv_top, kv_bot)
    tiles = (spatial_out, key_tiles, tile_counts, slab, columns, peers, xor)
    mixed_a, send_a = spatial(False, SPLIT[0], x, q, kv, None, *tiles)
    got_a = exchange(send_a, xor, False)
    mixed_b, send_b = spatial(True, SPLIT[1], x, q, kv, halos, *tiles)
    got_b = exchange(send_b, xor, False)
    ret_a = exchange(temporal(got_a, temporal_qkv.T, peers, SPLIT[2]), xor, True)
    ret_b = exchange(temporal(got_b, temporal_qkv.T, peers, SPLIT[3]), xor, True)
    sizes = (temporal_out, slab, columns, pixels, peers, xor)
    out = final(False, ret_a, mixed_a, *sizes, None)
    out = final(True, ret_b, mixed_b, *sizes, out)
    return out.reshape(frames_in.shape)


def solution(mesh):
    in_specs = (
        P("frame", "row", None, None),
        P(),
        P(),
        P(),
        P(),
        P("frame", "row", None),
        P("frame", "row"),
    )
    out_specs = P("frame", "row", None, None)
    return jax.shard_map(body, mesh=mesh, in_specs=in_specs, out_specs=out_specs, check_vma=False)
```

```python
import functools

import jax
import jax.numpy as jnp
from jax import lax
from jax.experimental import pallas as pl
from jax.experimental.pallas import tpu as pltpu
from jax.sharding import PartitionSpec as P

HEADS = 8
HD = 72
TH = 4
TW = 16
LANES = 128
PACK = 16
NORM_EPS = 1e-06
NEG = -1e30
LOG2E = 1.4426950408889634
F32 = jnp.float32
BF16 = jnp.bfloat16
INNER = HEADS * HD
WIDE = -(-INNER // LANES) * LANES
PAIR = 2 * HD
PAIRS = HEADS // 2
PAIR_ROWS = PAIR + PACK
TILE = TH * TW
SPLIT = (True, True, True, True)
VMEM_LIMIT = 48 * 1024 * 1024


def params():
    return pltpu.CompilerParams(vmem_limit_bytes=VMEM_LIMIT)


def cost(flops, bytes_accessed):
    return pl.CostEstimate(flops=flops, bytes_accessed=bytes_accessed, transcendentals=0)


def nt_dot(a, b):
    return lax.dot_general(a, b, (((1,), (1,)), ((), ())), preferred_element_type=F32)


def nn_dot(a, b):
    return jnp.dot(a, b, preferred_element_type=F32)


def moments(x):
    x = x.astype(F32)
    mean = jnp.mean(x, axis=-1, keepdims=True)
    centred = x - mean
    spread = jnp.mean(centred * centred, axis=-1, keepdims=True)
    return mean, lax.rsqrt(spread + NORM_EPS)


def as_rows(column):
    return jnp.broadcast_to(column, (column.shape[0], LANES)).T[:1]


def tile_order(rows, columns):
    for col in range(columns // TW):
        for row in range(TH):
            yield (col * TH + row) * TW, row * columns + col * TW


def pair_window(pair):
    return pair * PAIR // LANES * LANES, -(-(pair + 1) * PAIR // LANES) * LANES


def two_heads(queries, pair):
    lo, hi = pair_window(pair)
    lane = lax.broadcasted_iota(jnp.int32, queries.shape, 1) + lo
    start = pair * PAIR
    first = jnp.where((lane >= start) & (lane < start + HD), queries, 0)
    second = jnp.where((lane >= start + HD) & (lane < start + PAIR), queries, 0)
    return jnp.concatenate([first, second], axis=0)


def split_queries_keys(prod):
    keys = prod[:, INNER // LANES * LANES :]
    shift = INNER % LANES
    if shift:
        keys = pltpu.roll(keys, keys.shape[1] - shift, 1)
    return prod[:, :WIDE], keys


def column_sums(w):
    return nt_dot(jnp.ones((PACK, w.shape[1]), BF16), w)[:1]


def store_values(v_ref, values, lanes):
    for pair in range(PAIRS):
        at = pair * PAIR_ROWS
        v_ref[at : at + PAIR, lanes] = values[pair * PAIR : (pair + 1) * PAIR]
        v_ref[at + PAIR : at + PAIR_ROWS, lanes] = jnp.ones((PACK, values.shape[1]), BF16)


def packed_keys(slab):
    per = slab // LANES
    for piece in range(WIDE // LANES):
        lanes = slice(piece * LANES, (piece + 1) * LANES)
        if piece < WIDE // slab * per:
            yield slice(0, slab), lanes, piece // per * slab, piece % per * LANES
        else:
            at = WIDE // slab * slab
            for part in range(per):
                rows = slab // per
                yield slice(part * rows, (part + 1) * rows), lanes, at, part * LANES


def pack_halo(halo_ref, k_ref, v_ref):
    slab = k_ref.shape[0]
    size = v_ref.shape[0]
    halo_ref[:size, :] = v_ref[...]
    for rows, lanes, row, lane in packed_keys(slab):
        count = rows.stop - rows.start
        halo_ref[size + row : size + row + count, lane : lane + LANES] = k_ref[rows, lanes]


def unpack_halo(halo_ref, k_ref, v_ref):
    slab = k_ref.shape[0]
    size = v_ref.shape[0]
    v_ref[...] = halo_ref[:size, :]
    for rows, lanes, row, lane in packed_keys(slab):
        count = rows.stop - rows.start
        k_ref[rows, lanes] = halo_ref[size + row : size + row + count, lane : lane + LANES]


def project_kernel(
    columns, x_ref, w_hbm, q_ref, k_ref, v_ref, top_ref, bot_ref, w_ref, xp_ref, sum_ref, col_ref, sem
):
    step = pl.program_id(0)
    slab = x_ref.shape[0]
    first = pltpu.make_async_copy(
        w_hbm.at[pl.ds(0, 2 * INNER)], w_ref.at[pl.ds(0, 2 * INNER)], sem.at[0]
    )
    second = pltpu.make_async_copy(
        w_hbm.at[pl.ds(2 * INNER, INNER)], w_ref.at[pl.ds(2 * INNER, INNER)], sem.at[1]
    )

    @pl.when(step == 0)
    def _():
        first.start()
        second.start()

    for to, at in tile_order(slab, columns):
        xp_ref[pl.ds(to, TW), :] = x_ref[pl.ds(at, TW), :]

    @pl.when(step == 0)
    def _():
        first.wait()
        second.wait()
        sum_ref[...] = column_sums(w_ref[: 2 * INNER, :])
        ones = jnp.ones((LANES, w_ref.shape[1]), BF16)
        col_ref[...] = nt_dot(w_ref[2 * INNER :, :], ones)[:, :1]

    x = xp_ref[...]
    mean, rstd = moments(x)
    prod = (nt_dot(x, w_ref[: 2 * INNER, :]) - mean * sum_ref[...]) * rstd
    q, k = split_queries_keys(prod)
    q_ref[...] = (q * (LOG2E * HD**-0.5)).astype(BF16)
    k_ref[...] = k.astype(BF16)
    values = nt_dot(w_ref[2 * INNER :, :], x) - col_ref[...] * as_rows(mean)
    store_values(v_ref, (values * as_rows(rstd)).astype(BF16), slice(None))

    @pl.when(step == 0)
    def _():
        pack_halo(top_ref, k_ref, v_ref)

    @pl.when(step == pl.num_programs(0) - 1)
    def _():
        pack_halo(bot_ref, k_ref, v_ref)


def project(x, w, slab, columns):
    pixels, feat = x.shape
    steps = pixels // slab
    v_rows = PAIRS * PAIR_ROWS
    halo_rows = v_rows + WIDE
    return pl.pallas_call(
        functools.partial(project_kernel, columns),
        grid=(steps,),
        in_specs=[
            pl.BlockSpec((slab, feat), lambda i: (i, 0)),
            pl.BlockSpec(memory_space=pl.ANY),
        ],
        out_specs=[
            pl.BlockSpec((slab, WIDE), lambda i: (i, 0)),
            pl.BlockSpec((slab, WIDE), lambda i: (i, 0)),
            pl.BlockSpec((v_rows, slab), lambda i: (i, 0)),
            pl.BlockSpec((halo_rows, slab), lambda i: (0, 0)),
            pl.BlockSpec((halo_rows, slab), lambda i: (0, 0)),
        ],
        out_shape=[
            jax.ShapeDtypeStruct((pixels, WIDE), BF16),
            jax.ShapeDtypeStruct((pixels, WIDE), BF16),
            jax.ShapeDtypeStruct((steps * v_rows, slab), BF16),
            jax.ShapeDtypeStruct((halo_rows, slab), BF16),
            jax.ShapeDtypeStruct((halo_rows, slab), BF16),
        ],
        scratch_shapes=[
            pltpu.VMEM(w.shape, BF16),
            pltpu.VMEM((slab, feat), BF16),
            pltpu.VMEM((1, 2 * INNER), F32),
            pltpu.VMEM((INNER, 1), F32),
            pltpu.SemaphoreType.DMA((2,)),
        ],
        compiler_params=params(),
        cost_estimate=cost(5 * 10**9, 12 * 2**20),
        name="project",
    )(x, w)


def visible_bits(tile, count, global_row, tile_cols, slot_num, targets_ref):
    bits = jnp.int32(0)
    for slot in range(slot_num):
        target = targets_ref[0, tile, slot]
        cand = (lax.div(target, tile_cols) - global_row + 1) * tile_cols + lax.rem(target, tile_cols)
        bits = bits | jnp.where(slot < count, jnp.left_shift(1, cand), 0)
    return bits


def hidden(bits, index):
    return (1 - (jnp.right_shift(bits, index) & 1)).astype(F32) * NEG


def spatial_kernel(
    edges, first_row, group, peers, xor, split, tile_rows, columns,
    targets_ref, counts_ref, x_ref, q_ref, *rest,
):
    k_refs, v_refs, rest = rest[:3], rest[3:6], rest[6:]
    if edges:
        top_ref, bot_ref = rest[:2]
        rest = rest[2:]
    w_ref, mixed_ref = rest[:2]
    rest = rest[2:]
    if split:
        send_refs, rest = rest[:peers], rest[peers:]
    p_ref, acc_ref, out_ref = rest[:3]
    rest = rest[3:]
    step = pl.program_id(0)
    steps = pl.num_programs(0)
    slab, feat = x_ref.shape
    tile_cols = columns // TW
    slot_num = targets_ref.shape[2]

    @pl.when(step == 0)
    def _():
        p_ref[...] = jnp.zeros(p_ref.shape, BF16)

    if edges:
        (k_prev, k_next, v_prev, v_next) = rest

        @pl.when(step == 0)
        def _():
            unpack_halo(top_ref, k_prev, v_prev)
            k_next[...] = k_refs[2][...]
            v_next[...] = v_refs[2][...]

        @pl.when(step != 0)
        def _():
            k_prev[...] = k_refs[0][...]
            v_prev[...] = v_refs[0][...]
            unpack_halo(bot_ref, k_next, v_next)

        k_refs = (k_prev, k_refs[1], k_next)
        v_refs = (v_prev, v_refs[1], v_next)
        tile_row = step * (tile_rows - 1)
    else:
        tile_row = step + first_row
    global_row = lax.axis_index("row") * tile_rows + tile_row

    left = lax.broadcasted_iota(jnp.int32, (1, 4 * TILE), 1) % (2 * TILE) < TILE
    for duo in range(tile_cols // 2):
        bits = []
        for tile in (2 * duo, 2 * duo + 1):
            tile = tile_row * tile_cols + tile
            bits.append(
                visible_bits(tile, counts_ref[0, tile], global_row, tile_cols, slot_num, targets_ref)
            )
        lowest, highest = max(2 * duo - 1, 0), min(2 * duo + 2, tile_cols - 1)
        span = range(lowest, highest + 1)
        bias = {}
        for j in range(3):
            for col in span:
                at = j * tile_cols + col
                bias[j, col] = jnp.where(left, hidden(bits[0], at), hidden(bits[1], at))
        for pair in range(PAIRS):
            lo, hi = pair_window(pair)
            queries = two_heads(q_ref[2 * duo * TILE : (2 * duo + 2) * TILE, lo:hi], pair)
            scores = {}
            for j, ref in enumerate(k_refs):
                part = nt_dot(ref[lowest * TILE : (highest + 1) * TILE, lo:hi], queries)
                for col in span:
                    at = (col - lowest) * TILE
                    scores[j, col] = part[at : at + TILE] + bias[j, col]
            top = functools.reduce(jnp.maximum, scores.values())
            top = jnp.max(top, axis=0, keepdims=True)
            for (j, col), score in scores.items():
                at = j * slab + col * TILE
                p_ref[duo * PAIRS + pair, at : at + TILE, :] = jnp.exp2(score - top).astype(BF16)

    for duo in range(tile_cols // 2):
        for pair in range(PAIRS):
            out = sum(
                nn_dot(
                    ref[pair * PAIR_ROWS : (pair + 1) * PAIR_ROWS, :],
                    p_ref[duo * PAIRS + pair, j * slab : (j + 1) * slab, :],
                )
                for j, ref in enumerate(v_refs)
            )
            out = out[:PAIR] * (1.0 / out[PAIR : PAIR + 1])
            lanes = slice(2 * duo * TILE, (2 * duo + 2) * TILE)
            acc_ref[pair * PAIR : pair * PAIR + HD, lanes] = out[:HD, : 2 * TILE]
            acc_ref[pair * PAIR + HD : (pair + 1) * PAIR, lanes] = out[HD:, 2 * TILE :]

    branch = nn_dot(acc_ref[...].T.astype(BF16), w_ref[...])
    base = step * slab
    for to, at in tile_order(slab, columns):
        mixed = (x_ref[pl.ds(at, TW), :].astype(F32) + branch[to : to + TW]).astype(BF16)
        mixed_ref[pl.ds(to, TW), :] = mixed
        if split:
            out_ref[pl.ds(pl.multiple_of(base + to, TW), TW), :] = mixed

    if split:

        @pl.when(step == steps - 1)
        def _():
            me = lax.axis_index("frame")
            for j in range(peers):
                peer = me ^ j if xor else lax.rem(me + j, peers)
                send_refs[j][...] = out_ref[pl.ds(pl.multiple_of(peer * group, PACK), group), :]


def spatial(edges, split, x, q, k, v, halos, w, targets, counts, slab, columns, peers, xor):
    pixels, feat = x.shape
    tile_rows = pixels // slab
    steps = 2 if edges else tile_rows - 2
    group = steps * slab // peers
    v_rows = PAIRS * PAIR_ROWS
    if edges:
        at = lambda i: i * (tile_rows - 1)
        prev_at = lambda i: tile_rows - 2
        next_at = lambda i: 1
    else:
        at = lambda i: i + 1
        prev_at = lambda i: i
        next_at = lambda i: i + 2
    smem = pl.BlockSpec(memory_space=pltpu.SMEM)
    whole = lambda *shape: pl.BlockSpec(shape, lambda i: (0, 0))
    in_specs = [
        smem,
        smem,
        pl.BlockSpec((slab, feat), lambda i: (at(i), 0)),
        pl.BlockSpec((slab, WIDE), lambda i: (at(i), 0)),
    ]
    for block in ((slab, WIDE), (v_rows, slab)):
        in_specs += [
            pl.BlockSpec(block, lambda i: (prev_at(i), 0)),
            pl.BlockSpec(block, lambda i: (at(i), 0)),
            pl.BlockSpec(block, lambda i: (next_at(i), 0)),
        ]
    args = [targets, counts, x, q, k, k, k, v, v, v]
    scratch = [
        pltpu.VMEM((columns // TW // 2 * PAIRS, 3 * slab, 4 * TILE), BF16),
        pltpu.VMEM((INNER, slab), F32),
        pltpu.VMEM((steps * slab, feat), BF16),
    ]
    if edges:
        in_specs += [whole(*halos[0].shape)] * 2
        args += list(halos)
        scratch += [pltpu.VMEM((slab, WIDE), BF16)] * 2 + [pltpu.VMEM((v_rows, slab), BF16)] * 2
    in_specs.append(whole(*w.shape))
    args.append(w)
    out_specs = [pl.BlockSpec((slab, feat), lambda i: (i, 0))]
    out_shape = [jax.ShapeDtypeStruct((steps * slab, feat), BF16)]
    if split:
        out_specs += [whole(group, feat)] * peers
        out_shape += [jax.ShapeDtypeStruct((group, feat), BF16)] * peers
    outs = pl.pallas_call(
        functools.partial(
            spatial_kernel, edges, 0 if edges else 1, group, peers, xor, split, tile_rows, columns
        ),
        grid=(steps,),
        in_specs=in_specs,
        out_specs=out_specs,
        out_shape=out_shape,
        scratch_shapes=scratch,
        compiler_params=params(),
        cost_estimate=cost(6 * 10**9, 8 * 2**20),
        name="spatial_edges" if edges else "spatial_inner",
    )(*args)
    return outs[0], outs[1:] if split else [outs[0]]


def temporal_kernel(peers, group, split_in, split_out, *refs):
    count = peers if split_in else 1
    in_refs, w_ref, refs = refs[:count], refs[count], refs[count + 1 :]
    count = peers if split_out else 1
    out_refs = refs[:count]
    x_ref, q_ref, k_ref, v_ref, p_ref, acc_ref = refs[count:]
    block = peers * PACK
    parts = group // PACK
    tokens = peers * group
    for part in range(parts):
        for j in range(peers):
            to = pl.ds(part * block + j * PACK, PACK)
            if split_in:
                x_ref[to, :] = in_refs[j][pl.ds(part * PACK, PACK), :]
            else:
                x_ref[to, :] = in_refs[0][pl.ds(j * group + part * PACK, PACK), :]
    x = x_ref[...]
    mean, rstd = moments(x)
    prod = (nt_dot(x, w_ref[: 2 * INNER, :]) - mean * column_sums(w_ref[: 2 * INNER, :])) * rstd
    q, k = split_queries_keys(prod)
    q_ref[...] = (q * (LOG2E * HD**-0.5)).astype(BF16)
    k_ref[...] = k.astype(BF16)
    w_values = w_ref[2 * INNER :, :]
    col = nt_dot(w_values, jnp.ones((LANES, w_values.shape[1]), BF16))[:, :1]
    values = (nt_dot(w_values, x) - col * as_rows(mean)) * as_rows(rstd)
    store_values(v_ref, values.astype(BF16), slice(None))
    row = lax.broadcasted_iota(jnp.int32, (block, 2 * block), 0)
    col = lax.broadcasted_iota(jnp.int32, (block, 2 * block), 1)
    bias = jnp.where(row % PACK == col % PACK, 0.0, NEG).astype(F32)
    for part in range(parts):
        at = part * block
        for pair in range(PAIRS):
            lo, hi = pair_window(pair)
            queries = two_heads(q_ref[at : at + block, lo:hi], pair)
            scores = nt_dot(k_ref[at : at + block, lo:hi], queries) + bias
            expo = jnp.exp2(scores - jnp.max(scores, axis=0, keepdims=True))
            p_ref[part * PAIRS + pair] = expo.astype(BF16)
    for part in range(parts):
        at = part * block
        for pair in range(PAIRS):
            weights = v_ref[pair * PAIR_ROWS : (pair + 1) * PAIR_ROWS, at : at + block]
            out = nn_dot(weights, p_ref[part * PAIRS + pair])
            out = out[:PAIR] * (1.0 / out[PAIR : PAIR + 1])
            acc_ref[pair * PAIR : pair * PAIR + HD, at : at + block] = out[:HD, :block]
            acc_ref[pair * PAIR + HD : (pair + 1) * PAIR, at : at + block] = out[HD:, block:]
    for part in range(parts):
        at = part * block
        heads = acc_ref[:, at : at + block].T.astype(BF16)
        for j in range(peers):
            rows = heads[j * PACK : (j + 1) * PACK]
            if split_out:
                out_refs[j][pl.ds(part * PACK, PACK), :] = rows
            else:
                out_refs[0][pl.ds(j * group + part * PACK, PACK), :] = rows


def temporal(pieces, w, peers, split_out):
    split_in = len(pieces) > 1
    feat = pieces[0].shape[1]
    tokens = sum(piece.shape[0] for piece in pieces)
    group = tokens // peers
    if split_out:
        out_shape = [jax.ShapeDtypeStruct((group, INNER), BF16)] * peers
    else:
        out_shape = [jax.ShapeDtypeStruct((tokens, INNER), BF16)]
    return pl.pallas_call(
        functools.partial(temporal_kernel, peers, group, split_in, split_out),
        out_shape=out_shape,
        scratch_shapes=[
            pltpu.VMEM((tokens, feat), BF16),
            pltpu.VMEM((tokens, WIDE), BF16),
            pltpu.VMEM((tokens, WIDE), BF16),
            pltpu.VMEM((PAIRS * PAIR_ROWS, tokens), BF16),
            pltpu.VMEM((group // PACK * PAIRS, peers * PACK, 2 * peers * PACK), BF16),
            pltpu.VMEM((INNER, tokens), F32),
        ],
        compiler_params=params(),
        cost_estimate=cost(4 * 10**9, 6 * 2**20),
        name="temporal",
    )(*pieces, w)


def final_kernel(peers, group, xor, split, columns, *refs):
    count = peers if split else 1
    in_refs = refs[:count]
    mixed_ref, w_ref = refs[count : count + 2]
    out_ref, heads_ref = refs[-2:]
    step = pl.program_id(0)
    slab = mixed_ref.shape[0]

    if split:

        @pl.when(step == 0)
        def _():
            me = lax.axis_index("frame")
            for j in range(peers):
                peer = me ^ j if xor else lax.rem(me + j, peers)
                heads_ref[pl.ds(pl.multiple_of(peer * group, PACK), group), :] = in_refs[j][...]

        heads = heads_ref[pl.ds(pl.multiple_of(step * slab, slab), slab), :]
    else:
        heads = in_refs[0][pl.ds(pl.multiple_of(step * slab, slab), slab), :]
    result = mixed_ref[...].astype(F32) + nn_dot(heads, w_ref[...])
    for to, at in tile_order(slab, columns):
        out_ref[pl.ds(at, TW), :] = result[to : to + TW].astype(BF16)


def final(edges, pieces, mixed, w, slab, columns, pixels, peers, xor, base):
    split = len(pieces) > 1
    group = mixed.shape[0] // peers
    feat = mixed.shape[1]
    steps = mixed.shape[0] // slab
    tile_rows = pixels // slab
    at = (lambda i: i * (tile_rows - 1)) if edges else (lambda i: i + 1)
    whole = lambda *shape: pl.BlockSpec(shape, lambda i: (0, 0))
    in_specs = [whole(*piece.shape) for piece in pieces] + [
        pl.BlockSpec((slab, feat), lambda i: (i, 0)),
        whole(*w.shape),
    ]
    args = list(pieces) + [mixed, w]
    aliases = {}
    if base is not None:
        in_specs.append(pl.BlockSpec(memory_space=pl.ANY))
        aliases = {len(args): 0}
        args.append(base)
    return pl.pallas_call(
        functools.partial(final_kernel, peers, group, xor, split, columns),
        grid=(steps,),
        in_specs=in_specs,
        out_specs=pl.BlockSpec((slab, feat), lambda i: (at(i), 0)),
        out_shape=jax.ShapeDtypeStruct((pixels, feat), BF16),
        scratch_shapes=[pltpu.VMEM((peers * group, INNER), BF16)],
        input_output_aliases=aliases,
        compiler_params=params(),
        cost_estimate=cost(10**9, 4 * 2**20),
        name="final",
    )(*args)


def neighbours(top, bot):
    size = lax.axis_size("row")
    up = [(i, i + 1) for i in range(size - 1)]
    down = [(j, i) for i, j in up]
    return lax.ppermute(bot, "row", up), lax.ppermute(top, "row", down)


def exchange(pieces, xor, back):
    size = lax.axis_size("frame")
    if len(pieces) == 1:
        whole = pieces[0].reshape(size, -1, pieces[0].shape[-1])
        got = lax.all_to_all(whole, "frame", split_axis=0, concat_axis=0)
        return [got.reshape(pieces[0].shape)]
    result = [pieces[0]]
    for j in range(1, size):
        if xor:
            pairs = [(i, i ^ j) for i in range(size)]
        else:
            pairs = [(i, (i - j if back else i + j) % size) for i in range(size)]
        result.append(lax.ppermute(pieces[j], "frame", pairs))
    return result


def body(frames_in, spatial_qkv, spatial_out, temporal_qkv, temporal_out, key_tiles, tile_counts):
    _, rows_dev, columns, feat = frames_in.shape
    slab = TH * columns
    pixels = rows_dev * columns
    peers = lax.axis_size("frame")
    xor = peers & (peers - 1) == 0
    x = frames_in.reshape(pixels, feat)
    q, k, v, top, bot = project(x, spatial_qkv.T, slab, columns)
    halos = neighbours(top, bot)
    tiles = (spatial_out, key_tiles, tile_counts, slab, columns, peers, xor)
    mixed_a, send_a = spatial(False, SPLIT[0], x, q, k, v, None, *tiles)
    got_a = exchange(send_a, xor, False)
    mixed_b, send_b = spatial(True, SPLIT[1], x, q, k, v, halos, *tiles)
    got_b = exchange(send_b, xor, False)
    ret_a = exchange(temporal(got_a, temporal_qkv.T, peers, SPLIT[2]), xor, True)
    ret_b = exchange(temporal(got_b, temporal_qkv.T, peers, SPLIT[3]), xor, True)
    sizes = (temporal_out, slab, columns, pixels, peers, xor)
    out = final(False, ret_a, mixed_a, *sizes, None)
    out = final(True, ret_b, mixed_b, *sizes, out)
    return out.reshape(frames_in.shape)


def solution(mesh):
    in_specs = (
        P("frame", "row", None, None),
        P(),
        P(),
        P(),
        P(),
        P("frame", "row", None),
        P("frame", "row"),
    )
    out_specs = P("frame", "row", None, None)
    return jax.shard_map(body, mesh=mesh, in_specs=in_specs, out_specs=out_specs, check_vma=False)
```

```python
import functools

import jax
import jax.numpy as jnp
from jax import lax
from jax.experimental import pallas as pl
from jax.experimental.pallas import tpu as pltpu
from jax.sharding import PartitionSpec as P

HEADS = 8
HD = 72
TH = 4
TW = 16
LANES = 128
PACK = 16
NORM_EPS = 1e-06
NEG = -1e30
LOG2E = 1.4426950408889634
F32 = jnp.float32
BF16 = jnp.bfloat16
INNER = HEADS * HD
WIDE = -(-INNER // LANES) * LANES
PAIR = 2 * HD
PAIRS = HEADS // 2
PAIR_ROWS = PAIR + PACK
TILE = TH * TW
VMEM_LIMIT = 28 * 1024 * 1024
VMEM_WHOLE = 57 * 1024 * 1024


def params(limit=VMEM_LIMIT):
    return pltpu.CompilerParams(vmem_limit_bytes=limit)


def cost(flops, bytes_accessed):
    return pl.CostEstimate(flops=flops, bytes_accessed=bytes_accessed, transcendentals=0)


def nt_dot(a, b):
    return lax.dot_general(a, b, (((1,), (1,)), ((), ())), preferred_element_type=F32)


def nn_dot(a, b):
    return jnp.dot(a, b, preferred_element_type=F32)


def moments(x):
    x = x.astype(F32)
    mean = jnp.mean(x, axis=-1, keepdims=True)
    centred = x - mean
    spread = jnp.mean(centred * centred, axis=-1, keepdims=True)
    return mean, lax.rsqrt(spread + NORM_EPS)


def as_rows(column):
    return jnp.broadcast_to(column, (column.shape[0], LANES)).T[:1]


def tile_order(rows, columns):
    for col in range(columns // TW):
        for row in range(TH):
            yield (col * TH + row) * TW, row * columns + col * TW


def pair_window(pair):
    return pair * PAIR // LANES * LANES, -(-(pair + 1) * PAIR // LANES) * LANES


def two_heads(queries, pair):
    lo, hi = pair_window(pair)
    lane = lax.broadcasted_iota(jnp.int32, queries.shape, 1) + lo
    start = pair * PAIR
    first = jnp.where((lane >= start) & (lane < start + HD), queries, 0)
    second = jnp.where((lane >= start + HD) & (lane < start + PAIR), queries, 0)
    return jnp.concatenate([first, second], axis=0)


def split_queries_keys(prod):
    keys = prod[:, INNER // LANES * LANES :]
    shift = INNER % LANES
    if shift:
        keys = pltpu.roll(keys, keys.shape[1] - shift, 1)
    return prod[:, :WIDE], keys


def column_sums(w):
    return nt_dot(jnp.ones((PACK, w.shape[1]), BF16), w)[:1]


def store_values(v_ref, values, lanes):
    for pair in range(PAIRS):
        at = pair * PAIR_ROWS
        v_ref[at : at + PAIR, lanes] = values[pair * PAIR : (pair + 1) * PAIR]
        v_ref[at + PAIR : at + PAIR_ROWS, lanes] = jnp.ones((PACK, values.shape[1]), BF16)


def keys_values(x, mean, rstd, w_keys, w_values, k_ref, v_ref):
    k = (nt_dot(x, w_keys) - mean * column_sums(w_keys)) * rstd
    k_ref[:, :INNER] = k.astype(BF16)
    if WIDE > INNER:
        k_ref[:, INNER:] = jnp.zeros((x.shape[0], WIDE - INNER), BF16)
    col = nt_dot(w_values, jnp.ones((LANES, x.shape[1]), BF16))[:, :1]
    values = (nt_dot(w_values, x) - col * as_rows(mean)) * as_rows(rstd)
    store_values(v_ref, values.astype(BF16), slice(None))


def halo_kernel(columns, top_ref, bot_ref, wk_ref, wv_ref, k_ref, v_ref, x_ref):
    slab = top_ref.shape[0]
    v_rows = v_ref.shape[0] // 2
    for part, ref in enumerate((top_ref, bot_ref)):
        for to, at in tile_order(slab, columns):
            x_ref[pl.ds(to, TW), :] = ref[pl.ds(at, TW), :]
        x = x_ref[...]
        mean, rstd = moments(x)
        keys_values(
            x, mean, rstd, wk_ref[...], wv_ref[...],
            k_ref.at[pl.ds(part * slab, slab)], v_ref.at[pl.ds(part * v_rows, v_rows)],
        )


def project_halos(top, bot, w, columns):
    slab, feat = top.shape
    v_rows = PAIRS * PAIR_ROWS
    whole = lambda *shape: pl.BlockSpec(shape, lambda i: (0, 0))
    return pl.pallas_call(
        functools.partial(halo_kernel, columns),
        grid=(1,),
        in_specs=[
            whole(slab, feat),
            whole(slab, feat),
            pl.BlockSpec((INNER, feat), lambda i: (1, 0)),
            pl.BlockSpec((INNER, feat), lambda i: (2, 0)),
        ],
        out_specs=[whole(2 * slab, WIDE), whole(2 * v_rows, slab)],
        out_shape=[
            jax.ShapeDtypeStruct((2 * slab, WIDE), BF16),
            jax.ShapeDtypeStruct((2 * v_rows, slab), BF16),
        ],
        scratch_shapes=[pltpu.VMEM((slab, feat), BF16)],
        compiler_params=params(),
        cost_estimate=cost(2 * 10**9, 4 * 2**20),
        name="project_halos",
    )(top, bot, w, w)


def visible_bits(tile, count, global_row, tile_cols, slot_num, targets_ref):
    bits = jnp.int32(0)
    for slot in range(slot_num):
        target = targets_ref[0, tile, slot]
        cand = (lax.div(target, tile_cols) - global_row + 1) * tile_cols + lax.rem(target, tile_cols)
        bits = bits | jnp.where(slot < count, jnp.left_shift(1, cand), 0)
    return bits


def hidden(bits, index):
    return (1 - (jnp.right_shift(bits, index) & 1)).astype(F32) * NEG


def attend_tile_row(
    tile_row, tile_rows, columns, targets_ref, counts_ref, q_ref, k_refs, v_refs, p_ref, acc_ref
):
    slab = q_ref.shape[0]
    tile_cols = columns // TW
    slot_num = targets_ref.shape[2]
    global_row = lax.axis_index("row") * tile_rows + tile_row
    left = lax.broadcasted_iota(jnp.int32, (1, 4 * TILE), 1) % (2 * TILE) < TILE
    for duo in range(tile_cols // 2):
        bits = []
        for tile in (2 * duo, 2 * duo + 1):
            tile = tile_row * tile_cols + tile
            bits.append(
                visible_bits(tile, counts_ref[0, tile], global_row, tile_cols, slot_num, targets_ref)
            )
        lowest, highest = max(2 * duo - 1, 0), min(2 * duo + 2, tile_cols - 1)
        span = range(lowest, highest + 1)
        bias = {}
        for j in range(3):
            for col in span:
                at = j * tile_cols + col
                bias[j, col] = jnp.where(left, hidden(bits[0], at), hidden(bits[1], at))
        for pair in range(PAIRS):
            lo, hi = pair_window(pair)
            queries = two_heads(q_ref[2 * duo * TILE : (2 * duo + 2) * TILE, lo:hi], pair)
            scores = {}
            for j, ref in enumerate(k_refs):
                part = nt_dot(ref[lowest * TILE : (highest + 1) * TILE, lo:hi], queries)
                for col in span:
                    at = (col - lowest) * TILE
                    scores[j, col] = part[at : at + TILE] + bias[j, col]
            top = functools.reduce(jnp.maximum, scores.values())
            top = jnp.max(top, axis=0, keepdims=True)
            for (j, col), score in scores.items():
                at = j * slab + col * TILE
                p_ref[duo * PAIRS + pair, at : at + TILE, :] = jnp.exp2(score - top).astype(BF16)

    for duo in range(tile_cols // 2):
        for pair in range(PAIRS):
            out = sum(
                nn_dot(
                    ref[pair * PAIR_ROWS : (pair + 1) * PAIR_ROWS, :],
                    p_ref[duo * PAIRS + pair, j * slab : (j + 1) * slab, :],
                )
                for j, ref in enumerate(v_refs)
            )
            out = out[:PAIR] * (1.0 / out[PAIR : PAIR + 1])
            lanes = slice(2 * duo * TILE, (2 * duo + 2) * TILE)
            acc_ref[pair * PAIR : pair * PAIR + HD, lanes] = out[:HD, : 2 * TILE]
            acc_ref[pair * PAIR + HD : (pair + 1) * PAIR, lanes] = out[HD:, 2 * TILE :]


def peer_of(slot, peers, xor):
    me, j = lax.axis_index("frame"), (peers - slot) % peers
    return me ^ j if xor else lax.rem(me + j, peers)


def hand_out(send_refs, out_ref, group, xor):
    for slot, ref in enumerate(send_refs):
        peer = peer_of(slot, len(send_refs), xor)
        ref[...] = out_ref[pl.ds(pl.multiple_of(peer * group, PACK), group), :]


def inner_kernel(
    group, peers, xor,
    targets_ref, counts_ref, x_hbm, w_hbm, wo_hbm, q_hbm, k_hbm, v_hbm, mixed_ref, *rest,
):
    send_refs, rest = rest[:peers], rest[peers:]
    (w_ref, wo_ref, x_ref, q_ref, k_ref, v_ref, sum_ref, col_ref, p_ref, acc_ref, out_ref) = rest[:11]
    x_sem, w_sem, out_sem = rest[11:]
    step = pl.program_id(0)
    tile_rows, tile_cols = x_ref.shape[:2]
    columns = tile_cols * TW
    feat = x_ref.shape[-1]
    slab = tile_cols * TILE
    v_rows = PAIRS * PAIR_ROWS
    low = INNER // LANES * LANES
    bounds = (0, low, 2 * INNER, 3 * INNER)

    def x_copy(at, col):
        return pltpu.make_async_copy(
            x_hbm.at[pl.ds(at * TH, TH), pl.ds(col * TW, TW), :], x_ref.at[at, col], x_sem.at[at, col]
        )

    def w_copy(part):
        if part == 3:
            return pltpu.make_async_copy(wo_hbm, wo_ref, w_sem.at[3])
        rows = pl.ds(bounds[part], bounds[part + 1] - bounds[part])
        return pltpu.make_async_copy(w_hbm.at[rows], w_ref.at[rows], w_sem.at[part])

    def out_copies(at):
        rows, wide = pl.ds(at * slab, slab), pl.ds(at * v_rows, v_rows)
        return (
            pltpu.make_async_copy(q_ref.at[at], q_hbm.at[rows], out_sem.at[0, at]),
            pltpu.make_async_copy(k_ref.at[at], k_hbm.at[rows], out_sem.at[1, at]),
            pltpu.make_async_copy(v_ref.at[at], v_hbm.at[wide], out_sem.at[2, at]),
        )

    def work(first):
        for col in range(tile_cols):
            x_copy(step, col).wait()
        x = x_ref[step].reshape(slab, feat)
        mean, rstd = moments(x)
        if first:
            w_copy(0).wait()
            sum_ref[:, :low] = column_sums(w_ref[:low, :])
        scale = rstd * (LOG2E * HD**-0.5)
        q = (nt_dot(x, w_ref[:low, :]) - mean * sum_ref[:, :low]) * scale
        q_ref[step, :, :low] = q.astype(BF16)
        if first:
            w_copy(1).wait()
            sum_ref[:, low:] = column_sums(w_ref[low : 2 * INNER, :])
        k = (nt_dot(x, w_ref[low : 2 * INNER, :]) - mean * sum_ref[:, low:]) * rstd
        if INNER > low:
            q_ref[step, :, low:] = (k[:, : WIDE - low] * (LOG2E * HD**-0.5)).astype(BF16)
            k = pltpu.roll(k, k.shape[1] - (INNER - low), 1)
        k_ref[step] = k.astype(BF16)
        if first:
            w_copy(2).wait()
            ones = jnp.ones((LANES, feat), BF16)
            col_ref[...] = nt_dot(w_ref[2 * INNER :, :], ones)[:, :1]
        values = nt_dot(w_ref[2 * INNER :, :], x) - col_ref[...] * as_rows(mean)
        store_values(v_ref.at[step], (values * as_rows(rstd)).astype(BF16), slice(None))
        for copy in out_copies(step):
            copy.start()

    @pl.when(step == 0)
    def _():
        for col in range(tile_cols):
            x_copy(0, col).start()
        for part in range(3):
            w_copy(part).start()
        for at in range(1, tile_rows):
            for col in range(tile_cols):
                x_copy(at, col).start()
        w_copy(3).start()
        work(True)

    @pl.when((step > 0) & (step < tile_rows))
    def _():
        work(False)

    @pl.when(step == tile_rows)
    def _():
        w_copy(3).wait()
        p_ref[...] = jnp.zeros(p_ref.shape, BF16)

    @pl.when(step >= tile_rows)
    def _():
        tile_row = step - tile_rows + 1
        k_refs = [k_ref.at[tile_row + j] for j in (-1, 0, 1)]
        v_refs = [v_ref.at[tile_row + j] for j in (-1, 0, 1)]
        attend_tile_row(
            tile_row, tile_rows, columns, targets_ref, counts_ref, q_ref.at[tile_row],
            k_refs, v_refs, p_ref, acc_ref,
        )
        branch = nn_dot(acc_ref[...].T.astype(BF16), wo_ref[...])
        mixed = (x_ref[tile_row].reshape(slab, feat).astype(F32) + branch).astype(BF16)
        mixed_ref[...] = mixed
        out_ref[pl.ds(pl.multiple_of((tile_row - 1) * slab, slab), slab), :] = mixed

    @pl.when(step == 2 * tile_rows - 3)
    def _():
        hand_out(send_refs, out_ref, group, xor)
        for at in range(tile_rows):
            for copy in out_copies(at):
                copy.wait()


def spatial_inner(x, w, wo, targets, counts, peers, xor):
    rows, columns, feat = x.shape
    tile_rows = rows // TH
    slab = TH * columns
    v_rows = PAIRS * PAIR_ROWS
    group = (tile_rows - 2) * slab // peers
    smem = pl.BlockSpec(memory_space=pltpu.SMEM)
    hbm = pl.BlockSpec(memory_space=pltpu.HBM)
    outs = pl.pallas_call(
        functools.partial(inner_kernel, group, peers, xor),
        grid=(2 * tile_rows - 2,),
        in_specs=[smem, smem, hbm, hbm, hbm],
        out_specs=[hbm, hbm, hbm, pl.BlockSpec((slab, feat), lambda i: (jnp.maximum(i - tile_rows, 0), 0))]
        + [pl.BlockSpec((group, feat), lambda i: (0, 0))] * peers,
        out_shape=[
            jax.ShapeDtypeStruct((tile_rows * slab, WIDE), BF16),
            jax.ShapeDtypeStruct((tile_rows * slab, WIDE), BF16),
            jax.ShapeDtypeStruct((tile_rows * v_rows, slab), BF16),
            jax.ShapeDtypeStruct((tile_rows * slab, feat), BF16),
        ]
        + [jax.ShapeDtypeStruct((group, feat), BF16)] * peers,
        scratch_shapes=[
            pltpu.VMEM(w.shape, BF16),
            pltpu.VMEM(wo.shape, BF16),
            pltpu.VMEM((tile_rows, columns // TW, TH, TW, feat), BF16),
            pltpu.VMEM((tile_rows, slab, WIDE), BF16),
            pltpu.VMEM((tile_rows, slab, WIDE), BF16),
            pltpu.VMEM((tile_rows, v_rows, slab), BF16),
            pltpu.VMEM((1, 2 * INNER), F32),
            pltpu.VMEM((INNER, 1), F32),
            pltpu.VMEM((columns // TW // 2 * PAIRS, 3 * slab, 4 * TILE), BF16),
            pltpu.VMEM((INNER, slab), F32),
            pltpu.VMEM(((tile_rows - 2) * slab, feat), BF16),
            pltpu.SemaphoreType.DMA((tile_rows, columns // TW)),
            pltpu.SemaphoreType.DMA((4,)),
            pltpu.SemaphoreType.DMA((3, tile_rows)),
        ],
        compiler_params=params(VMEM_WHOLE),
        cost_estimate=cost(12 * 10**9, 16 * 2**20),
        name="spatial_inner",
    )(targets, counts, x, w, wo)
    return outs[:3], outs[3], outs[4:]


def edges_kernel(
    group, peers, xor, tile_rows, columns,
    targets_ref, counts_ref, x_ref, q_ref, k0, k1, k2, v0, v1, v2, k_halo, v_halo, _, w_ref, mixed_ref, *rest,
):
    send_refs, rest = rest[:peers], rest[peers:]
    p_ref, acc_ref, out_ref, k_prev, k_next, v_prev, v_next = rest
    step = pl.program_id(0)
    slab = x_ref.shape[0]
    v_rows = v_prev.shape[0]

    @pl.when(step == 0)
    def _():
        p_ref[...] = jnp.zeros(p_ref.shape, BF16)
        k_prev[...] = k_halo[:slab, :]
        v_prev[...] = v_halo[:v_rows, :]
        k_next[...] = k2[...]
        v_next[...] = v2[...]

    @pl.when(step != 0)
    def _():
        k_prev[...] = k0[...]
        v_prev[...] = v0[...]
        k_next[...] = k_halo[slab:, :]
        v_next[...] = v_halo[v_rows:, :]

    attend_tile_row(
        step * (tile_rows - 1), tile_rows, columns, targets_ref, counts_ref, q_ref,
        (k_prev, k1, k_next), (v_prev, v1, v_next), p_ref, acc_ref,
    )
    branch = nn_dot(acc_ref[...].T.astype(BF16), w_ref[...])
    base = step * slab
    for to, at in tile_order(slab, columns):
        mixed = (x_ref[pl.ds(at, TW), :].astype(F32) + branch[to : to + TW]).astype(BF16)
        mixed_ref[pl.ds(to, TW), :] = mixed
        out_ref[pl.ds(pl.multiple_of(base + to, TW), TW), :] = mixed

    @pl.when(step == 1)
    def _():
        hand_out(send_refs, out_ref, group, xor)


def spatial_edges(x, q, k, v, halos, base, w, targets, counts, slab, columns, peers, xor):
    pixels, feat = x.shape
    tile_rows = pixels // slab
    group = 2 * slab // peers
    v_rows = PAIRS * PAIR_ROWS
    at = lambda i: i * (tile_rows - 1)
    smem = pl.BlockSpec(memory_space=pltpu.SMEM)
    whole = lambda *shape: pl.BlockSpec(shape, lambda i: (0, 0))
    in_specs = [
        smem,
        smem,
        pl.BlockSpec((slab, feat), lambda i: (at(i), 0)),
        pl.BlockSpec((slab, WIDE), lambda i: (at(i), 0)),
    ]
    for block in ((slab, WIDE), (v_rows, slab)):
        in_specs += [
            pl.BlockSpec(block, lambda i: (tile_rows - 2, 0)),
            pl.BlockSpec(block, lambda i: (at(i), 0)),
            pl.BlockSpec(block, lambda i: (1, 0)),
        ]
    in_specs += [whole(*halo.shape) for halo in halos]
    in_specs += [pl.BlockSpec(memory_space=pl.ANY), whole(*w.shape)]
    outs = pl.pallas_call(
        functools.partial(edges_kernel, group, peers, xor, tile_rows, columns),
        grid=(2,),
        in_specs=in_specs,
        out_specs=[pl.BlockSpec((slab, feat), lambda i: (tile_rows - 2 + i, 0))]
        + [whole(group, feat)] * peers,
        out_shape=[jax.ShapeDtypeStruct((pixels, feat), BF16)]
        + [jax.ShapeDtypeStruct((group, feat), BF16)] * peers,
        scratch_shapes=[
            pltpu.VMEM((columns // TW // 2 * PAIRS, 3 * slab, 4 * TILE), BF16),
            pltpu.VMEM((INNER, slab), F32),
            pltpu.VMEM((2 * slab, feat), BF16),
            pltpu.VMEM((slab, WIDE), BF16),
            pltpu.VMEM((slab, WIDE), BF16),
            pltpu.VMEM((v_rows, slab), BF16),
            pltpu.VMEM((v_rows, slab), BF16),
        ],
        input_output_aliases={12: 0},
        compiler_params=params(),
        cost_estimate=cost(6 * 10**9, 8 * 2**20),
        name="spatial_edges",
    )(targets, counts, x, q, k, k, k, v, v, v, *halos, base, w)
    return outs[0], outs[1:]


def temporal_kernel(peers, group, earlier, *refs):
    in_refs, w_ref, refs = refs[:peers], refs[peers], refs[peers + 1 :]
    if earlier:
        early_refs, refs = refs[:peers], refs[peers:]
    out_refs = refs[:peers]
    x_ref, q_ref, k_ref, v_ref, p_ref, acc_ref = refs[peers:]
    if earlier:
        for j in range(peers):
            out_refs[j][:earlier, :] = early_refs[j][...]
    block = peers * PACK
    parts = group // PACK
    tokens = peers * group
    for part in range(parts):
        for j in range(peers):
            to = pl.ds(part * block + j * PACK, PACK)
            x_ref[to, :] = in_refs[j][pl.ds(part * PACK, PACK), :]
    x = x_ref[...]
    mean, rstd = moments(x)
    prod = (nt_dot(x, w_ref[: 2 * INNER, :]) - mean * column_sums(w_ref[: 2 * INNER, :])) * rstd
    q, k = split_queries_keys(prod)
    q_ref[...] = (q * (LOG2E * HD**-0.5)).astype(BF16)
    k_ref[...] = k.astype(BF16)
    w_values = w_ref[2 * INNER :, :]
    col = nt_dot(w_values, jnp.ones((LANES, w_values.shape[1]), BF16))[:, :1]
    values = (nt_dot(w_values, x) - col * as_rows(mean)) * as_rows(rstd)
    store_values(v_ref, values.astype(BF16), slice(None))
    row = lax.broadcasted_iota(jnp.int32, (block, 2 * block), 0)
    col = lax.broadcasted_iota(jnp.int32, (block, 2 * block), 1)
    bias = jnp.where(row % PACK == col % PACK, 0.0, NEG).astype(F32)
    for part in range(parts):
        at = part * block
        for pair in range(PAIRS):
            lo, hi = pair_window(pair)
            queries = two_heads(q_ref[at : at + block, lo:hi], pair)
            scores = nt_dot(k_ref[at : at + block, lo:hi], queries) + bias
            expo = jnp.exp2(scores - jnp.max(scores, axis=0, keepdims=True))
            p_ref[part * PAIRS + pair] = expo.astype(BF16)
    for part in range(parts):
        at = part * block
        for pair in range(PAIRS):
            weights = v_ref[pair * PAIR_ROWS : (pair + 1) * PAIR_ROWS, at : at + block]
            out = nn_dot(weights, p_ref[part * PAIRS + pair])
            out = out[:PAIR] * (1.0 / out[PAIR : PAIR + 1])
            acc_ref[pair * PAIR : pair * PAIR + HD, at : at + block] = out[:HD, :block]
            acc_ref[pair * PAIR + HD : (pair + 1) * PAIR, at : at + block] = out[HD:, block:]
    for part in range(parts):
        at = part * block
        heads = acc_ref[:, at : at + block].T.astype(BF16)
        for j in range(peers):
            rows = heads[j * PACK : (j + 1) * PACK]
            out_refs[j][pl.ds(earlier + part * PACK, PACK), :] = rows


def temporal(pieces, w, early):
    peers = len(pieces)
    group, feat = pieces[0].shape
    tokens = peers * group
    earlier = early[0].shape[0] if early else 0
    return pl.pallas_call(
        functools.partial(temporal_kernel, peers, group, earlier),
        out_shape=[jax.ShapeDtypeStruct((earlier + group, INNER), BF16)] * peers,
        scratch_shapes=[
            pltpu.VMEM((tokens, feat), BF16),
            pltpu.VMEM((tokens, WIDE), BF16),
            pltpu.VMEM((tokens, WIDE), BF16),
            pltpu.VMEM((PAIRS * PAIR_ROWS, tokens), BF16),
            pltpu.VMEM((group // PACK * PAIRS, peers * PACK, 2 * peers * PACK), BF16),
            pltpu.VMEM((INNER, tokens), F32),
        ],
        compiler_params=params(),
        cost_estimate=cost(4 * 10**9, 6 * 2**20),
        name="temporal",
    )(*pieces, w, *early)


def final_kernel(groups, xor, columns, *refs):
    in_refs, (mixed_ref, w_ref, out_ref, heads_ref) = refs[:-4], refs[-4:]
    step = pl.program_id(0)
    slab = mixed_ref.shape[0]
    peers = len(in_refs)

    @pl.when(step == 0)
    def _():
        for j in range(peers):
            peer = peer_of(j, peers, xor)
            base = start = 0
            for group in groups:
                to = pl.multiple_of(base + peer * group, PACK)
                heads_ref[pl.ds(to, group), :] = in_refs[j][start : start + group, :]
                base += peers * group
                start += group

    heads = heads_ref[pl.ds(pl.multiple_of(step * slab, slab), slab), :]
    result = mixed_ref[...].astype(F32) + nn_dot(heads, w_ref[...])
    for to, at in tile_order(slab, columns):
        out_ref[pl.ds(at, TW), :] = result[to : to + TW].astype(BF16)


def final(pieces, groups, mixed, w, slab, columns, xor):
    pixels, feat = mixed.shape
    tile_rows = pixels // slab
    inner = tile_rows - 2
    at = lambda i: jnp.where(i < inner, i + 1, (i - inner) * (tile_rows - 1))
    whole = lambda *shape: pl.BlockSpec(shape, lambda i: (0, 0))
    return pl.pallas_call(
        functools.partial(final_kernel, groups, xor, columns),
        grid=(tile_rows,),
        in_specs=[whole(*piece.shape) for piece in pieces]
        + [pl.BlockSpec((slab, feat), lambda i: (i, 0)), whole(*w.shape)],
        out_specs=pl.BlockSpec((slab, feat), lambda i: (at(i), 0)),
        out_shape=jax.ShapeDtypeStruct((pixels, feat), BF16),
        scratch_shapes=[pltpu.VMEM((pixels, INNER), BF16)],
        compiler_params=params(),
        cost_estimate=cost(2 * 10**9, 6 * 2**20),
        name="final",
    )(*pieces, mixed, w)


def neighbours(x, slab):
    size = lax.axis_size("row")
    up = [(i, i + 1) for i in range(size - 1)]
    down = [(j, i) for i, j in up]
    return lax.ppermute(x[-slab:], "row", up), lax.ppermute(x[:slab], "row", down)


def exchange(pieces, xor, back):
    size = lax.axis_size("frame")
    result = [pieces[0]]
    for slot in range(1, size):
        j = size - slot
        if xor:
            pairs = [(i, i ^ j) for i in range(size)]
        else:
            pairs = [(i, (i - j if back else i + j) % size) for i in range(size)]
        result.append(lax.ppermute(pieces[slot], "frame", pairs))
    return result


def body(frames_in, spatial_qkv, spatial_out, temporal_qkv, temporal_out, key_tiles, tile_counts):
    _, rows_dev, columns, feat = frames_in.shape
    slab = TH * columns
    pixels = rows_dev * columns
    peers = lax.axis_size("frame")
    xor = peers & (peers - 1) == 0
    x = frames_in.reshape(pixels, feat)
    top, bot = neighbours(x, slab)
    qkv, mixed, send_a = spatial_inner(
        frames_in[0], spatial_qkv.T, spatial_out, key_tiles, tile_counts, peers, xor
    )
    got_a = exchange(send_a, xor, False)
    top, bot, mixed = lax.optimization_barrier((top, bot, mixed))
    halos = project_halos(top, bot, spatial_qkv.T, columns)
    mixed, send_b = spatial_edges(
        x, *qkv, halos, mixed, spatial_out, key_tiles, tile_counts, slab, columns, peers, xor
    )
    got_b = exchange(send_b, xor, False)
    heads_a = temporal(got_a, temporal_qkv.T, ())
    heads = temporal(got_b, temporal_qkv.T, heads_a)
    groups = (got_a[0].shape[0], got_b[0].shape[0])
    out = final(exchange(heads, xor, True), groups, mixed, temporal_out, slab, columns, xor)
    return out.reshape(frames_in.shape)


def solution(mesh):
    in_specs = (
        P("frame", "row", None, None),
        P(),
        P(),
        P(),
        P(),
        P("frame", "row", None),
        P("frame", "row"),
    )
    out_specs = P("frame", "row", None, None)
    return jax.shard_map(body, mesh=mesh, in_specs=in_specs, out_specs=out_specs, check_vma=False)
```

```python
import functools

import jax
import jax.numpy as jnp
from jax import lax
from jax.experimental import pallas as pl
from jax.experimental.pallas import tpu as pltpu
from jax.sharding import PartitionSpec as P

HEADS = 8
HD = 72
TH = 4
TW = 16
LANES = 128
PACK = 16
NORM_EPS = 1e-06
NEG = -1e30
LOG2E = 1.4426950408889634
F32 = jnp.float32
BF16 = jnp.bfloat16
INNER = HEADS * HD
WIDE = -(-INNER // LANES) * LANES
PAIR = 2 * HD
PAIRS = HEADS // 2
PAIR_ROWS = PAIR + PACK
TILE = TH * TW
VMEM_LIMIT = 28 * 1024 * 1024
VMEM_WHOLE = 58 * 1024 * 1024


def params(limit=VMEM_LIMIT):
    return pltpu.CompilerParams(vmem_limit_bytes=limit)


def cost(flops, bytes_accessed):
    return pl.CostEstimate(flops=flops, bytes_accessed=bytes_accessed, transcendentals=0)


def nt_dot(a, b):
    return lax.dot_general(a, b, (((1,), (1,)), ((), ())), preferred_element_type=F32)


def nn_dot(a, b):
    return jnp.dot(a, b, preferred_element_type=F32)


def moments(x):
    x = x.astype(F32)
    mean = jnp.mean(x, axis=-1, keepdims=True)
    centred = x - mean
    spread = jnp.mean(centred * centred, axis=-1, keepdims=True)
    return mean, lax.rsqrt(spread + NORM_EPS)


def as_rows(column):
    return jnp.broadcast_to(column, (column.shape[0], LANES)).T[:1]


def tile_order(rows, columns):
    for col in range(columns // TW):
        for row in range(TH):
            yield (col * TH + row) * TW, row * columns + col * TW


def pair_window(pair):
    return pair * PAIR // LANES * LANES, -(-(pair + 1) * PAIR // LANES) * LANES


def two_heads(queries, pair):
    lo, hi = pair_window(pair)
    lane = lax.broadcasted_iota(jnp.int32, queries.shape, 1) + lo
    start = pair * PAIR
    first = jnp.where((lane >= start) & (lane < start + HD), queries, 0)
    second = jnp.where((lane >= start + HD) & (lane < start + PAIR), queries, 0)
    return jnp.concatenate([first, second], axis=0)


def split_queries_keys(prod):
    keys = prod[:, INNER // LANES * LANES :]
    shift = INNER % LANES
    if shift:
        keys = pltpu.roll(keys, keys.shape[1] - shift, 1)
    return prod[:, :WIDE], keys


def row_sums(w):
    return jnp.sum(w.astype(F32), axis=-1, keepdims=True)


def store_values(v_ref, values, lanes):
    for pair in range(PAIRS):
        at = pair * PAIR_ROWS
        v_ref[at : at + PAIR, lanes] = values[pair * PAIR : (pair + 1) * PAIR]
        v_ref[at + PAIR : at + PAIR_ROWS, lanes] = jnp.ones((PACK, values.shape[1]), BF16)


def packed_keys(slab):
    per = slab // LANES
    full = WIDE // slab * per
    for piece in range(WIDE // LANES):
        lanes = pl.ds(piece * LANES, LANES)
        if piece < full:
            yield pl.ds(0, slab), lanes, pl.ds(piece // per * slab, slab), pl.ds(piece % per * LANES, LANES)
        else:
            rows = slab // per
            for part in range(per):
                to = pl.ds(full // per * slab, rows), pl.ds(part * LANES, LANES)
                yield pl.ds(part * rows, rows), lanes, *to


def unpack_halo(halo_ref, k_ref, v_ref):
    size = v_ref.shape[0]
    v_ref[...] = halo_ref[:size, :]
    for rows, lanes, at, to in packed_keys(k_ref.shape[0]):
        k_ref[rows, lanes] = halo_ref[pl.ds(size + at.start, at.size), to]


def visible_bits(tile, count, global_row, tile_cols, slot_num, targets_ref):
    bits = jnp.int32(0)
    for slot in range(slot_num):
        target = targets_ref[0, tile, slot]
        cand = (lax.div(target, tile_cols) - global_row + 1) * tile_cols + lax.rem(target, tile_cols)
        bits = bits | jnp.where(slot < count, jnp.left_shift(1, cand), 0)
    return bits


def hidden(bits, index):
    return (1 - (jnp.right_shift(bits, index) & 1)).astype(F32) * NEG


def attend_tile_row(
    tile_row, tile_rows, columns, targets_ref, counts_ref, q_ref, k_refs, v_refs, p_ref, acc_ref
):
    slab = q_ref.shape[0]
    tile_cols = columns // TW
    slot_num = targets_ref.shape[2]
    global_row = lax.axis_index("row") * tile_rows + tile_row
    left = lax.broadcasted_iota(jnp.int32, (1, 4 * TILE), 1) % (2 * TILE) < TILE
    for duo in range(tile_cols // 2):
        bits = []
        for tile in (2 * duo, 2 * duo + 1):
            tile = tile_row * tile_cols + tile
            bits.append(
                visible_bits(tile, counts_ref[0, tile], global_row, tile_cols, slot_num, targets_ref)
            )
        lowest, highest = max(2 * duo - 1, 0), min(2 * duo + 2, tile_cols - 1)
        span = range(lowest, highest + 1)
        bias = {}
        for j in range(3):
            for col in span:
                at = j * tile_cols + col
                bias[j, col] = jnp.where(left, hidden(bits[0], at), hidden(bits[1], at))
        for pair in range(PAIRS):
            lo, hi = pair_window(pair)
            queries = two_heads(q_ref[2 * duo * TILE : (2 * duo + 2) * TILE, lo:hi], pair)
            scores = {}
            for j, ref in enumerate(k_refs):
                part = nt_dot(ref[lowest * TILE : (highest + 1) * TILE, lo:hi], queries)
                for col in span:
                    at = (col - lowest) * TILE
                    scores[j, col] = part[at : at + TILE] + bias[j, col]
            top = functools.reduce(jnp.maximum, scores.values())
            top = jnp.max(top, axis=0, keepdims=True)
            for (j, col), score in scores.items():
                at = j * slab + col * TILE
                p_ref[duo * PAIRS + pair, at : at + TILE, :] = jnp.exp2(score - top).astype(BF16)

    for duo in range(tile_cols // 2):
        for pair in range(PAIRS):
            out = sum(
                nn_dot(
                    ref[pair * PAIR_ROWS : (pair + 1) * PAIR_ROWS, :],
                    p_ref[duo * PAIRS + pair, j * slab : (j + 1) * slab, :],
                )
                for j, ref in enumerate(v_refs)
            )
            out = out[:PAIR] * (1.0 / out[PAIR : PAIR + 1])
            lanes = slice(2 * duo * TILE, (2 * duo + 2) * TILE)
            acc_ref[pair * PAIR : pair * PAIR + HD, lanes] = out[:HD, : 2 * TILE]
            acc_ref[pair * PAIR + HD : (pair + 1) * PAIR, lanes] = out[HD:, 2 * TILE :]


def peer_of(slot, peers, xor):
    me, j = lax.axis_index("frame"), (peers - slot) % peers
    return me ^ j if xor else lax.rem(me + j, peers)


def hand_out(send_refs, out_ref, group, xor):
    for slot, ref in enumerate(send_refs):
        peer = peer_of(slot, len(send_refs), xor)
        ref[...] = out_ref[pl.ds(pl.multiple_of(peer * group, PACK), group), :]


def inner_kernel(
    group, peers, xor,
    targets_ref, counts_ref, x_hbm, w_ref, wo_ref, q_hbm, k_hbm, v_hbm, edge_hbm, top_hbm, bot_hbm, mixed_ref,
    *rest,
):
    send_refs, rest = rest[:peers], rest[peers:]
    x_ref, q_ref, k_ref, v_ref, sum_ref, col_ref, p_ref, acc_ref, out_ref, x_sem, out_sem, halo_sem = rest
    step = pl.program_id(0)
    tile_rows, tile_cols = x_ref.shape[:2]
    columns = tile_cols * TW
    feat = x_ref.shape[-1]
    slab = tile_cols * TILE
    v_rows = PAIRS * PAIR_ROWS
    low = INNER // LANES * LANES

    def x_copy(at, col):
        return pltpu.make_async_copy(
            x_hbm.at[pl.ds(at * TH, TH), pl.ds(col * TW, TW), :], x_ref.at[at, col], x_sem.at[at, col]
        )

    def out_copies(at):
        rows, wide = pl.ds(at * slab, slab), pl.ds(at * v_rows, v_rows)
        return (
            pltpu.make_async_copy(q_ref.at[at], q_hbm.at[rows], out_sem.at[0, at]),
            pltpu.make_async_copy(k_ref.at[at], k_hbm.at[rows], out_sem.at[1, at]),
            pltpu.make_async_copy(v_ref.at[at], v_hbm.at[wide], out_sem.at[2, at]),
        )

    def edge_copies():
        for part, at in enumerate((0, tile_rows - 1)):
            yield pltpu.make_async_copy(x_ref.at[at], edge_hbm.at[part], out_sem.at[3, part])

    def halo_copies():
        for part, (at, halo) in enumerate(((0, top_hbm), (tile_rows - 1, bot_hbm))):
            yield pltpu.make_async_copy(v_ref.at[at], halo.at[pl.ds(0, v_rows)], halo_sem.at[part, 0])
            for piece, (rows, lanes, to, lane) in enumerate(packed_keys(slab)):
                to = pl.ds(v_rows + to.start, to.size)
                yield pltpu.make_async_copy(
                    k_ref.at[at, rows, lanes], halo.at[to, lane], halo_sem.at[part, 1 + piece]
                )

    def work(first):
        for col in range(tile_cols):
            x_copy(step, col).wait()
        x = x_ref[step].reshape(slab, feat)
        mean, rstd = moments(x)
        if first:
            rows = jnp.concatenate([x, jnp.ones((PACK, feat), BF16)], axis=0)
            q, k = nt_dot(rows, w_ref[:low, :]), nt_dot(rows, w_ref[low : 2 * INNER, :])
            sum_ref[:, :low], sum_ref[:, low:] = q[slab : slab + 1], k[slab : slab + 1]
            q, k = q[:slab], k[:slab]
        else:
            q, k = nt_dot(x, w_ref[:low, :]), nt_dot(x, w_ref[low : 2 * INNER, :])
        q = (q - mean * sum_ref[:, :low]) * (rstd * (LOG2E * HD**-0.5))
        q_ref[step, :, :low] = q.astype(BF16)
        k = (k - mean * sum_ref[:, low:]) * rstd
        if INNER > low:
            q_ref[step, :, low:] = (k[:, : WIDE - low] * (LOG2E * HD**-0.5)).astype(BF16)
            k = pltpu.roll(k, k.shape[1] - (INNER - low), 1)
        k_ref[step] = k.astype(BF16)
        if first:
            col_ref[...] = row_sums(w_ref[2 * INNER :, :])
        values = nt_dot(w_ref[2 * INNER :, :], x) - col_ref[...] * as_rows(mean)
        store_values(v_ref.at[step], (values * as_rows(rstd)).astype(BF16), slice(None))
        for copy in out_copies(step):
            copy.start()

    @pl.when(step == 0)
    def _():
        for col in range(tile_cols):
            x_copy(0, col).start()
        for at in range(1, tile_rows):
            for col in range(tile_cols):
                x_copy(at, col).start()
        work(True)

    @pl.when((step > 0) & (step < tile_rows))
    def _():
        work(False)

    @pl.when(step == tile_rows)
    def _():
        for copy in (*edge_copies(), *halo_copies()):
            copy.start()
        p_ref[...] = jnp.zeros(p_ref.shape, BF16)

    @pl.when(step >= tile_rows)
    def _():
        tile_row = step - tile_rows + 1
        k_refs = [k_ref.at[tile_row + j] for j in (-1, 0, 1)]
        v_refs = [v_ref.at[tile_row + j] for j in (-1, 0, 1)]
        attend_tile_row(
            tile_row, tile_rows, columns, targets_ref, counts_ref, q_ref.at[tile_row],
            k_refs, v_refs, p_ref, acc_ref,
        )
        branch = nn_dot(acc_ref[...].T.astype(BF16), wo_ref[...])
        mixed = (x_ref[tile_row].reshape(slab, feat).astype(F32) + branch).astype(BF16)
        mixed_ref[...] = mixed
        out_ref[pl.ds(pl.multiple_of((tile_row - 1) * slab, slab), slab), :] = mixed

    @pl.when(step == 2 * tile_rows - 3)
    def _():
        hand_out(send_refs, out_ref, group, xor)
        for at in range(tile_rows):
            for copy in out_copies(at):
                copy.wait()
        for copy in (*edge_copies(), *halo_copies()):
            copy.wait()


def spatial_inner(x, w, wo, targets, counts, peers, xor):
    rows, columns, feat = x.shape
    tile_rows = rows // TH
    slab = TH * columns
    v_rows = PAIRS * PAIR_ROWS
    group = (tile_rows - 2) * slab // peers
    smem = pl.BlockSpec(memory_space=pltpu.SMEM)
    hbm, vmem = pl.BlockSpec(memory_space=pltpu.HBM), pl.BlockSpec(memory_space=pltpu.VMEM)
    outs = pl.pallas_call(
        functools.partial(inner_kernel, group, peers, xor),
        grid=(2 * tile_rows - 2,),
        in_specs=[smem, smem, hbm, vmem, vmem],
        out_specs=[hbm] * 6 + [pl.BlockSpec((slab, feat), lambda i: (jnp.maximum(i - tile_rows, 0), 0))]
        + [pl.BlockSpec((group, feat), lambda i: (0, 0))] * peers,
        out_shape=[
            jax.ShapeDtypeStruct((tile_rows * slab, WIDE), BF16),
            jax.ShapeDtypeStruct((tile_rows * slab, WIDE), BF16),
            jax.ShapeDtypeStruct((tile_rows * v_rows, slab), BF16),
            jax.ShapeDtypeStruct((2, columns // TW, TH, TW, feat), BF16),
            jax.ShapeDtypeStruct((v_rows + WIDE, slab), BF16),
            jax.ShapeDtypeStruct((v_rows + WIDE, slab), BF16),
            jax.ShapeDtypeStruct(((tile_rows - 2) * slab, feat), BF16),
        ]
        + [jax.ShapeDtypeStruct((group, feat), BF16)] * peers,
        scratch_shapes=[
            pltpu.VMEM((tile_rows, columns // TW, TH, TW, feat), BF16),
            pltpu.VMEM((tile_rows, slab, WIDE), BF16),
            pltpu.VMEM((tile_rows, slab, WIDE), BF16),
            pltpu.VMEM((tile_rows, v_rows, slab), BF16),
            pltpu.VMEM((1, 2 * INNER), F32),
            pltpu.VMEM((INNER, 1), F32),
            pltpu.VMEM((columns // TW // 2 * PAIRS, 3 * slab, 4 * TILE), BF16),
            pltpu.VMEM((INNER, slab), F32),
            pltpu.VMEM(((tile_rows - 2) * slab, feat), BF16),
            pltpu.SemaphoreType.DMA((tile_rows, columns // TW)),
            pltpu.SemaphoreType.DMA((4, tile_rows)),
            pltpu.SemaphoreType.DMA((2, 1 + len(list(packed_keys(slab))))),
        ],
        compiler_params=params(VMEM_WHOLE),
        cost_estimate=cost(12 * 10**9, 16 * 2**20),
        name="spatial_inner",
    )(targets, counts, x, w, wo)
    return outs[:3], outs[3].reshape(2 * slab, feat), outs[4:6], outs[6], outs[7:]


def edges_kernel(
    group, peers, xor, tile_rows, columns,
    targets_ref, counts_ref, x_ref, q_ref, k0, k1, k2, v0, v1, v2, top_ref, bot_ref, w_ref, mixed_ref, *rest,
):
    send_refs, rest = rest[:peers], rest[peers:]
    p_ref, acc_ref, out_ref, k_prev, k_next, v_prev, v_next = rest
    step = pl.program_id(0)
    slab = x_ref.shape[0]

    @pl.when(step == 0)
    def _():
        p_ref[...] = jnp.zeros(p_ref.shape, BF16)
        unpack_halo(top_ref, k_prev, v_prev)
        k_next[...] = k2[...]
        v_next[...] = v2[...]

    @pl.when(step != 0)
    def _():
        k_prev[...] = k0[...]
        v_prev[...] = v0[...]
        unpack_halo(bot_ref, k_next, v_next)

    attend_tile_row(
        step * (tile_rows - 1), tile_rows, columns, targets_ref, counts_ref, q_ref,
        (k_prev, k1, k_next), (v_prev, v1, v_next), p_ref, acc_ref,
    )
    branch = nn_dot(acc_ref[...].T.astype(BF16), w_ref[...])
    mixed = (x_ref[...].astype(F32) + branch).astype(BF16)
    mixed_ref[...] = mixed
    out_ref[pl.ds(pl.multiple_of(step * slab, slab), slab), :] = mixed

    @pl.when(step == 1)
    def _():
        hand_out(send_refs, out_ref, group, xor)


def spatial_edges(x, q, k, v, halos, w, targets, counts, slab, columns, peers, xor):
    feat = x.shape[1]
    tile_rows = q.shape[0] // slab
    group = 2 * slab // peers
    v_rows = PAIRS * PAIR_ROWS
    at = lambda i: i * (tile_rows - 1)
    smem = pl.BlockSpec(memory_space=pltpu.SMEM)
    whole = lambda *shape: pl.BlockSpec(shape, lambda i: (0, 0))
    in_specs = [
        smem,
        smem,
        pl.BlockSpec((slab, feat), lambda i: (i, 0)),
        pl.BlockSpec((slab, WIDE), lambda i: (at(i), 0)),
    ]
    for block in ((slab, WIDE), (v_rows, slab)):
        in_specs += [
            pl.BlockSpec(block, lambda i: (tile_rows - 2, 0)),
            pl.BlockSpec(block, lambda i: (at(i), 0)),
            pl.BlockSpec(block, lambda i: (1, 0)),
        ]
    in_specs += [whole(*halo.shape) for halo in halos]
    in_specs.append(whole(*w.shape))
    outs = pl.pallas_call(
        functools.partial(edges_kernel, group, peers, xor, tile_rows, columns),
        grid=(2,),
        in_specs=in_specs,
        out_specs=[pl.BlockSpec((slab, feat), lambda i: (i, 0))]
        + [whole(group, feat)] * peers,
        out_shape=[jax.ShapeDtypeStruct((2 * slab, feat), BF16)]
        + [jax.ShapeDtypeStruct((group, feat), BF16)] * peers,
        scratch_shapes=[
            pltpu.VMEM((columns // TW // 2 * PAIRS, 3 * slab, 4 * TILE), BF16),
            pltpu.VMEM((INNER, slab), F32),
            pltpu.VMEM((2 * slab, feat), BF16),
            pltpu.VMEM((slab, WIDE), BF16),
            pltpu.VMEM((slab, WIDE), BF16),
            pltpu.VMEM((v_rows, slab), BF16),
            pltpu.VMEM((v_rows, slab), BF16),
        ],
        compiler_params=params(),
        cost_estimate=cost(6 * 10**9, 8 * 2**20),
        name="spatial_edges",
    )(targets, counts, x, q, k, k, k, v, v, v, *halos, w)
    return outs[0], outs[1:]


def temporal_kernel(peers, group, early, *refs):
    in_refs, w_ref, early_refs = refs[:peers], refs[peers], refs[peers + 1 : -6 - peers]
    out_refs, (x_ref, q_ref, k_ref, v_ref, p_ref, acc_ref) = refs[-6 - peers : -6], refs[-6:]
    for slot, ref in zip(early, early_refs):
        out_refs[slot][: ref.shape[0], :] = ref[...]
    block = peers * PACK
    parts = group // PACK
    tokens = peers * group

    for part in range(parts):
        for j in range(peers):
            to = pl.ds(part * block + j * PACK, PACK)
            x_ref[to, :] = in_refs[j][pl.ds(part * PACK, PACK), :]
    x_ref[tokens:, :] = jnp.ones((PACK, x_ref.shape[1]), BF16)
    x = x_ref[:tokens, :]
    mean, rstd = moments(x)
    prod = nt_dot(x_ref[...], w_ref[: 2 * INNER, :])
    prod = (prod[:tokens] - mean * prod[tokens : tokens + 1]) * rstd
    q, k = split_queries_keys(prod)
    q_ref[...] = (q * (LOG2E * HD**-0.5)).astype(BF16)
    k_ref[...] = k.astype(BF16)
    w_values = w_ref[2 * INNER :, :]
    values = (nt_dot(w_values, x) - row_sums(w_values) * as_rows(mean)) * as_rows(rstd)
    store_values(v_ref, values.astype(BF16), slice(None))
    row = lax.broadcasted_iota(jnp.int32, (block, 2 * block), 0)
    col = lax.broadcasted_iota(jnp.int32, (block, 2 * block), 1)
    bias = jnp.where(row % PACK == col % PACK, 0.0, NEG).astype(F32)
    for part in range(parts):
        at = part * block
        for pair in range(PAIRS):
            lo, hi = pair_window(pair)
            queries = two_heads(q_ref[at : at + block, lo:hi], pair)
            scores = nt_dot(k_ref[at : at + block, lo:hi], queries) + bias
            expo = jnp.exp2(scores - jnp.max(scores, axis=0, keepdims=True))
            p_ref[part * PAIRS + pair] = expo.astype(BF16)
    for part in range(parts):
        at = part * block
        for pair in range(PAIRS):
            weights = v_ref[pair * PAIR_ROWS : (pair + 1) * PAIR_ROWS, at : at + block]
            out = nn_dot(weights, p_ref[part * PAIRS + pair])
            out = out[:PAIR] * (1.0 / out[PAIR : PAIR + 1])
            acc_ref[pair * PAIR : pair * PAIR + HD, at : at + block] = out[:HD, :block]
            acc_ref[pair * PAIR + HD : (pair + 1) * PAIR, at : at + block] = out[HD:, block:]
    for part in range(parts):
        at = part * block
        heads = acc_ref[:, at : at + block].T.astype(BF16)
        for j in range(peers):
            rows = pl.ds(out_refs[j].shape[0] - group + part * PACK, PACK)
            out_refs[j][rows, :] = heads[j * PACK : (j + 1) * PACK]


def temporal(pieces, w, early=None):
    early = early or {}
    peers = len(pieces)
    group, feat = pieces[0].shape
    tokens = peers * group
    rows = [group + (early[slot].shape[0] if slot in early else 0) for slot in range(peers)]
    return pl.pallas_call(
        functools.partial(temporal_kernel, peers, group, tuple(early)),
        out_shape=[jax.ShapeDtypeStruct((count, INNER), BF16) for count in rows],
        scratch_shapes=[
            pltpu.VMEM((tokens + PACK, feat), BF16),
            pltpu.VMEM((tokens, WIDE), BF16),
            pltpu.VMEM((tokens, WIDE), BF16),
            pltpu.VMEM((PAIRS * PAIR_ROWS, tokens), BF16),
            pltpu.VMEM((group // PACK * PAIRS, peers * PACK, 2 * peers * PACK), BF16),
            pltpu.VMEM((INNER, tokens), F32),
        ],
        compiler_params=params(),
        cost_estimate=cost(4 * 10**9, 6 * 2**20),
        name="temporal",
    )(*pieces, w, *early.values())


def final_kernel(inner, groups, early, xor, columns, *refs):
    in_refs, (first_ref, second_ref, w_ref, out_ref, heads_ref) = refs[:-5], refs[-5:]
    in_refs, early_refs = in_refs[: -len(early)], dict(zip(early, in_refs[-len(early) :]))
    step = pl.program_id(0)
    slab = first_ref.shape[0]
    peers = len(in_refs)

    @pl.when(step == 0)
    def _():
        for slot, ref in enumerate(in_refs):
            peer = peer_of(slot, peers, xor)
            to = pl.ds(pl.multiple_of(peer * groups[0], PACK), groups[0])
            heads_ref[to, :] = early_refs[slot][...] if slot in early_refs else ref[: groups[0], :]
            to = pl.multiple_of(peers * groups[0] + peer * groups[1], PACK)
            heads_ref[pl.ds(to, groups[1]), :] = ref[ref.shape[0] - groups[1] :, :]

    def work(mixed_ref):
        heads = heads_ref[pl.ds(pl.multiple_of(step * slab, slab), slab), :]
        result = mixed_ref[...].astype(F32) + nn_dot(heads, w_ref[...])
        for to, at in tile_order(slab, columns):
            out_ref[pl.ds(at, TW), :] = result[to : to + TW].astype(BF16)

    @pl.when(step < inner)
    def _():
        work(first_ref)

    @pl.when(step >= inner)
    def _():
        work(second_ref)


def final(pieces, early, first, second, w, slab, columns, xor):
    feat = first.shape[1]
    inner = first.shape[0] // slab
    tile_rows = inner + 2
    peers = len(pieces)
    groups = (first.shape[0] // peers, second.shape[0] // peers)
    at = lambda i: jnp.where(i < inner, i + 1, (i - inner) * (tile_rows - 1))
    whole = lambda *shape: pl.BlockSpec(shape, lambda i: (0, 0))
    return pl.pallas_call(
        functools.partial(final_kernel, inner, groups, tuple(early), xor, columns),
        grid=(tile_rows,),
        in_specs=[whole(*piece.shape) for piece in (*pieces, *early.values())]
        + [
            pl.BlockSpec((slab, feat), lambda i: (jnp.minimum(i, inner - 1), 0)),
            pl.BlockSpec((slab, feat), lambda i: (jnp.maximum(i - inner, 0), 0)),
            whole(*w.shape),
        ],
        out_specs=pl.BlockSpec((slab, feat), lambda i: (at(i), 0)),
        out_shape=jax.ShapeDtypeStruct((tile_rows * slab, feat), BF16),
        scratch_shapes=[pltpu.VMEM((tile_rows * slab, INNER), BF16)],
        compiler_params=params(),
        cost_estimate=cost(2 * 10**9, 6 * 2**20),
        name="final",
    )(*pieces, *early.values(), first, second, w)


def neighbours(top, bot):
    size = lax.axis_size("row")
    up = [(i, i + 1) for i in range(size - 1)]
    down = [(j, i) for i, j in up]
    return lax.ppermute(bot, "row", up), lax.ppermute(top, "row", down)


def exchange(pieces, xor, back):
    size = lax.axis_size("frame")
    result = {}
    for slot, piece in pieces.items():
        j = (size - slot) % size
        if xor:
            pairs = [(i, i ^ j) for i in range(size)]
        else:
            pairs = [(i, (i - j if back else i + j) % size) for i in range(size)]
        result[slot] = lax.ppermute(piece, "frame", pairs) if slot else piece
    return result


def by_slot(pieces):
    return dict(enumerate(pieces))


def body(frames_in, spatial_qkv, spatial_out, temporal_qkv, temporal_out, key_tiles, tile_counts):
    _, rows_dev, columns, feat = frames_in.shape
    slab = TH * columns
    peers = lax.axis_size("frame")
    xor = peers & (peers - 1) == 0
    qkv, edges, halos, mixed_a, send_a = spatial_inner(
        frames_in[0], spatial_qkv.T, spatial_out, key_tiles, tile_counts, peers, xor
    )
    got_a = exchange(by_slot(send_a), xor, False)
    halos = neighbours(*halos)
    mixed_b, send_b = spatial_edges(
        edges, *qkv, halos, spatial_out, key_tiles, tile_counts, slab, columns, peers, xor
    )
    got_b = exchange(by_slot(send_b), xor, False)
    heads_a = by_slot(temporal(list(got_a.values()), temporal_qkv.T))
    far = range(1, 1 + peers // 4)
    early = exchange({slot: heads_a.pop(slot) for slot in far}, xor, True)
    heads = by_slot(temporal(list(got_b.values()), temporal_qkv.T, heads_a))
    back = exchange(heads, xor, True)
    out = final(
        list(back.values()), early, mixed_a, mixed_b, temporal_out, slab, columns, xor
    )
    return out.reshape(frames_in.shape)


def solution(mesh):
    in_specs = (
        P("frame", "row", None, None),
        P(),
        P(),
        P(),
        P(),
        P("frame", "row", None),
        P("frame", "row"),
    )
    out_specs = P("frame", "row", None, None)
    return jax.shard_map(body, mesh=mesh, in_specs=in_specs, out_specs=out_specs, check_vma=False)
```

```python
import functools

import jax
import jax.numpy as jnp
from jax import lax
from jax.experimental import pallas as pl
from jax.experimental.pallas import tpu as pltpu
from jax.sharding import PartitionSpec as P

HEADS = 8
HD = 72
TH = 4
TW = 16
LANES = 128
PACK = 16
NORM_EPS = 1e-06
NEG = -1e30
LOG2E = 1.4426950408889634
F32 = jnp.float32
BF16 = jnp.bfloat16
INNER = HEADS * HD
WIDE = -(-INNER // LANES) * LANES
PAIR = 2 * HD
PAIRS = HEADS // 2
PACE = 2
PAIR_ROWS = PAIR + PACK
TILE = TH * TW
VMEM_LIMIT = 28 * 1024 * 1024
VMEM_WHOLE = 58 * 1024 * 1024


def params(limit=VMEM_LIMIT):
    return pltpu.CompilerParams(vmem_limit_bytes=limit)


def cost(flops, bytes_accessed):
    return pl.CostEstimate(flops=flops, bytes_accessed=bytes_accessed, transcendentals=0)


def nt_dot(a, b):
    return lax.dot_general(a, b, (((1,), (1,)), ((), ())), preferred_element_type=F32)


def nn_dot(a, b):
    return jnp.dot(a, b, preferred_element_type=F32)


def moments(x):
    x = x.astype(F32)
    mean = jnp.mean(x, axis=-1, keepdims=True)
    centred = x - mean
    spread = jnp.mean(centred * centred, axis=-1, keepdims=True)
    return mean, lax.rsqrt(spread + NORM_EPS)


def as_rows(column):
    return jnp.broadcast_to(column, (column.shape[0], LANES)).T[:1]


def tile_order(rows, columns):
    for col in range(columns // TW):
        for row in range(TH):
            yield (col * TH + row) * TW, row * columns + col * TW


def pair_window(pair):
    return pair * PAIR // LANES * LANES, -(-(pair + 1) * PAIR // LANES) * LANES


def two_heads(queries, pair):
    lo, hi = pair_window(pair)
    lane = lax.broadcasted_iota(jnp.int32, queries.shape, 1) + lo
    start = pair * PAIR
    first = jnp.where((lane >= start) & (lane < start + HD), queries, 0)
    second = jnp.where((lane >= start + HD) & (lane < start + PAIR), queries, 0)
    return jnp.concatenate([first, second], axis=0)


def split_queries_keys(prod):
    keys = prod[:, INNER // LANES * LANES :]
    shift = INNER % LANES
    if shift:
        keys = pltpu.roll(keys, keys.shape[1] - shift, 1)
    return prod[:, :WIDE], keys


def row_sums(w):
    return jnp.sum(w.astype(F32), axis=-1, keepdims=True)


def store_values(v_ref, values, lanes):
    for pair in range(PAIRS):
        at = pair * PAIR_ROWS
        v_ref[at : at + PAIR, lanes] = values[pair * PAIR : (pair + 1) * PAIR]
        v_ref[at + PAIR : at + PAIR_ROWS, lanes] = jnp.ones((PACK, values.shape[1]), BF16)


def packed_keys(slab):
    per = slab // LANES
    full = WIDE // slab * per
    for piece in range(WIDE // LANES):
        lanes = pl.ds(piece * LANES, LANES)
        if piece < full:
            yield pl.ds(0, slab), lanes, pl.ds(piece // per * slab, slab), pl.ds(piece % per * LANES, LANES)
        else:
            rows = slab // per
            for part in range(per):
                to = pl.ds(full // per * slab, rows), pl.ds(part * LANES, LANES)
                yield pl.ds(part * rows, rows), lanes, *to


def unpack_halo(halo_ref, k_ref, v_ref):
    size = v_ref.shape[0]
    v_ref[...] = halo_ref[:size, :]
    for rows, lanes, at, to in packed_keys(k_ref.shape[0]):
        k_ref[rows, lanes] = halo_ref[pl.ds(size + at.start, at.size), to]


def visible_bits(tile, count, global_row, tile_cols, slot_num, targets_ref):
    bits = jnp.int32(0)
    for slot in range(slot_num):
        target = targets_ref[slot, 0, tile]
        cand = (lax.div(target, tile_cols) - global_row + 1) * tile_cols + lax.rem(target, tile_cols)
        bits = bits | jnp.where(slot < count, jnp.left_shift(1, cand), 0)
    return bits


def hidden(bits, index):
    return (1 - (jnp.right_shift(bits, index) & 1)).astype(F32) * NEG


def attend_tile_row(
    tile_row, tile_rows, columns, targets_ref, counts_ref, q_ref, k_refs, v_refs, p_ref, acc_ref
):
    slab = q_ref.shape[0]
    tile_cols = columns // TW
    slot_num = targets_ref.shape[0]
    global_row = lax.axis_index("row") * tile_rows + tile_row
    left = lax.broadcasted_iota(jnp.int32, (1, 4 * TILE), 1) % (2 * TILE) < TILE
    for duo in range(tile_cols // 2):
        bits = []
        for tile in (2 * duo, 2 * duo + 1):
            tile = tile_row * tile_cols + tile
            bits.append(
                visible_bits(tile, counts_ref[0, tile], global_row, tile_cols, slot_num, targets_ref)
            )
        lowest, highest = max(2 * duo - 1, 0), min(2 * duo + 2, tile_cols - 1)
        span = range(lowest, highest + 1)
        bias = {}
        for j in range(3):
            for col in span:
                at = j * tile_cols + col
                bias[j, col] = jnp.where(left, hidden(bits[0], at), hidden(bits[1], at))
        for pair in range(PAIRS):
            lo, hi = pair_window(pair)
            queries = two_heads(q_ref[2 * duo * TILE : (2 * duo + 2) * TILE, lo:hi], pair)
            scores = {}
            for j, ref in enumerate(k_refs):
                part = nt_dot(ref[lowest * TILE : (highest + 1) * TILE, lo:hi], queries)
                for col in span:
                    at = (col - lowest) * TILE
                    scores[j, col] = part[at : at + TILE] + bias[j, col]
            top = functools.reduce(jnp.maximum, scores.values())
            top = jnp.max(top, axis=0, keepdims=True)
            for (j, col), score in scores.items():
                at = j * slab + col * TILE
                p_ref[duo * PAIRS + pair, at : at + TILE, :] = jnp.exp2(score - top).astype(BF16)

    for duo in range(tile_cols // 2):
        for pair in range(PAIRS):
            out = sum(
                nn_dot(
                    ref[pair * PAIR_ROWS : (pair + 1) * PAIR_ROWS, :],
                    p_ref[duo * PAIRS + pair, j * slab : (j + 1) * slab, :],
                )
                for j, ref in enumerate(v_refs)
            )
            out = out[:PAIR] * (1.0 / out[PAIR : PAIR + 1])
            lanes = slice(2 * duo * TILE, (2 * duo + 2) * TILE)
            acc_ref[pair * PAIR : pair * PAIR + HD, lanes] = out[:HD, : 2 * TILE]
            acc_ref[pair * PAIR + HD : (pair + 1) * PAIR, lanes] = out[HD:, 2 * TILE :]


def reach(peers):
    far, near = list(range(peers - 1, peers // 2 - 1, -1)), list(range(peers // 2 - 1, 0, -1))
    half = len(far) // 2
    return [0] + far[:half] + near[:1] + far[half:] + near[1:]


def peer_of(slot, peers, xor):
    me, j = lax.axis_index("frame"), reach(peers)[slot]
    return me ^ j if xor else lax.rem(me + j, peers)


def hand_out(send_refs, out_ref, group, xor):
    for slot, ref in enumerate(send_refs):
        peer = peer_of(slot, len(send_refs), xor)
        ref[...] = out_ref[pl.ds(pl.multiple_of(peer * group, PACK), group), :]


def inner_kernel(
    group, peers, xor,
    targets_ref, counts_ref, x_hbm, w_ref, wo_ref, q_hbm, k_hbm, v_hbm, edge_hbm, top_hbm, bot_hbm, mixed_ref,
    *rest,
):
    send_refs, rest = rest[:peers], rest[peers:]
    x_ref, q_ref, k_ref, v_ref, sum_ref, col_ref, p_ref, acc_ref, out_ref, x_sem, out_sem, halo_sem = rest
    step = pl.program_id(0)
    tile_rows, tile_cols = x_ref.shape[:2]
    columns = tile_cols * TW
    feat = x_ref.shape[-1]
    slab = tile_cols * TILE
    v_rows = PAIRS * PAIR_ROWS
    ahead = tile_rows // PACE

    def x_copy(at, col):
        return pltpu.make_async_copy(
            x_hbm.at[pl.ds(at * TH, TH), pl.ds(col * TW, TW), :], x_ref.at[at, col], x_sem.at[at, col]
        )

    def out_copies(at):
        rows, wide = pl.ds(at * slab, slab), pl.ds(at * v_rows, v_rows)
        return (
            pltpu.make_async_copy(q_ref.at[at], q_hbm.at[rows], out_sem.at[0, at]),
            pltpu.make_async_copy(k_ref.at[at], k_hbm.at[rows], out_sem.at[1, at]),
            pltpu.make_async_copy(v_ref.at[at], v_hbm.at[wide], out_sem.at[2, at]),
        )

    def edge_copies():
        for part, at in enumerate((0, tile_rows - 1)):
            yield pltpu.make_async_copy(x_ref.at[at], edge_hbm.at[part], out_sem.at[3, part])

    def halo_copies():
        for part, (at, halo) in enumerate(((0, top_hbm), (tile_rows - 1, bot_hbm))):
            yield pltpu.make_async_copy(v_ref.at[at], halo.at[pl.ds(0, v_rows)], halo_sem.at[part, 0])
            for piece, (rows, lanes, to, lane) in enumerate(packed_keys(slab)):
                to = pl.ds(v_rows + to.start, to.size)
                yield pltpu.make_async_copy(
                    k_ref.at[at, rows, lanes], halo.at[to, lane], halo_sem.at[part, 1 + piece]
                )

    def work(first):
        for part in range(PACE):
            for col in range(tile_cols):
                x_copy(step * PACE + part, col).wait()
        size = PACE * slab
        x = x_ref[pl.ds(step * PACE, PACE)].reshape(size, feat)
        mean, rstd = moments(x)
        rows = x
        if first:
            rows = jnp.concatenate([x, jnp.ones((PACK, feat), BF16)], axis=0)
        prod = nt_dot(rows, w_ref[: 2 * INNER, :])
        if first:
            sum_ref[...] = prod[size : size + 1]
            col_ref[...] = row_sums(w_ref[2 * INNER :, :])
        q, k = split_queries_keys((prod[:size] - mean * sum_ref[...]) * rstd)
        q, k = (q * (LOG2E * HD**-0.5)).astype(BF16), k.astype(BF16)
        values = nt_dot(w_ref[2 * INNER :, :], x) - col_ref[...] * as_rows(mean)
        values = (values * as_rows(rstd)).astype(BF16)
        for part in range(PACE):
            at, own = step * PACE + part, slice(part * slab, (part + 1) * slab)
            q_ref[at], k_ref[at] = q[own], k[own]
            store_values(v_ref.at[at], values[:, own], slice(None))
            for copy in out_copies(at):
                copy.start()

    @pl.when(step == 0)
    def _():
        for at in range(tile_rows):
            for col in range(tile_cols):
                x_copy(at, col).start()
        work(True)

    @pl.when((step > 0) & (step < ahead))
    def _():
        work(False)

    @pl.when(step == ahead)
    def _():
        for copy in (*edge_copies(), *halo_copies()):
            copy.start()
        p_ref[...] = jnp.zeros(p_ref.shape, BF16)

    @pl.when(step >= ahead)
    def _():
        tile_row = step - ahead + 1
        k_refs = [k_ref.at[tile_row + j] for j in (-1, 0, 1)]
        v_refs = [v_ref.at[tile_row + j] for j in (-1, 0, 1)]
        attend_tile_row(
            tile_row, tile_rows, columns, targets_ref, counts_ref, q_ref.at[tile_row],
            k_refs, v_refs, p_ref, acc_ref,
        )
        branch = nn_dot(acc_ref[...].T.astype(BF16), wo_ref[...])
        mixed = (x_ref[tile_row].reshape(slab, feat).astype(F32) + branch).astype(BF16)
        mixed_ref[...] = mixed
        out_ref[pl.ds(pl.multiple_of((tile_row - 1) * slab, slab), slab), :] = mixed

    @pl.when(step == ahead + tile_rows - 3)
    def _():
        hand_out(send_refs, out_ref, group, xor)
        for at in range(tile_rows):
            for copy in out_copies(at):
                copy.wait()
        for copy in (*edge_copies(), *halo_copies()):
            copy.wait()


def spatial_inner(x, w, wo, targets, counts, peers, xor):
    rows, columns, feat = x.shape
    tile_rows = rows // TH
    slab = TH * columns
    v_rows = PAIRS * PAIR_ROWS
    ahead = tile_rows // PACE
    group = (tile_rows - 2) * slab // peers
    smem = pl.BlockSpec(memory_space=pltpu.SMEM)
    hbm, vmem = pl.BlockSpec(memory_space=pltpu.HBM), pl.BlockSpec(memory_space=pltpu.VMEM)
    outs = pl.pallas_call(
        functools.partial(inner_kernel, group, peers, xor),
        grid=(ahead + tile_rows - 2,),
        in_specs=[smem, smem, hbm, vmem, vmem],
        out_specs=[hbm] * 6 + [pl.BlockSpec((slab, feat), lambda i: (jnp.maximum(i - ahead, 0), 0))]
        + [pl.BlockSpec((group, feat), lambda i: (0, 0))] * peers,
        out_shape=[
            jax.ShapeDtypeStruct((tile_rows * slab, WIDE), BF16),
            jax.ShapeDtypeStruct((tile_rows * slab, WIDE), BF16),
            jax.ShapeDtypeStruct((tile_rows * v_rows, slab), BF16),
            jax.ShapeDtypeStruct((2, columns // TW, TH, TW, feat), BF16),
            jax.ShapeDtypeStruct((v_rows + WIDE, slab), BF16),
            jax.ShapeDtypeStruct((v_rows + WIDE, slab), BF16),
            jax.ShapeDtypeStruct(((tile_rows - 2) * slab, feat), BF16),
        ]
        + [jax.ShapeDtypeStruct((group, feat), BF16)] * peers,
        scratch_shapes=[
            pltpu.VMEM((tile_rows, columns // TW, TH, TW, feat), BF16),
            pltpu.VMEM((tile_rows, slab, WIDE), BF16),
            pltpu.VMEM((tile_rows, slab, WIDE), BF16),
            pltpu.VMEM((tile_rows, v_rows, slab), BF16),
            pltpu.VMEM((1, 2 * INNER), F32),
            pltpu.VMEM((INNER, 1), F32),
            pltpu.VMEM((columns // TW // 2 * PAIRS, 3 * slab, 4 * TILE), BF16),
            pltpu.VMEM((INNER, slab), F32),
            pltpu.VMEM(((tile_rows - 2) * slab, feat), BF16),
            pltpu.SemaphoreType.DMA((tile_rows, columns // TW)),
            pltpu.SemaphoreType.DMA((4, tile_rows)),
            pltpu.SemaphoreType.DMA((2, 1 + len(list(packed_keys(slab))))),
        ],
        compiler_params=params(VMEM_WHOLE),
        cost_estimate=cost(12 * 10**9, 16 * 2**20),
        name="spatial_inner",
    )(targets, counts, x, w, wo)
    return outs[:3], outs[3].reshape(2 * slab, feat), outs[4:6], outs[6], outs[7:]


def edges_kernel(
    group, peers, xor, tile_rows, columns,
    targets_ref, counts_ref, x_ref, q_ref, k0, k1, k2, v0, v1, v2, top_ref, bot_ref, w_ref, mixed_ref, *rest,
):
    send_refs, rest = rest[:peers], rest[peers:]
    p_ref, acc_ref, out_ref, k_prev, k_next, v_prev, v_next = rest
    step = pl.program_id(0)
    slab = x_ref.shape[0]

    @pl.when(step == 0)
    def _():
        p_ref[...] = jnp.zeros(p_ref.shape, BF16)
        unpack_halo(top_ref, k_prev, v_prev)
        k_next[...] = k2[...]
        v_next[...] = v2[...]

    @pl.when(step != 0)
    def _():
        k_prev[...] = k0[...]
        v_prev[...] = v0[...]
        unpack_halo(bot_ref, k_next, v_next)

    attend_tile_row(
        step * (tile_rows - 1), tile_rows, columns, targets_ref, counts_ref, q_ref,
        (k_prev, k1, k_next), (v_prev, v1, v_next), p_ref, acc_ref,
    )
    branch = nn_dot(acc_ref[...].T.astype(BF16), w_ref[...])
    mixed = (x_ref[...].astype(F32) + branch).astype(BF16)
    mixed_ref[...] = mixed
    out_ref[pl.ds(pl.multiple_of(step * slab, slab), slab), :] = mixed

    @pl.when(step == 1)
    def _():
        hand_out(send_refs, out_ref, group, xor)


def spatial_edges(x, q, k, v, halos, w, targets, counts, slab, columns, peers, xor):
    feat = x.shape[1]
    tile_rows = q.shape[0] // slab
    group = 2 * slab // peers
    v_rows = PAIRS * PAIR_ROWS
    at = lambda i: i * (tile_rows - 1)
    smem = pl.BlockSpec(memory_space=pltpu.SMEM)
    whole = lambda *shape: pl.BlockSpec(shape, lambda i: (0, 0))
    in_specs = [
        smem,
        smem,
        pl.BlockSpec((slab, feat), lambda i: (i, 0)),
        pl.BlockSpec((slab, WIDE), lambda i: (at(i), 0)),
    ]
    for block in ((slab, WIDE), (v_rows, slab)):
        in_specs += [
            pl.BlockSpec(block, lambda i: (tile_rows - 2, 0)),
            pl.BlockSpec(block, lambda i: (at(i), 0)),
            pl.BlockSpec(block, lambda i: (1, 0)),
        ]
    in_specs += [whole(*halo.shape) for halo in halos]
    in_specs.append(whole(*w.shape))
    outs = pl.pallas_call(
        functools.partial(edges_kernel, group, peers, xor, tile_rows, columns),
        grid=(2,),
        in_specs=in_specs,
        out_specs=[pl.BlockSpec((slab, feat), lambda i: (i, 0))]
        + [whole(group, feat)] * peers,
        out_shape=[jax.ShapeDtypeStruct((2 * slab, feat), BF16)]
        + [jax.ShapeDtypeStruct((group, feat), BF16)] * peers,
        scratch_shapes=[
            pltpu.VMEM((columns // TW // 2 * PAIRS, 3 * slab, 4 * TILE), BF16),
            pltpu.VMEM((INNER, slab), F32),
            pltpu.VMEM((2 * slab, feat), BF16),
            pltpu.VMEM((slab, WIDE), BF16),
            pltpu.VMEM((slab, WIDE), BF16),
            pltpu.VMEM((v_rows, slab), BF16),
            pltpu.VMEM((v_rows, slab), BF16),
        ],
        compiler_params=params(),
        cost_estimate=cost(6 * 10**9, 8 * 2**20),
        name="spatial_edges",
    )(targets, counts, x, q, k, k, k, v, v, v, *halos, w)
    return outs[0], outs[1:]


def temporal_kernel(peers, group, early, *refs):
    in_refs, w_ref, early_refs = refs[:peers], refs[peers], refs[peers + 1 : -6 - peers]
    out_refs, (x_ref, q_ref, k_ref, v_ref, p_ref, acc_ref) = refs[-6 - peers : -6], refs[-6:]
    for slot, ref in zip(early, early_refs):
        out_refs[slot][: ref.shape[0], :] = ref[...]
    block = peers * PACK
    parts = group // PACK
    tokens = peers * group

    for part in range(parts):
        for j in range(peers):
            to = pl.ds(part * block + j * PACK, PACK)
            x_ref[to, :] = in_refs[j][pl.ds(part * PACK, PACK), :]
    x_ref[tokens:, :] = jnp.ones((PACK, x_ref.shape[1]), BF16)
    x = x_ref[:tokens, :]
    mean, rstd = moments(x)
    prod = nt_dot(x_ref[...], w_ref[: 2 * INNER, :])
    prod = (prod[:tokens] - mean * prod[tokens : tokens + 1]) * rstd
    q, k = split_queries_keys(prod)
    q_ref[...] = (q * (LOG2E * HD**-0.5)).astype(BF16)
    k_ref[...] = k.astype(BF16)
    w_values = w_ref[2 * INNER :, :]
    values = (nt_dot(w_values, x) - row_sums(w_values) * as_rows(mean)) * as_rows(rstd)
    store_values(v_ref, values.astype(BF16), slice(None))
    row = lax.broadcasted_iota(jnp.int32, (block, 2 * block), 0)
    col = lax.broadcasted_iota(jnp.int32, (block, 2 * block), 1)
    bias = jnp.where(row % PACK == col % PACK, 0.0, NEG).astype(F32)
    for part in range(parts):
        at = part * block
        for pair in range(PAIRS):
            lo, hi = pair_window(pair)
            queries = two_heads(q_ref[at : at + block, lo:hi], pair)
            scores = nt_dot(k_ref[at : at + block, lo:hi], queries) + bias
            expo = jnp.exp2(scores - jnp.max(scores, axis=0, keepdims=True))
            p_ref[part * PAIRS + pair] = expo.astype(BF16)
    for part in range(parts):
        at = part * block
        for pair in range(PAIRS):
            weights = v_ref[pair * PAIR_ROWS : (pair + 1) * PAIR_ROWS, at : at + block]
            out = nn_dot(weights, p_ref[part * PAIRS + pair])
            out = out[:PAIR] * (1.0 / out[PAIR : PAIR + 1])
            acc_ref[pair * PAIR : pair * PAIR + HD, at : at + block] = out[:HD, :block]
            acc_ref[pair * PAIR + HD : (pair + 1) * PAIR, at : at + block] = out[HD:, block:]
    for part in range(parts):
        at = part * block
        heads = acc_ref[:, at : at + block].T.astype(BF16)
        for j in range(peers):
            rows = pl.ds(out_refs[j].shape[0] - group + part * PACK, PACK)
            out_refs[j][rows, :] = heads[j * PACK : (j + 1) * PACK]


def temporal(pieces, w, early=None):
    early = early or {}
    peers = len(pieces)
    group, feat = pieces[0].shape
    tokens = peers * group
    rows = [group + (early[slot].shape[0] if slot in early else 0) for slot in range(peers)]
    return pl.pallas_call(
        functools.partial(temporal_kernel, peers, group, tuple(early)),
        out_shape=[jax.ShapeDtypeStruct((count, INNER), BF16) for count in rows],
        scratch_shapes=[
            pltpu.VMEM((tokens + PACK, feat), BF16),
            pltpu.VMEM((tokens, WIDE), BF16),
            pltpu.VMEM((tokens, WIDE), BF16),
            pltpu.VMEM((PAIRS * PAIR_ROWS, tokens), BF16),
            pltpu.VMEM((group // PACK * PAIRS, peers * PACK, 2 * peers * PACK), BF16),
            pltpu.VMEM((INNER, tokens), F32),
        ],
        compiler_params=params(),
        cost_estimate=cost(4 * 10**9, 6 * 2**20),
        name="temporal",
    )(*pieces, w, *early.values())


def final_kernel(inner, groups, early, xor, columns, *refs):
    in_refs, (first_ref, second_ref, w_ref, out_ref, heads_ref) = refs[:-5], refs[-5:]
    in_refs, early_refs = in_refs[: -len(early)], dict(zip(early, in_refs[-len(early) :]))
    step = pl.program_id(0)
    slab = first_ref.shape[0]
    peers = len(in_refs)

    @pl.when(step == 0)
    def _():
        for slot, ref in enumerate(in_refs):
            peer = peer_of(slot, peers, xor)
            to = pl.ds(pl.multiple_of(peer * groups[0], PACK), groups[0])
            heads_ref[to, :] = early_refs[slot][...] if slot in early_refs else ref[: groups[0], :]
            to = pl.multiple_of(peers * groups[0] + peer * groups[1], PACK)
            heads_ref[pl.ds(to, groups[1]), :] = ref[ref.shape[0] - groups[1] :, :]

    def work(mixed_ref):
        heads = heads_ref[pl.ds(pl.multiple_of(step * slab, slab), slab), :]
        result = mixed_ref[...].astype(F32) + nn_dot(heads, w_ref[...])
        for to, at in tile_order(slab, columns):
            out_ref[pl.ds(at, TW), :] = result[to : to + TW].astype(BF16)

    @pl.when(step < inner)
    def _():
        work(first_ref)

    @pl.when(step >= inner)
    def _():
        work(second_ref)


def final(pieces, early, first, second, w, slab, columns, xor):
    feat = first.shape[1]
    inner = first.shape[0] // slab
    tile_rows = inner + 2
    peers = len(pieces)
    groups = (first.shape[0] // peers, second.shape[0] // peers)
    at = lambda i: jnp.where(i < inner, i + 1, (i - inner) * (tile_rows - 1))
    whole = lambda *shape: pl.BlockSpec(shape, lambda i: (0, 0))
    return pl.pallas_call(
        functools.partial(final_kernel, inner, groups, tuple(early), xor, columns),
        grid=(tile_rows,),
        in_specs=[whole(*piece.shape) for piece in (*pieces, *early.values())]
        + [
            pl.BlockSpec((slab, feat), lambda i: (jnp.minimum(i, inner - 1), 0)),
            pl.BlockSpec((slab, feat), lambda i: (jnp.maximum(i - inner, 0), 0)),
            whole(*w.shape),
        ],
        out_specs=pl.BlockSpec((slab, feat), lambda i: (at(i), 0)),
        out_shape=jax.ShapeDtypeStruct((tile_rows * slab, feat), BF16),
        scratch_shapes=[pltpu.VMEM((tile_rows * slab, INNER), BF16)],
        compiler_params=params(),
        cost_estimate=cost(2 * 10**9, 6 * 2**20),
        name="final",
    )(*pieces, *early.values(), first, second, w)


def neighbours(top, bot):
    size = lax.axis_size("row")
    up = [(i, i + 1) for i in range(size - 1)]
    down = [(j, i) for i, j in up]
    return lax.ppermute(bot, "row", up), lax.ppermute(top, "row", down)


def exchange(pieces, xor, back):
    size = lax.axis_size("frame")
    result = {}
    for slot, piece in pieces.items():
        j = reach(size)[slot]
        if xor:
            pairs = [(i, i ^ j) for i in range(size)]
        else:
            pairs = [(i, (i - j if back else i + j) % size) for i in range(size)]
        result[slot] = lax.ppermute(piece, "frame", pairs) if slot else piece
    return result


def by_slot(pieces):
    return dict(enumerate(pieces))


def body(frames_in, spatial_qkv, spatial_out, temporal_qkv, temporal_out, key_tiles, tile_counts):
    _, rows_dev, columns, feat = frames_in.shape
    slab = TH * columns
    key_tiles = key_tiles.transpose(2, 0, 1)
    peers = lax.axis_size("frame")
    xor = peers & (peers - 1) == 0
    qkv, edges, halos, mixed_a, send_a = spatial_inner(
        frames_in[0], spatial_qkv.T, spatial_out, key_tiles, tile_counts, peers, xor
    )
    got_a = exchange(by_slot(send_a), xor, False)
    halos = neighbours(*halos)
    mixed_b, send_b = spatial_edges(
        edges, *qkv, halos, spatial_out, key_tiles, tile_counts, slab, columns, peers, xor
    )
    got_b = exchange(by_slot(send_b), xor, False)
    heads_a = by_slot(temporal(list(got_a.values()), temporal_qkv.T))
    far = range(1, 1 + peers // 4)
    early = exchange({slot: heads_a.pop(slot) for slot in far}, xor, True)
    heads = by_slot(temporal(list(got_b.values()), temporal_qkv.T, heads_a))
    back = exchange(heads, xor, True)
    out = final(
        list(back.values()), early, mixed_a, mixed_b, temporal_out, slab, columns, xor
    )
    return out.reshape(frames_in.shape)


def solution(mesh):
    in_specs = (
        P("frame", "row", None, None),
        P(),
        P(),
        P(),
        P(),
        P("frame", "row", None),
        P("frame", "row"),
    )
    out_specs = P("frame", "row", None, None)
    return jax.shard_map(body, mesh=mesh, in_specs=in_specs, out_specs=out_specs, check_vma=False)
```

```python
import functools

import jax
import jax.numpy as jnp
from jax import lax
from jax.experimental import pallas as pl
from jax.experimental.pallas import tpu as pltpu
from jax.sharding import PartitionSpec as P

HEADS = 8
HD = 72
TH = 4
TW = 16
LANES = 128
PACK = 16
NORM_EPS = 1e-06
NEG = -1e30
LOG2E = 1.4426950408889634
F32 = jnp.float32
BF16 = jnp.bfloat16
INNER = HEADS * HD
WIDE = -(-INNER // LANES) * LANES
PAIR = 2 * HD
PAIRS = HEADS // 2
PACE = 2
PAIR_ROWS = PAIR + PACK
TILE = TH * TW
VMEM_LIMIT = 28 * 1024 * 1024
VMEM_WHOLE = 58 * 1024 * 1024


def params(limit=VMEM_LIMIT):
    return pltpu.CompilerParams(vmem_limit_bytes=limit)


def cost(flops, bytes_accessed):
    return pl.CostEstimate(flops=flops, bytes_accessed=bytes_accessed, transcendentals=0)


def nt_dot(a, b):
    return lax.dot_general(a, b, (((1,), (1,)), ((), ())), preferred_element_type=F32)


def nn_dot(a, b):
    return jnp.dot(a, b, preferred_element_type=F32)


def moments(x):
    x = x.astype(F32)
    mean = jnp.mean(x, axis=-1, keepdims=True)
    centred = x - mean
    spread = jnp.mean(centred * centred, axis=-1, keepdims=True)
    return mean, lax.rsqrt(spread + NORM_EPS)


def as_rows(column):
    return jnp.broadcast_to(column, (column.shape[0], LANES)).T[:1]


def tile_order(rows, columns):
    for col in range(columns // TW):
        for row in range(TH):
            yield (col * TH + row) * TW, row * columns + col * TW


def pair_window(pair):
    return pair * PAIR // LANES * LANES, -(-(pair + 1) * PAIR // LANES) * LANES


def two_heads(queries, pair):
    lo, hi = pair_window(pair)
    lane = lax.broadcasted_iota(jnp.int32, queries.shape, 1) + lo
    start = pair * PAIR
    first = jnp.where((lane >= start) & (lane < start + HD), queries, 0)
    second = jnp.where((lane >= start + HD) & (lane < start + PAIR), queries, 0)
    return jnp.concatenate([first, second], axis=0)


def split_queries_keys(prod):
    keys = prod[:, INNER // LANES * LANES :]
    shift = INNER % LANES
    if shift:
        keys = pltpu.roll(keys, keys.shape[1] - shift, 1)
    return prod[:, :WIDE], keys


def row_sums(w):
    return jnp.sum(w.astype(F32), axis=-1, keepdims=True)


def store_values(v_ref, values, lanes):
    for pair in range(PAIRS):
        at = pair * PAIR_ROWS
        v_ref[at : at + PAIR, lanes] = values[pair * PAIR : (pair + 1) * PAIR]
        v_ref[at + PAIR : at + PAIR_ROWS, lanes] = jnp.ones((PACK, values.shape[1]), BF16)


def packed_keys(slab):
    per = slab // LANES
    full = WIDE // slab * per
    for piece in range(WIDE // LANES):
        lanes = pl.ds(piece * LANES, LANES)
        if piece < full:
            yield pl.ds(0, slab), lanes, pl.ds(piece // per * slab, slab), pl.ds(piece % per * LANES, LANES)
        else:
            rows = slab // per
            for part in range(per):
                to = pl.ds(full // per * slab, rows), pl.ds(part * LANES, LANES)
                yield pl.ds(part * rows, rows), lanes, *to


def unpack_halo(halo_ref, k_ref, v_ref):
    size = v_ref.shape[0]
    v_ref[...] = halo_ref[:size, :]
    for rows, lanes, at, to in packed_keys(k_ref.shape[0]):
        k_ref[rows, lanes] = halo_ref[pl.ds(size + at.start, at.size), to]


def visible_bits(tile, count, global_row, tile_cols, slot_num, targets_ref):
    bits = jnp.int32(0)
    for slot in range(slot_num):
        target = targets_ref[slot, 0, tile]
        cand = (lax.div(target, tile_cols) - global_row + 1) * tile_cols + lax.rem(target, tile_cols)
        bits = bits | jnp.where(slot < count, jnp.left_shift(1, cand), 0)
    return bits


def hidden(bits, index):
    return (1 - (jnp.right_shift(bits, index) & 1)).astype(F32) * NEG


def attend_tile_row(
    tile_row, tile_rows, columns, targets_ref, counts_ref, q_ref, k_refs, v_refs, p_ref, acc_ref
):
    slab = q_ref.shape[0]
    tile_cols = columns // TW
    slot_num = targets_ref.shape[0]
    global_row = lax.axis_index("row") * tile_rows + tile_row
    left = lax.broadcasted_iota(jnp.int32, (1, 4 * TILE), 1) % (2 * TILE) < TILE
    for duo in range(tile_cols // 2):
        bits = []
        for tile in (2 * duo, 2 * duo + 1):
            tile = tile_row * tile_cols + tile
            bits.append(
                visible_bits(tile, counts_ref[0, tile], global_row, tile_cols, slot_num, targets_ref)
            )
        lowest, highest = max(2 * duo - 1, 0), min(2 * duo + 2, tile_cols - 1)
        span = range(lowest, highest + 1)
        bias = {}
        for j in range(3):
            for col in span:
                at = j * tile_cols + col
                bias[j, col] = jnp.where(left, hidden(bits[0], at), hidden(bits[1], at))
        for pair in range(PAIRS):
            lo, hi = pair_window(pair)
            queries = two_heads(q_ref[2 * duo * TILE : (2 * duo + 2) * TILE, lo:hi], pair)
            scores = {}
            for j, ref in enumerate(k_refs):
                part = nt_dot(ref[lowest * TILE : (highest + 1) * TILE, lo:hi], queries)
                for col in span:
                    at = (col - lowest) * TILE
                    scores[j, col] = part[at : at + TILE] + bias[j, col]
            top = functools.reduce(jnp.maximum, scores.values())
            top = jnp.max(top, axis=0, keepdims=True)
            for (j, col), score in scores.items():
                at = j * slab + col * TILE
                p_ref[duo * PAIRS + pair, at : at + TILE, :] = jnp.exp2(score - top).astype(BF16)

    for duo in range(tile_cols // 2):
        for pair in range(PAIRS):
            out = sum(
                nn_dot(
                    ref[pair * PAIR_ROWS : (pair + 1) * PAIR_ROWS, :],
                    p_ref[duo * PAIRS + pair, j * slab : (j + 1) * slab, :],
                )
                for j, ref in enumerate(v_refs)
            )
            out = out[:PAIR] * (1.0 / out[PAIR : PAIR + 1])
            lanes = slice(2 * duo * TILE, (2 * duo + 2) * TILE)
            acc_ref[pair * PAIR : pair * PAIR + HD, lanes] = out[:HD, : 2 * TILE]
            acc_ref[pair * PAIR + HD : (pair + 1) * PAIR, lanes] = out[HD:, 2 * TILE :]


def reach(peers):
    far, near = list(range(peers - 1, peers // 2 - 1, -1)), list(range(peers // 2 - 1, 0, -1))
    half = len(far) // 2
    return [0] + far[:half] + near[:1] + far[half:] + near[1:]


def peer_of(slot, peers, xor):
    me, j = lax.axis_index("frame"), reach(peers)[slot]
    return me ^ j if xor else lax.rem(me + j, peers)


def hand_out(send_refs, out_ref, group, xor):
    for slot, ref in enumerate(send_refs):
        peer = peer_of(slot, len(send_refs), xor)
        ref[...] = out_ref[pl.ds(pl.multiple_of(peer * group, PACK), group), :]


def inner_kernel(
    group, peers, xor,
    targets_ref, counts_ref, x_hbm, w_ref, wo_ref, q_hbm, k_hbm, v_hbm, edge_hbm, top_hbm, bot_hbm, mixed_ref,
    *rest,
):
    send_refs, rest = rest[:peers], rest[peers:]
    x_ref, q_ref, k_ref, v_ref, sum_ref, col_ref, p_ref, acc_ref, out_ref, x_sem, out_sem, halo_sem = rest
    step = pl.program_id(0)
    tile_rows, tile_cols = x_ref.shape[:2]
    columns = tile_cols * TW
    feat = x_ref.shape[-1]
    slab = tile_cols * TILE
    v_rows = PAIRS * PAIR_ROWS
    ahead = tile_rows // PACE

    def x_copy(at, col):
        return pltpu.make_async_copy(
            x_hbm.at[pl.ds(at * TH, TH), pl.ds(col * TW, TW), :], x_ref.at[at, col], x_sem.at[at, col]
        )

    def out_copies(at):
        rows, wide = pl.ds(at * slab, slab), pl.ds(at * v_rows, v_rows)
        return (
            pltpu.make_async_copy(q_ref.at[at], q_hbm.at[rows], out_sem.at[0, at]),
            pltpu.make_async_copy(k_ref.at[at], k_hbm.at[rows], out_sem.at[1, at]),
            pltpu.make_async_copy(v_ref.at[at], v_hbm.at[wide], out_sem.at[2, at]),
        )

    def edge_copies():
        for part, at in enumerate((0, tile_rows - 1)):
            yield pltpu.make_async_copy(x_ref.at[at], edge_hbm.at[part], out_sem.at[3, part])

    def halo_copies():
        for part, (at, halo) in enumerate(((0, top_hbm), (tile_rows - 1, bot_hbm))):
            yield pltpu.make_async_copy(v_ref.at[at], halo.at[pl.ds(0, v_rows)], halo_sem.at[part, 0])
            for piece, (rows, lanes, to, lane) in enumerate(packed_keys(slab)):
                to = pl.ds(v_rows + to.start, to.size)
                yield pltpu.make_async_copy(
                    k_ref.at[at, rows, lanes], halo.at[to, lane], halo_sem.at[part, 1 + piece]
                )

    def work(first):
        for part in range(PACE):
            for col in range(tile_cols):
                x_copy(step * PACE + part, col).wait()
        size = PACE * slab
        x = x_ref[pl.ds(step * PACE, PACE)].reshape(size, feat)
        mean, rstd = moments(x)
        rows = x
        if first:
            rows = jnp.concatenate([x, jnp.ones((PACK, feat), BF16)], axis=0)
        prod = nt_dot(rows, w_ref[: 2 * INNER, :])
        if first:
            sum_ref[...] = prod[size : size + 1]
            col_ref[...] = row_sums(w_ref[2 * INNER :, :])
        q, k = split_queries_keys((prod[:size] - mean * sum_ref[...]) * rstd)
        q, k = (q * (LOG2E * HD**-0.5)).astype(BF16), k.astype(BF16)
        values = nt_dot(w_ref[2 * INNER :, :], x) - col_ref[...] * as_rows(mean)
        values = (values * as_rows(rstd)).astype(BF16)
        for part in range(PACE):
            at, own = step * PACE + part, slice(part * slab, (part + 1) * slab)
            q_ref[at], k_ref[at] = q[own], k[own]
            store_values(v_ref.at[at], values[:, own], slice(None))
            for copy in out_copies(at):
                copy.start()

    @pl.when(step == 0)
    def _():
        for at in range(tile_rows):
            for col in range(tile_cols):
                x_copy(at, col).start()
        work(True)

    @pl.when((step > 0) & (step < ahead))
    def _():
        work(False)

    @pl.when(step == ahead)
    def _():
        for copy in (*edge_copies(), *halo_copies()):
            copy.start()
        p_ref[...] = jnp.zeros(p_ref.shape, BF16)

    @pl.when(step >= ahead)
    def _():
        tile_row = step - ahead + 1
        k_refs = [k_ref.at[tile_row + j] for j in (-1, 0, 1)]
        v_refs = [v_ref.at[tile_row + j] for j in (-1, 0, 1)]
        attend_tile_row(
            tile_row, tile_rows, columns, targets_ref, counts_ref, q_ref.at[tile_row],
            k_refs, v_refs, p_ref, acc_ref,
        )
        branch = nn_dot(acc_ref[...].T.astype(BF16), wo_ref[...])
        mixed = (x_ref[tile_row].reshape(slab, feat).astype(F32) + branch).astype(BF16)
        mixed_ref[...] = mixed
        out_ref[pl.ds(pl.multiple_of((tile_row - 1) * slab, slab), slab), :] = mixed

    @pl.when(step == ahead + tile_rows - 3)
    def _():
        hand_out(send_refs, out_ref, group, xor)
        for at in range(tile_rows):
            for copy in out_copies(at):
                copy.wait()
        for copy in (*edge_copies(), *halo_copies()):
            copy.wait()


def spatial_inner(x, w, wo, targets, counts, peers, xor):
    rows, columns, feat = x.shape
    tile_rows = rows // TH
    slab = TH * columns
    v_rows = PAIRS * PAIR_ROWS
    ahead = tile_rows // PACE
    group = (tile_rows - 2) * slab // peers
    smem = pl.BlockSpec(memory_space=pltpu.SMEM)
    hbm, vmem = pl.BlockSpec(memory_space=pltpu.HBM), pl.BlockSpec(memory_space=pltpu.VMEM)
    outs = pl.pallas_call(
        functools.partial(inner_kernel, group, peers, xor),
        grid=(ahead + tile_rows - 2,),
        in_specs=[smem, smem, hbm, vmem, vmem],
        out_specs=[hbm] * 6 + [pl.BlockSpec((slab, feat), lambda i: (jnp.maximum(i - ahead, 0), 0))]
        + [pl.BlockSpec((group, feat), lambda i: (0, 0))] * peers,
        out_shape=[
            jax.ShapeDtypeStruct((tile_rows * slab, WIDE), BF16),
            jax.ShapeDtypeStruct((tile_rows * slab, WIDE), BF16),
            jax.ShapeDtypeStruct((tile_rows * v_rows, slab), BF16),
            jax.ShapeDtypeStruct((2, columns // TW, TH, TW, feat), BF16),
            jax.ShapeDtypeStruct((v_rows + WIDE, slab), BF16),
            jax.ShapeDtypeStruct((v_rows + WIDE, slab), BF16),
            jax.ShapeDtypeStruct(((tile_rows - 2) * slab, feat), BF16),
        ]
        + [jax.ShapeDtypeStruct((group, feat), BF16)] * peers,
        scratch_shapes=[
            pltpu.VMEM((tile_rows, columns // TW, TH, TW, feat), BF16),
            pltpu.VMEM((tile_rows, slab, WIDE), BF16),
            pltpu.VMEM((tile_rows, slab, WIDE), BF16),
            pltpu.VMEM((tile_rows, v_rows, slab), BF16),
            pltpu.VMEM((1, 2 * INNER), F32),
            pltpu.VMEM((INNER, 1), F32),
            pltpu.VMEM((columns // TW // 2 * PAIRS, 3 * slab, 4 * TILE), BF16),
            pltpu.VMEM((INNER, slab), F32),
            pltpu.VMEM(((tile_rows - 2) * slab, feat), BF16),
            pltpu.SemaphoreType.DMA((tile_rows, columns // TW)),
            pltpu.SemaphoreType.DMA((4, tile_rows)),
            pltpu.SemaphoreType.DMA((2, 1 + len(list(packed_keys(slab))))),
        ],
        compiler_params=params(VMEM_WHOLE),
        cost_estimate=cost(12 * 10**9, 16 * 2**20),
        name="spatial_inner",
    )(targets, counts, x, w, wo)
    return outs[:3], outs[3].reshape(2 * slab, feat), outs[4:6], outs[6], outs[7:]


def edges_kernel(
    group, peers, xor, tile_rows, columns,
    targets_ref, counts_ref, x_ref, q_ref, k0, k1, k2, v0, v1, v2, top_ref, bot_ref, w_ref, mixed_ref, *rest,
):
    send_refs, rest = rest[:peers], rest[peers:]
    p_ref, acc_ref, out_ref, k_prev, k_next, v_prev, v_next = rest
    step = pl.program_id(0)
    slab = x_ref.shape[0]

    @pl.when(step == 0)
    def _():
        p_ref[...] = jnp.zeros(p_ref.shape, BF16)
        unpack_halo(top_ref, k_prev, v_prev)
        k_next[...] = k2[...]
        v_next[...] = v2[...]

    @pl.when(step != 0)
    def _():
        k_prev[...] = k0[...]
        v_prev[...] = v0[...]
        unpack_halo(bot_ref, k_next, v_next)

    attend_tile_row(
        step * (tile_rows - 1), tile_rows, columns, targets_ref, counts_ref, q_ref,
        (k_prev, k1, k_next), (v_prev, v1, v_next), p_ref, acc_ref,
    )
    branch = nn_dot(acc_ref[...].T.astype(BF16), w_ref[...])
    mixed = (x_ref[...].astype(F32) + branch).astype(BF16)
    mixed_ref[...] = mixed
    mean, rstd = moments(mixed)
    normed = ((mixed.astype(F32) - mean) * rstd).astype(BF16)
    out_ref[pl.ds(pl.multiple_of(step * slab, slab), slab), :] = normed

    @pl.when(step == 1)
    def _():
        hand_out(send_refs, out_ref, group, xor)


def spatial_edges(x, q, k, v, halos, w, targets, counts, slab, columns, peers, xor):
    feat = x.shape[1]
    tile_rows = q.shape[0] // slab
    group = 2 * slab // peers
    v_rows = PAIRS * PAIR_ROWS
    at = lambda i: i * (tile_rows - 1)
    smem = pl.BlockSpec(memory_space=pltpu.SMEM)
    whole = lambda *shape: pl.BlockSpec(shape, lambda i: (0, 0))
    in_specs = [
        smem,
        smem,
        pl.BlockSpec((slab, feat), lambda i: (i, 0)),
        pl.BlockSpec((slab, WIDE), lambda i: (at(i), 0)),
    ]
    for block in ((slab, WIDE), (v_rows, slab)):
        in_specs += [
            pl.BlockSpec(block, lambda i: (tile_rows - 2, 0)),
            pl.BlockSpec(block, lambda i: (at(i), 0)),
            pl.BlockSpec(block, lambda i: (1, 0)),
        ]
    in_specs += [whole(*halo.shape) for halo in halos]
    in_specs.append(whole(*w.shape))
    outs = pl.pallas_call(
        functools.partial(edges_kernel, group, peers, xor, tile_rows, columns),
        grid=(2,),
        in_specs=in_specs,
        out_specs=[pl.BlockSpec((slab, feat), lambda i: (i, 0))]
        + [whole(group, feat)] * peers,
        out_shape=[jax.ShapeDtypeStruct((2 * slab, feat), BF16)]
        + [jax.ShapeDtypeStruct((group, feat), BF16)] * peers,
        scratch_shapes=[
            pltpu.VMEM((columns // TW // 2 * PAIRS, 3 * slab, 4 * TILE), BF16),
            pltpu.VMEM((INNER, slab), F32),
            pltpu.VMEM((2 * slab, feat), BF16),
            pltpu.VMEM((slab, WIDE), BF16),
            pltpu.VMEM((slab, WIDE), BF16),
            pltpu.VMEM((v_rows, slab), BF16),
            pltpu.VMEM((v_rows, slab), BF16),
        ],
        compiler_params=params(),
        cost_estimate=cost(6 * 10**9, 8 * 2**20),
        name="spatial_edges",
    )(targets, counts, x, q, k, k, k, v, v, v, *halos, w)
    return outs[0], outs[1:]


def temporal_kernel(peers, group, normed, early, *refs):
    in_refs, w_ref, early_refs = refs[:peers], refs[peers], refs[peers + 1 : -6 - peers]
    out_refs, (x_ref, q_ref, k_ref, v_ref, p_ref, acc_ref) = refs[-6 - peers : -6], refs[-6:]
    for slot, ref in zip(early, early_refs):
        out_refs[slot][: ref.shape[0], :] = ref[...]
    block = peers * PACK
    parts = group // PACK
    tokens = peers * group

    for part in range(parts):
        for j in range(peers):
            to = pl.ds(part * block + j * PACK, PACK)
            x_ref[to, :] = in_refs[j][pl.ds(part * PACK, PACK), :]
    x_ref[tokens:, :] = jnp.ones((PACK, x_ref.shape[1]), BF16)
    x = x_ref[:tokens, :]
    w_values = w_ref[2 * INNER :, :]
    if normed:
        prod = nt_dot(x, w_ref[: 2 * INNER, :])
        values = nt_dot(w_values, x)
    else:
        mean, rstd = moments(x)
        prod = nt_dot(x_ref[...], w_ref[: 2 * INNER, :])
        prod = (prod[:tokens] - mean * prod[tokens : tokens + 1]) * rstd
        values = (nt_dot(w_values, x) - row_sums(w_values) * as_rows(mean)) * as_rows(rstd)
    q, k = split_queries_keys(prod)
    q_ref[...] = (q * (LOG2E * HD**-0.5)).astype(BF16)
    k_ref[...] = k.astype(BF16)
    store_values(v_ref, values.astype(BF16), slice(None))
    row = lax.broadcasted_iota(jnp.int32, (block, 2 * block), 0)
    col = lax.broadcasted_iota(jnp.int32, (block, 2 * block), 1)
    bias = jnp.where(row % PACK == col % PACK, 0.0, NEG).astype(F32)
    for part in range(parts):
        at = part * block
        for pair in range(PAIRS):
            lo, hi = pair_window(pair)
            queries = two_heads(q_ref[at : at + block, lo:hi], pair)
            scores = nt_dot(k_ref[at : at + block, lo:hi], queries) + bias
            expo = jnp.exp2(scores - jnp.max(scores, axis=0, keepdims=True))
            p_ref[part * PAIRS + pair] = expo.astype(BF16)
    for part in range(parts):
        at = part * block
        for pair in range(PAIRS):
            weights = v_ref[pair * PAIR_ROWS : (pair + 1) * PAIR_ROWS, at : at + block]
            out = nn_dot(weights, p_ref[part * PAIRS + pair])
            out = out[:PAIR] * (1.0 / out[PAIR : PAIR + 1])
            acc_ref[pair * PAIR : pair * PAIR + HD, at : at + block] = out[:HD, :block]
            acc_ref[pair * PAIR + HD : (pair + 1) * PAIR, at : at + block] = out[HD:, block:]
    for part in range(parts):
        at = part * block
        heads = acc_ref[:, at : at + block].T.astype(BF16)
        for j in range(peers):
            rows = pl.ds(out_refs[j].shape[0] - group + part * PACK, PACK)
            out_refs[j][rows, :] = heads[j * PACK : (j + 1) * PACK]


def temporal(pieces, w, normed, early=None):
    early = early or {}
    peers = len(pieces)
    group, feat = pieces[0].shape
    tokens = peers * group
    rows = [group + (early[slot].shape[0] if slot in early else 0) for slot in range(peers)]
    return pl.pallas_call(
        functools.partial(temporal_kernel, peers, group, normed, tuple(early)),
        out_shape=[jax.ShapeDtypeStruct((count, INNER), BF16) for count in rows],
        scratch_shapes=[
            pltpu.VMEM((tokens + PACK, feat), BF16),
            pltpu.VMEM((tokens, WIDE), BF16),
            pltpu.VMEM((tokens, WIDE), BF16),
            pltpu.VMEM((PAIRS * PAIR_ROWS, tokens), BF16),
            pltpu.VMEM((group // PACK * PAIRS, peers * PACK, 2 * peers * PACK), BF16),
            pltpu.VMEM((INNER, tokens), F32),
        ],
        compiler_params=params(),
        cost_estimate=cost(4 * 10**9, 6 * 2**20),
        name="temporal",
    )(*pieces, w, *early.values())


def final_kernel(groups, early, xor, columns, *refs):
    in_refs, (first_ref, second_ref, w_ref, out_hbm, heads_ref, out_ref, sem) = refs[:-7], refs[-7:]
    in_refs, early_refs = in_refs[: -len(early)], dict(zip(early, in_refs[-len(early) :]))
    peers = len(in_refs)
    slab = TH * columns
    tile_rows = out_ref.shape[0]
    for slot, ref in enumerate(in_refs):
        peer = peer_of(slot, peers, xor)
        to = pl.ds(pl.multiple_of(peer * groups[0], PACK), groups[0])
        heads_ref[to, :] = early_refs[slot][...] if slot in early_refs else ref[: groups[0], :]
        to = pl.multiple_of(peers * groups[0] + peer * groups[1], PACK)
        heads_ref[pl.ds(to, groups[1]), :] = ref[ref.shape[0] - groups[1] :, :]

    copies = []
    begin = 0
    for mixed_ref, rows in ((first_ref, range(1, tile_rows - 1)), (second_ref, (0, tile_rows - 1))):
        end = begin + mixed_ref.shape[0]
        result = mixed_ref[...].astype(F32) + nn_dot(heads_ref[begin:end, :], w_ref[...])
        result = result.astype(BF16)
        begin = end
        for part, row in enumerate(rows):
            for to, at in tile_order(slab, columns):
                to += part * slab
                out_ref[row, pl.ds(at, TW), :] = result[to : to + TW]
            copies.append(
                pltpu.make_async_copy(out_ref.at[row], out_hbm.at[pl.ds(row * slab, slab)], sem.at[row])
            )
            copies[-1].start()
    for copy in copies:
        copy.wait()


def final(pieces, early, first, second, w, slab, columns, xor):
    feat = first.shape[1]
    tile_rows = (first.shape[0] + second.shape[0]) // slab
    peers = len(pieces)
    groups = (first.shape[0] // peers, second.shape[0] // peers)
    vmem = pl.BlockSpec(memory_space=pltpu.VMEM)
    return pl.pallas_call(
        functools.partial(final_kernel, groups, tuple(early), xor, columns),
        in_specs=[vmem] * (peers + len(early) + 3),
        out_specs=pl.BlockSpec(memory_space=pltpu.HBM),
        out_shape=jax.ShapeDtypeStruct((tile_rows * slab, feat), BF16),
        scratch_shapes=[
            pltpu.VMEM((tile_rows * slab, INNER), BF16),
            pltpu.VMEM((tile_rows, slab, feat), BF16),
            pltpu.SemaphoreType.DMA((tile_rows,)),
        ],
        compiler_params=params(),
        cost_estimate=cost(2 * 10**9, 6 * 2**20),
        name="final",
    )(*pieces, *early.values(), first, second, w)


def neighbours(top, bot):
    size = lax.axis_size("row")
    up = [(i, i + 1) for i in range(size - 1)]
    down = [(j, i) for i, j in up]
    return lax.ppermute(bot, "row", up), lax.ppermute(top, "row", down)


def exchange(pieces, xor, back):
    size = lax.axis_size("frame")
    result = {}
    for slot, piece in pieces.items():
        j = reach(size)[slot]
        if xor:
            pairs = [(i, i ^ j) for i in range(size)]
        else:
            pairs = [(i, (i - j if back else i + j) % size) for i in range(size)]
        result[slot] = lax.ppermute(piece, "frame", pairs) if slot else piece
    return result


def by_slot(pieces):
    return dict(enumerate(pieces))


def body(frames_in, spatial_qkv, spatial_out, temporal_qkv, temporal_out, key_tiles, tile_counts):
    _, rows_dev, columns, feat = frames_in.shape
    slab = TH * columns
    key_tiles = key_tiles.transpose(2, 0, 1)
    peers = lax.axis_size("frame")
    xor = peers & (peers - 1) == 0
    qkv, edges, halos, mixed_a, send_a = spatial_inner(
        frames_in[0], spatial_qkv.T, spatial_out, key_tiles, tile_counts, peers, xor
    )
    got_a = exchange(by_slot(send_a), xor, False)
    halos = neighbours(*halos)
    mixed_b, send_b = spatial_edges(
        edges, *qkv, halos, spatial_out, key_tiles, tile_counts, slab, columns, peers, xor
    )
    got_b = exchange(by_slot(send_b), xor, False)
    heads_a = by_slot(temporal(list(got_a.values()), temporal_qkv.T, False))
    far = range(1, 1 + peers // 4)
    early = exchange({slot: heads_a.pop(slot) for slot in far}, xor, True)
    heads = by_slot(temporal(list(got_b.values()), temporal_qkv.T, True, heads_a))
    back = exchange(heads, xor, True)
    out = final(
        list(back.values()), early, mixed_a, mixed_b, temporal_out, slab, columns, xor
    )
    return out.reshape(frames_in.shape)


def solution(mesh):
    in_specs = (
        P("frame", "row", None, None),
        P(),
        P(),
        P(),
        P(),
        P("frame", "row", None),
        P("frame", "row"),
    )
    out_specs = P("frame", "row", None, None)
    return jax.shard_map(body, mesh=mesh, in_specs=in_specs, out_specs=out_specs, check_vma=False)
```

```python
import functools

import jax
import jax.numpy as jnp
from jax import lax
from jax.experimental import pallas as pl
from jax.experimental.pallas import tpu as pltpu
from jax.sharding import PartitionSpec as P

HEADS = 8
HD = 72
TH = 4
TW = 16
LANES = 128
PACK = 16
NORM_EPS = 1e-06
NEG = -1e30
LOG2E = 1.4426950408889634
F32 = jnp.float32
BF16 = jnp.bfloat16
INNER = HEADS * HD
WIDE = -(-INNER // LANES) * LANES
PAIR = 2 * HD
PAIRS = HEADS // 2
PACE = 2
PAIR_ROWS = PAIR + PACK
TILE = TH * TW
VMEM_LIMIT = 28 * 1024 * 1024
VMEM_WHOLE = 58 * 1024 * 1024


def params(limit=VMEM_LIMIT):
    return pltpu.CompilerParams(vmem_limit_bytes=limit)


def cost(flops, bytes_accessed):
    return pl.CostEstimate(flops=flops, bytes_accessed=bytes_accessed, transcendentals=0)


def nt_dot(a, b):
    return lax.dot_general(a, b, (((1,), (1,)), ((), ())), preferred_element_type=F32)


def nn_dot(a, b):
    return jnp.dot(a, b, preferred_element_type=F32)


def moments(x):
    x = x.astype(F32)
    mean = jnp.mean(x, axis=-1, keepdims=True)
    centred = x - mean
    spread = jnp.mean(centred * centred, axis=-1, keepdims=True)
    return mean, lax.rsqrt(spread + NORM_EPS)


def as_rows(column):
    return jnp.broadcast_to(column, (column.shape[0], LANES)).T[:1]


def tile_order(rows, columns):
    for col in range(columns // TW):
        for row in range(TH):
            yield (col * TH + row) * TW, row * columns + col * TW


def pair_window(pair):
    return pair * PAIR // LANES * LANES, -(-(pair + 1) * PAIR // LANES) * LANES


def two_heads(queries, pair):
    lo, hi = pair_window(pair)
    lane = lax.broadcasted_iota(jnp.int32, queries.shape, 1) + lo
    start = pair * PAIR
    first = jnp.where((lane >= start) & (lane < start + HD), queries, 0)
    second = jnp.where((lane >= start + HD) & (lane < start + PAIR), queries, 0)
    return jnp.concatenate([first, second], axis=0)


def split_queries_keys(prod):
    keys = prod[:, INNER // LANES * LANES :]
    shift = INNER % LANES
    if shift:
        keys = pltpu.roll(keys, keys.shape[1] - shift, 1)
    return prod[:, :WIDE], keys


def row_sums(w):
    return jnp.sum(w.astype(F32), axis=-1, keepdims=True)


def store_values(v_ref, values, lanes):
    for pair in range(PAIRS):
        at = pair * PAIR_ROWS
        v_ref[at : at + PAIR, lanes] = values[pair * PAIR : (pair + 1) * PAIR]
        v_ref[at + PAIR : at + PAIR_ROWS, lanes] = jnp.ones((PACK, values.shape[1]), BF16)


def packed_keys(slab):
    per = slab // LANES
    full = WIDE // slab * per
    for piece in range(WIDE // LANES):
        lanes = pl.ds(piece * LANES, LANES)
        if piece < full:
            yield pl.ds(0, slab), lanes, pl.ds(piece // per * slab, slab), pl.ds(piece % per * LANES, LANES)
        else:
            rows = slab // per
            for part in range(per):
                to = pl.ds(full // per * slab, rows), pl.ds(part * LANES, LANES)
                yield pl.ds(part * rows, rows), lanes, *to


def unpack_halo(halo_ref, k_ref, v_ref):
    size = v_ref.shape[0]
    v_ref[...] = halo_ref[:size, :]
    for rows, lanes, at, to in packed_keys(k_ref.shape[0]):
        k_ref[rows, lanes] = halo_ref[pl.ds(size + at.start, at.size), to]


def visible_bits(tile, count, global_row, tile_cols, slot_num, targets_ref):
    bits = jnp.int32(0)
    for slot in range(slot_num):
        target = targets_ref[slot, 0, tile]
        cand = (lax.div(target, tile_cols) - global_row + 1) * tile_cols + lax.rem(target, tile_cols)
        bits = bits | jnp.where(slot < count, jnp.left_shift(1, cand), 0)
    return bits


def hidden(bits, index):
    return (1 - (jnp.right_shift(bits, index) & 1)).astype(F32) * NEG


def attend_tile_row(
    tile_row, tile_rows, columns, targets_ref, counts_ref, q_ref, k_refs, v_refs, p_ref, acc_ref
):
    slab = q_ref.shape[0]
    tile_cols = columns // TW
    slot_num = targets_ref.shape[0]
    global_row = lax.axis_index("row") * tile_rows + tile_row
    left = lax.broadcasted_iota(jnp.int32, (1, 4 * TILE), 1) % (2 * TILE) < TILE
    for duo in range(tile_cols // 2):
        bits = []
        for tile in (2 * duo, 2 * duo + 1):
            tile = tile_row * tile_cols + tile
            bits.append(
                visible_bits(tile, counts_ref[0, tile], global_row, tile_cols, slot_num, targets_ref)
            )
        lowest, highest = max(2 * duo - 1, 0), min(2 * duo + 2, tile_cols - 1)
        span = range(lowest, highest + 1)
        bias = {}
        for j in range(3):
            for col in span:
                at = j * tile_cols + col
                bias[j, col] = jnp.where(left, hidden(bits[0], at), hidden(bits[1], at))
        for pair in range(PAIRS):
            lo, hi = pair_window(pair)
            queries = two_heads(q_ref[2 * duo * TILE : (2 * duo + 2) * TILE, lo:hi], pair)
            scores = {}
            for j, ref in enumerate(k_refs):
                part = nt_dot(ref[lowest * TILE : (highest + 1) * TILE, lo:hi], queries)
                for col in span:
                    at = (col - lowest) * TILE
                    scores[j, col] = part[at : at + TILE] + bias[j, col]
            top = functools.reduce(jnp.maximum, scores.values())
            top = jnp.max(top, axis=0, keepdims=True)
            for (j, col), score in scores.items():
                at = j * slab + col * TILE
                p_ref[duo * PAIRS + pair, at : at + TILE, :] = jnp.exp2(score - top).astype(BF16)

    for duo in range(tile_cols // 2):
        for pair in range(PAIRS):
            out = sum(
                nn_dot(
                    ref[pair * PAIR_ROWS : (pair + 1) * PAIR_ROWS, :],
                    p_ref[duo * PAIRS + pair, j * slab : (j + 1) * slab, :],
                )
                for j, ref in enumerate(v_refs)
            )
            out = out[:PAIR] * (1.0 / out[PAIR : PAIR + 1])
            lanes = slice(2 * duo * TILE, (2 * duo + 2) * TILE)
            acc_ref[pair * PAIR : pair * PAIR + HD, lanes] = out[:HD, : 2 * TILE]
            acc_ref[pair * PAIR + HD : (pair + 1) * PAIR, lanes] = out[HD:, 2 * TILE :]


def reach(peers):
    far, near = list(range(peers - 1, peers // 2 - 1, -1)), list(range(peers // 2 - 1, 0, -1))
    half = len(far) // 2
    return [0] + far[:half] + near[:1] + far[half:] + near[1:]


def peer_of(slot, peers, xor):
    me, j = lax.axis_index("frame"), reach(peers)[slot]
    return me ^ j if xor else lax.rem(me + j, peers)


def hand_out(send_refs, out_ref, group, xor):
    for slot, ref in enumerate(send_refs):
        peer = peer_of(slot, len(send_refs), xor)
        ref[...] = out_ref[pl.ds(pl.multiple_of(peer * group, PACK), group), :]


def inner_kernel(
    group, peers, xor,
    targets_ref, counts_ref, x_hbm, w_ref, wo_ref, q_hbm, k_hbm, v_hbm, edge_hbm, top_hbm, bot_hbm, mixed_ref,
    *rest,
):
    send_refs, rest = rest[:peers], rest[peers:]
    x_ref, q_ref, k_ref, v_ref, sum_ref, col_ref, p_ref, acc_ref, out_ref, x_sem, out_sem, halo_sem = rest
    step = pl.program_id(0)
    tile_rows, tile_cols = x_ref.shape[:2]
    columns = tile_cols * TW
    feat = x_ref.shape[-1]
    slab = tile_cols * TILE
    v_rows = PAIRS * PAIR_ROWS
    ahead = tile_rows // PACE

    def x_copy(at, col):
        return pltpu.make_async_copy(
            x_hbm.at[pl.ds(at * TH, TH), pl.ds(col * TW, TW), :], x_ref.at[at, col], x_sem.at[at, col]
        )

    def out_copies(at):
        rows, wide = pl.ds(at * slab, slab), pl.ds(at * v_rows, v_rows)
        return (
            pltpu.make_async_copy(q_ref.at[at], q_hbm.at[rows], out_sem.at[0, at]),
            pltpu.make_async_copy(k_ref.at[at], k_hbm.at[rows], out_sem.at[1, at]),
            pltpu.make_async_copy(v_ref.at[at], v_hbm.at[wide], out_sem.at[2, at]),
        )

    def edge_copies():
        for part, at in enumerate((0, tile_rows - 1)):
            yield pltpu.make_async_copy(x_ref.at[at], edge_hbm.at[part], out_sem.at[3, part])

    def halo_copies():
        for part, (at, halo) in enumerate(((0, top_hbm), (tile_rows - 1, bot_hbm))):
            yield pltpu.make_async_copy(v_ref.at[at], halo.at[pl.ds(0, v_rows)], halo_sem.at[part, 0])
            for piece, (rows, lanes, to, lane) in enumerate(packed_keys(slab)):
                to = pl.ds(v_rows + to.start, to.size)
                yield pltpu.make_async_copy(
                    k_ref.at[at, rows, lanes], halo.at[to, lane], halo_sem.at[part, 1 + piece]
                )

    def work(first):
        for part in range(PACE):
            for col in range(tile_cols):
                x_copy(step * PACE + part, col).wait()
        size = PACE * slab
        x = x_ref[pl.ds(step * PACE, PACE)].reshape(size, feat)
        mean, rstd = moments(x)
        rows = x
        if first:
            rows = jnp.concatenate([x, jnp.ones((PACK, feat), BF16)], axis=0)
        prod = nt_dot(rows, w_ref[: 2 * INNER, :])
        if first:
            sum_ref[...] = prod[size : size + 1]
            col_ref[...] = row_sums(w_ref[2 * INNER :, :])
        q, k = split_queries_keys((prod[:size] - mean * sum_ref[...]) * rstd)
        q, k = (q * (LOG2E * HD**-0.5)).astype(BF16), k.astype(BF16)
        values = nt_dot(w_ref[2 * INNER :, :], x) - col_ref[...] * as_rows(mean)
        values = (values * as_rows(rstd)).astype(BF16)
        for part in range(PACE):
            at, own = step * PACE + part, slice(part * slab, (part + 1) * slab)
            q_ref[at], k_ref[at] = q[own], k[own]
            store_values(v_ref.at[at], values[:, own], slice(None))
            for copy in out_copies(at):
                copy.start()

    @pl.when(step == 0)
    def _():
        for at in range(tile_rows):
            for col in range(tile_cols):
                x_copy(at, col).start()
        work(True)

    @pl.when((step > 0) & (step < ahead))
    def _():
        work(False)

    @pl.when(step == ahead)
    def _():
        for copy in (*edge_copies(), *halo_copies()):
            copy.start()
        p_ref[...] = jnp.zeros(p_ref.shape, BF16)

    @pl.when(step >= ahead)
    def _():
        tile_row = step - ahead + 1
        k_refs = [k_ref.at[tile_row + j] for j in (-1, 0, 1)]
        v_refs = [v_ref.at[tile_row + j] for j in (-1, 0, 1)]
        attend_tile_row(
            tile_row, tile_rows, columns, targets_ref, counts_ref, q_ref.at[tile_row],
            k_refs, v_refs, p_ref, acc_ref,
        )
        branch = nn_dot(acc_ref[...].T.astype(BF16), wo_ref[...])
        mixed = (x_ref[tile_row].reshape(slab, feat).astype(F32) + branch).astype(BF16)
        mixed_ref[...] = mixed
        out_ref[pl.ds(pl.multiple_of((tile_row - 1) * slab, slab), slab), :] = mixed

    @pl.when(step == ahead + tile_rows - 3)
    def _():
        hand_out(send_refs, out_ref, group, xor)
        for at in range(tile_rows):
            for copy in out_copies(at):
                copy.wait()
        for copy in (*edge_copies(), *halo_copies()):
            copy.wait()


def spatial_inner(x, w, wo, targets, counts, peers, xor):
    rows, columns, feat = x.shape
    tile_rows = rows // TH
    slab = TH * columns
    v_rows = PAIRS * PAIR_ROWS
    ahead = tile_rows // PACE
    group = (tile_rows - 2) * slab // peers
    smem = pl.BlockSpec(memory_space=pltpu.SMEM)
    hbm, vmem = pl.BlockSpec(memory_space=pltpu.HBM), pl.BlockSpec(memory_space=pltpu.VMEM)
    outs = pl.pallas_call(
        functools.partial(inner_kernel, group, peers, xor),
        grid=(ahead + tile_rows - 2,),
        in_specs=[smem, smem, hbm, vmem, vmem],
        out_specs=[hbm] * 6 + [pl.BlockSpec((slab, feat), lambda i: (jnp.maximum(i - ahead, 0), 0))]
        + [pl.BlockSpec((group, feat), lambda i: (0, 0))] * peers,
        out_shape=[
            jax.ShapeDtypeStruct((tile_rows * slab, WIDE), BF16),
            jax.ShapeDtypeStruct((tile_rows * slab, WIDE), BF16),
            jax.ShapeDtypeStruct((tile_rows * v_rows, slab), BF16),
            jax.ShapeDtypeStruct((2, columns // TW, TH, TW, feat), BF16),
            jax.ShapeDtypeStruct((v_rows + WIDE, slab), BF16),
            jax.ShapeDtypeStruct((v_rows + WIDE, slab), BF16),
            jax.ShapeDtypeStruct(((tile_rows - 2) * slab, feat), BF16),
        ]
        + [jax.ShapeDtypeStruct((group, feat), BF16)] * peers,
        scratch_shapes=[
            pltpu.VMEM((tile_rows, columns // TW, TH, TW, feat), BF16),
            pltpu.VMEM((tile_rows, slab, WIDE), BF16),
            pltpu.VMEM((tile_rows, slab, WIDE), BF16),
            pltpu.VMEM((tile_rows, v_rows, slab), BF16),
            pltpu.VMEM((1, 2 * INNER), F32),
            pltpu.VMEM((INNER, 1), F32),
            pltpu.VMEM((columns // TW // 2 * PAIRS, 3 * slab, 4 * TILE), BF16),
            pltpu.VMEM((INNER, slab), F32),
            pltpu.VMEM(((tile_rows - 2) * slab, feat), BF16),
            pltpu.SemaphoreType.DMA((tile_rows, columns // TW)),
            pltpu.SemaphoreType.DMA((4, tile_rows)),
            pltpu.SemaphoreType.DMA((2, 1 + len(list(packed_keys(slab))))),
        ],
        compiler_params=params(VMEM_WHOLE),
        cost_estimate=cost(12 * 10**9, 16 * 2**20),
        name="spatial_inner",
    )(targets, counts, x, w, wo)
    return outs[:3], outs[3].reshape(2 * slab, feat), outs[4:6], outs[6], outs[7:]


def edges_kernel(
    group, peers, xor, tile_rows, columns,
    targets_ref, counts_ref, x_ref, q_ref, k0, k1, k2, v0, v1, v2, top_ref, bot_ref, w_ref, mixed_ref, *rest,
):
    send_refs, rest = rest[:peers], rest[peers:]
    p_ref, acc_ref, out_ref, k_prev, k_next, v_prev, v_next = rest
    step = pl.program_id(0)
    slab = x_ref.shape[0]

    @pl.when(step == 0)
    def _():
        p_ref[...] = jnp.zeros(p_ref.shape, BF16)
        unpack_halo(top_ref, k_prev, v_prev)
        k_next[...] = k2[...]
        v_next[...] = v2[...]

    @pl.when(step != 0)
    def _():
        k_prev[...] = k0[...]
        v_prev[...] = v0[...]
        unpack_halo(bot_ref, k_next, v_next)

    attend_tile_row(
        step * (tile_rows - 1), tile_rows, columns, targets_ref, counts_ref, q_ref,
        (k_prev, k1, k_next), (v_prev, v1, v_next), p_ref, acc_ref,
    )
    branch = nn_dot(acc_ref[...].T.astype(BF16), w_ref[...])
    mixed = (x_ref[...].astype(F32) + branch).astype(BF16)
    mixed_ref[...] = mixed
    mean, rstd = moments(mixed)
    normed = ((mixed.astype(F32) - mean) * rstd).astype(BF16)
    out_ref[pl.ds(pl.multiple_of(step * slab, slab), slab), :] = normed

    @pl.when(step == 1)
    def _():
        hand_out(send_refs, out_ref, group, xor)


def spatial_edges(x, q, k, v, halos, w, targets, counts, slab, columns, peers, xor):
    feat = x.shape[1]
    tile_rows = q.shape[0] // slab
    group = 2 * slab // peers
    v_rows = PAIRS * PAIR_ROWS
    at = lambda i: i * (tile_rows - 1)
    smem = pl.BlockSpec(memory_space=pltpu.SMEM)
    whole = lambda *shape: pl.BlockSpec(shape, lambda i: (0, 0))
    in_specs = [
        smem,
        smem,
        pl.BlockSpec((slab, feat), lambda i: (i, 0)),
        pl.BlockSpec((slab, WIDE), lambda i: (at(i), 0)),
    ]
    for block in ((slab, WIDE), (v_rows, slab)):
        in_specs += [
            pl.BlockSpec(block, lambda i: (tile_rows - 2, 0)),
            pl.BlockSpec(block, lambda i: (at(i), 0)),
            pl.BlockSpec(block, lambda i: (1, 0)),
        ]
    in_specs += [whole(*halo.shape) for halo in halos]
    in_specs.append(whole(*w.shape))
    outs = pl.pallas_call(
        functools.partial(edges_kernel, group, peers, xor, tile_rows, columns),
        grid=(2,),
        in_specs=in_specs,
        out_specs=[pl.BlockSpec((slab, feat), lambda i: (i, 0))]
        + [whole(group, feat)] * peers,
        out_shape=[jax.ShapeDtypeStruct((2 * slab, feat), BF16)]
        + [jax.ShapeDtypeStruct((group, feat), BF16)] * peers,
        scratch_shapes=[
            pltpu.VMEM((columns // TW // 2 * PAIRS, 3 * slab, 4 * TILE), BF16),
            pltpu.VMEM((INNER, slab), F32),
            pltpu.VMEM((2 * slab, feat), BF16),
            pltpu.VMEM((slab, WIDE), BF16),
            pltpu.VMEM((slab, WIDE), BF16),
            pltpu.VMEM((v_rows, slab), BF16),
            pltpu.VMEM((v_rows, slab), BF16),
        ],
        compiler_params=params(),
        cost_estimate=cost(6 * 10**9, 8 * 2**20),
        name="spatial_edges",
    )(targets, counts, x, q, k, k, k, v, v, v, *halos, w)
    return outs[0], outs[1:]


def temporal_kernel(peers, group, normed, early, *refs):
    in_refs, w_ref, early_refs = refs[:peers], refs[peers], refs[peers + 1 : -6 - peers]
    out_refs, (x_ref, q_ref, k_ref, v_ref, p_ref, acc_ref) = refs[-6 - peers : -6], refs[-6:]
    for slot, ref in zip(early, early_refs):
        out_refs[slot][: ref.shape[0], :] = ref[...]
    block = peers * PACK
    parts = group // PACK
    tokens = peers * group

    for part in range(parts):
        for j in range(peers):
            to = pl.ds(part * block + j * PACK, PACK)
            x_ref[to, :] = in_refs[j][pl.ds(part * PACK, PACK), :]
    x_ref[tokens:, :] = jnp.ones((PACK, x_ref.shape[1]), BF16)
    x = x_ref[:tokens, :]
    w_values = w_ref[2 * INNER :, :]
    if normed:
        prod = nt_dot(x, w_ref[: 2 * INNER, :])
        values = nt_dot(w_values, x)
    else:
        mean, rstd = moments(x)
        prod = nt_dot(x_ref[...], w_ref[: 2 * INNER, :])
        prod = (prod[:tokens] - mean * prod[tokens : tokens + 1]) * rstd
        values = (nt_dot(w_values, x) - row_sums(w_values) * as_rows(mean)) * as_rows(rstd)
    q, k = split_queries_keys(prod)
    q_ref[...] = (q * (LOG2E * HD**-0.5)).astype(BF16)
    k_ref[...] = k.astype(BF16)
    store_values(v_ref, values.astype(BF16), slice(None))
    row = lax.broadcasted_iota(jnp.int32, (block, 2 * block), 0)
    col = lax.broadcasted_iota(jnp.int32, (block, 2 * block), 1)
    bias = jnp.where(row % PACK == col % PACK, 0.0, NEG).astype(F32)
    for part in range(parts):
        at = part * block
        for pair in range(PAIRS):
            lo, hi = pair_window(pair)
            queries = two_heads(q_ref[at : at + block, lo:hi], pair)
            scores = nt_dot(k_ref[at : at + block, lo:hi], queries) + bias
            expo = jnp.exp2(scores - jnp.max(scores, axis=0, keepdims=True))
            p_ref[part * PAIRS + pair] = expo.astype(BF16)
    for part in range(parts):
        at = part * block
        for pair in range(PAIRS):
            weights = v_ref[pair * PAIR_ROWS : (pair + 1) * PAIR_ROWS, at : at + block]
            out = nn_dot(weights, p_ref[part * PAIRS + pair])
            out = out[:PAIR] * (1.0 / out[PAIR : PAIR + 1])
            acc_ref[pair * PAIR : pair * PAIR + HD, at : at + block] = out[:HD, :block]
            acc_ref[pair * PAIR + HD : (pair + 1) * PAIR, at : at + block] = out[HD:, block:]
    for part in range(parts):
        at = part * block
        heads = acc_ref[:, at : at + block].T.astype(BF16)
        for j in range(peers):
            rows = pl.ds(out_refs[j].shape[0] - group + part * PACK, PACK)
            out_refs[j][rows, :] = heads[j * PACK : (j + 1) * PACK]


def temporal(pieces, w, normed, early=None):
    early = early or {}
    peers = len(pieces)
    group, feat = pieces[0].shape
    tokens = peers * group
    rows = [group + (early[slot].shape[0] if slot in early else 0) for slot in range(peers)]
    return pl.pallas_call(
        functools.partial(temporal_kernel, peers, group, normed, tuple(early)),
        out_shape=[jax.ShapeDtypeStruct((count, INNER), BF16) for count in rows],
        scratch_shapes=[
            pltpu.VMEM((tokens + PACK, feat), BF16),
            pltpu.VMEM((tokens, WIDE), BF16),
            pltpu.VMEM((tokens, WIDE), BF16),
            pltpu.VMEM((PAIRS * PAIR_ROWS, tokens), BF16),
            pltpu.VMEM((group // PACK * PAIRS, peers * PACK, 2 * peers * PACK), BF16),
            pltpu.VMEM((INNER, tokens), F32),
        ],
        compiler_params=params(),
        cost_estimate=cost(4 * 10**9, 6 * 2**20),
        name="temporal",
    )(*pieces, w, *early.values())


def final_kernel(groups, early, xor, columns, *refs):
    in_refs, (first_ref, second_ref, w_ref, out_hbm, heads_ref, out_ref, sem) = refs[:-7], refs[-7:]
    in_refs, early_refs = in_refs[: -len(early)], dict(zip(early, in_refs[-len(early) :]))
    peers = len(in_refs)
    slab = TH * columns
    tile_rows = out_ref.shape[0]
    for slot, ref in enumerate(in_refs):
        peer = peer_of(slot, peers, xor)
        to = pl.ds(pl.multiple_of(peer * groups[0], PACK), groups[0])
        heads_ref[to, :] = early_refs[slot][...] if slot in early_refs else ref[: groups[0], :]
        to = pl.multiple_of(peers * groups[0] + peer * groups[1], PACK)
        heads_ref[pl.ds(to, groups[1]), :] = ref[ref.shape[0] - groups[1] :, :]

    copies = []
    begin = 0
    for mixed_ref, rows in ((first_ref, range(1, tile_rows - 1)), (second_ref, (0, tile_rows - 1))):
        end = begin + mixed_ref.shape[0]
        for part, row in enumerate(rows):
            own = slice(part * slab, (part + 1) * slab)
            heads = heads_ref[begin + own.start : begin + own.stop, :]
            result = (mixed_ref[own, :].astype(F32) + nn_dot(heads, w_ref[...])).astype(BF16)
            for to, at in tile_order(slab, columns):
                out_ref[row, pl.ds(at, TW), :] = result[to : to + TW]
            copies.append(
                pltpu.make_async_copy(out_ref.at[row], out_hbm.at[pl.ds(row * slab, slab)], sem.at[row])
            )
            copies[-1].start()
        begin = end
    for copy in copies:
        copy.wait()


def final(pieces, early, first, second, w, slab, columns, xor):
    feat = first.shape[1]
    tile_rows = (first.shape[0] + second.shape[0]) // slab
    peers = len(pieces)
    groups = (first.shape[0] // peers, second.shape[0] // peers)
    vmem = pl.BlockSpec(memory_space=pltpu.VMEM)
    return pl.pallas_call(
        functools.partial(final_kernel, groups, tuple(early), xor, columns),
        in_specs=[vmem] * (peers + len(early) + 3),
        out_specs=pl.BlockSpec(memory_space=pltpu.HBM),
        out_shape=jax.ShapeDtypeStruct((tile_rows * slab, feat), BF16),
        scratch_shapes=[
            pltpu.VMEM((tile_rows * slab, INNER), BF16),
            pltpu.VMEM((tile_rows, slab, feat), BF16),
            pltpu.SemaphoreType.DMA((tile_rows,)),
        ],
        compiler_params=params(),
        cost_estimate=cost(2 * 10**9, 6 * 2**20),
        name="final",
    )(*pieces, *early.values(), first, second, w)


def neighbours(top, bot):
    size = lax.axis_size("row")
    up = [(i, i + 1) for i in range(size - 1)]
    down = [(j, i) for i, j in up]
    return lax.ppermute(bot, "row", up), lax.ppermute(top, "row", down)


def exchange(pieces, xor, back):
    size = lax.axis_size("frame")
    result = {}
    for slot, piece in pieces.items():
        j = reach(size)[slot]
        if xor:
            pairs = [(i, i ^ j) for i in range(size)]
        else:
            pairs = [(i, (i - j if back else i + j) % size) for i in range(size)]
        result[slot] = lax.ppermute(piece, "frame", pairs) if slot else piece
    return result


def by_slot(pieces):
    return dict(enumerate(pieces))


def body(frames_in, spatial_qkv, spatial_out, temporal_qkv, temporal_out, key_tiles, tile_counts):
    _, rows_dev, columns, feat = frames_in.shape
    slab = TH * columns
    key_tiles = key_tiles.transpose(2, 0, 1)
    peers = lax.axis_size("frame")
    xor = peers & (peers - 1) == 0
    qkv, edges, halos, mixed_a, send_a = spatial_inner(
        frames_in[0], spatial_qkv.T, spatial_out, key_tiles, tile_counts, peers, xor
    )
    got_a = exchange(by_slot(send_a), xor, False)
    halos = neighbours(*halos)
    mixed_b, send_b = spatial_edges(
        edges, *qkv, halos, spatial_out, key_tiles, tile_counts, slab, columns, peers, xor
    )
    got_b = exchange(by_slot(send_b), xor, False)
    heads_a = by_slot(temporal(list(got_a.values()), temporal_qkv.T, False))
    far = range(1, 1 + peers // 4)
    early = exchange({slot: heads_a.pop(slot) for slot in far}, xor, True)
    heads = by_slot(temporal(list(got_b.values()), temporal_qkv.T, True, heads_a))
    back = exchange(heads, xor, True)
    out = final(
        list(back.values()), early, mixed_a, mixed_b, temporal_out, slab, columns, xor
    )
    return out.reshape(frames_in.shape)


def solution(mesh):
    in_specs = (
        P("frame", "row", None, None),
        P(),
        P(),
        P(),
        P(),
        P("frame", "row", None),
        P("frame", "row"),
    )
    out_specs = P("frame", "row", None, None)
    return jax.shard_map(body, mesh=mesh, in_specs=in_specs, out_specs=out_specs, check_vma=False)
```
